32 devices in a mesh: groups: 2 (over x), node: 16 (over z, y, core).
Axes of the slice: x: 2, y: 2, z: 4, core: 2. Of those that a mesh axis runs over, the one named last changes fastest.
Arguments:
- tokens: bfloat16 [1024, 3584], P(('groups', 'node')), parts along dimension 0, may hold values from -6 to 6
- routes: int32 [1024, 8], P(('groups', 'node')), parts along dimension 0, may hold values from 0 to 15, all different within a row; in each aligned block of 32 rows (0 to 31, 32 to 63, ...) at most 32 rows name the same one
- gates: float32 [1024, 8], P(('groups', 'node')), parts along dimension 0, may hold values from 0.1 to 0.5
- w_gate: bfloat16 [16, 3584, 1024], P('node'), may hold values from -0.09375 to 0.09375
- w_up: bfloat16 [16, 3584, 1024], P('node'), may hold values from -0.09375 to 0.09375
- w_down: bfloat16 [16, 1024, 3584], P('node'), may hold values from -0.1875 to 0.1875
Outputs:
- mixed: bfloat16 [1024, 3584], P(('groups', 'node')), parts along dimension 0
The draws below stay inside these ranges and needn't reach their ends.
There are 2 independent parts, one for each index of `groups`. The reference program is written for one: setup_inputs(seed, part) draws one part's arguments, and reference() takes and returns one part's arrays. A program takes and returns all parts, laid end to end along the dimension named above; an argument that names none is the same for every part. Nothing has to cross between parts.
Inputs may be any that keep to these rules, and one draw needn't show every extreme that they name: `routes`: each token names 8 different experts; at most 32 of the tokens of one device name the same expert, and exactly 32 do so for some expert and device.
All inputs are finite; a program needn't handle non-finite values.
Results may differ from the reference program's by a relative error of at most 0.0057.
Values may be sent and summed in bfloat16 or wider, within the bound.
No kernel may reach another device: no remote copies, remote signals or barrier semaphores. Data moves between devices by JAX's collectives and lax.ppermute only.
A program may use at most 128 MiB of HBM per device.

```python
import math
import jax
import jax.numpy as jnp
import numpy as np
from jax import lax

D = 3584
FF = 1024
TOPK = 8
TOK_DEV = 32
EXPERTS = 16
TOKENS = 512
MOST = 32
N_NODE = 16


def block_scale(stream_key, shape, cuts, low, high):
    factor_of, own = 1.0, jax.random.fold_in(stream_key, 6)
    for axis_at, parts in cuts:
        draws = jnp.exp(jax.random.uniform(jax.random.fold_in(own, axis_at), (parts,), jnp.float32, low / len(cuts), high / len(cuts)))
        factor_of = factor_of * jnp.repeat(draws, shape[axis_at] // parts).reshape([-1 if axis == axis_at else 1 for axis in range(len(shape))])
    return factor_of


def shared_out(own_key, own, number, rows, number_of, top, bound, slope):
    sequence = jax.random.permutation(own_key, number_of)
    heavy_load, ordinary = shares(number_of, rows * top, bound, slope, True), shares(number_of, rows * top, bound, slope, False)
    places = jnp.arange(number_of)

    def named(sizes, rotation):
        used = int((sizes > 0).sum())
        fixed = max(1, used // 4)
        passed = fixed + (places - fixed + rotation * (used - fixed)) % max(1, number_of - fixed)
        return jnp.zeros((number_of,), jnp.int32).at[sequence[jnp.where(places < fixed, places, passed)]].set(jnp.asarray(sizes, jnp.int32))

    sizes = jnp.where(number % 4 == 0, named(heavy_load, number // 4), named(ordinary, number - number // 4 - 1))
    mixed = jax.random.permutation(jax.random.fold_in(own, 3), number_of)
    source_of, receiver = mixed[0:number_of // 2 * 2:2], mixed[1:number_of // 2 * 2:2]
    slack = jnp.minimum(sizes[source_of] - 1, bound - sizes[receiver]) // 2
    slack = jnp.where((source_of == sequence[0]) | (receiver == sequence[0]) | (sizes[receiver] == 0), 0, jnp.maximum(slack, 0))
    passed = jax.random.randint(jax.random.fold_in(own, 4), (number_of // 2,), 0, 1 << 20) % (slack + 1)
    sizes = sizes.at[source_of].add(-passed).at[receiver].add(passed)
    labels = jnp.searchsorted(jnp.cumsum(sizes), jnp.arange(rows * top), side="right").astype(jnp.int32)
    listing = labels.reshape(top, rows).T
    listing = listing[jax.random.permutation(jax.random.fold_in(own, 1), rows)]
    rotation = jax.random.randint(jax.random.fold_in(own, 2), (rows, 1), 0, top)
    return jnp.take_along_axis(listing, (jnp.arange(top)[None, :] + rotation) % top, axis=1)


def shares(count, total, most, slope, full):
    weights = [(1 << 20) // math.isqrt(standing ** slope) + 1 for standing in range(1, count + 1)]
    largest = most if full else min(most, max(-(-total // count), total * weights[0] // sum(weights)))
    least = 1 if total - largest >= count - 1 else 0
    given, rest = [largest] + [least] * (count - 1), total - largest - least * (count - 1)
    while rest > 0:
        movable = [i for i in range(1, count) if given[i] < largest] or [i for i in range(1, count) if given[i] < most]
        pool, budget = sum([weights[i] for i in movable]), rest
        for i in movable:
            extra = min(most - given[i], max(1, budget * weights[i] // pool), rest)
            given[i] = given[i] + extra
            rest = rest - extra
    return np.array(given)


def scatter_about(key, dims, spread, limit, cuts=(), held_as=jnp.bfloat16):
    level = block_scale(key, dims, cuts, -0.22, 0.18) if cuts else 1.0
    drawn = jax.random.normal(key, dims, jnp.float32) * spread * level
    return jnp.minimum(jnp.maximum(drawn, -limit), limit).astype(held_as)


def setup_inputs(seed: int = 0, part: int = 0) -> dict:
    seeds = jax.random.split(jax.random.key(seed), 7)
    part_splits = jax.random.split(jax.random.fold_in(seeds[6], part), 7)
    tokens = scatter_about(part_splits[0], (TOKENS, D), 1.0, 6.0, ((0, 16),))
    routes_keys = jax.random.split(jax.random.fold_in(part_splits[1], 1), TOKENS // TOK_DEV)
    routes_turns = jax.random.permutation(jax.random.fold_in(part_splits[1], 3), TOKENS // TOK_DEV)
    routes = jax.vmap(lambda own, number: shared_out(jax.random.fold_in(part_splits[1], 2), own, number, TOK_DEV, EXPERTS, TOPK, MOST, 2))(routes_keys, routes_turns).reshape((TOKENS, TOPK))
    gates = jnp.clip(0.1 + 0.4 * jax.random.uniform(part_splits[2], (TOKENS, TOPK), jnp.float32) ** block_scale(part_splits[2], (TOKENS, TOPK), ((0, 16),), -0.2, 0.2), 0.1, 0.5)
    w_gate = scatter_about(seeds[3], (EXPERTS, D, FF), D ** -0.5, 0.09375, ((0, 16),))
    w_up = scatter_about(seeds[4], (EXPERTS, D, FF), D ** -0.5, 0.09375, ((0, 16),))
    w_down = scatter_about(seeds[5], (EXPERTS, FF, D), FF ** -0.5, 0.1875, ((0, 16),))
    return {"tokens": tokens, "routes": routes, "gates": gates, "w_gate": w_gate, "w_up": w_up, "w_down": w_down}


def reference(tokens, routes, gates, w_gate, w_up, w_down):
    capacity = N_NODE * MOST
    order = jnp.arange(TOKENS, dtype=jnp.int32)

    def one_expert(total, inputs):
        expert_id, gate_mat, up_mat, down_mat = inputs
        hits = routes == expert_id
        weight = jnp.sum(jnp.where(hits, gates, jnp.zeros_like(gates)), axis=1)
        routed = jnp.any(hits, axis=1)
        score = jnp.where(routed, 2 * TOKENS, 0).astype(jnp.int32) + (TOKENS - order)
        picked = lax.top_k(score, capacity)[1].astype(jnp.int32)
        rows = tokens[picked]
        gate = jnp.dot(rows, gate_mat, preferred_element_type=jnp.float32)
        upper = jnp.dot(rows, up_mat, preferred_element_type=jnp.float32)
        hidden = (jax.nn.silu(gate) * upper).astype(jnp.bfloat16)
        produced = jnp.dot(hidden, down_mat, preferred_element_type=jnp.float32).astype(jnp.bfloat16)
        contrib = weight[picked][:, None] * produced.astype(weight.dtype)
        return total.at[picked].add(contrib), None

    start = jnp.zeros((TOKENS, D), gates.dtype)
    total, _ = lax.scan(one_expert, start, (jnp.arange(EXPERTS, dtype=jnp.int32), w_gate, w_up, w_down))
    return total.astype(jnp.bfloat16)
```

```python
import functools

import jax
import jax.numpy as jnp
from jax import lax
from jax.experimental import pallas as pl
from jax.experimental.pallas import tpu as pltpu
from jax.sharding import PartitionSpec as P

F32, BF16 = jnp.float32, jnp.bfloat16


def chip_layout(mesh):
    names = list(mesh.axis_names)
    count = mesh.shape["node"]
    row = mesh.devices.transpose([names.index(n) for n in names if n != "node"] + [names.index("node")])
    row = list(row.reshape(-1, count)[0])
    where = [tuple(getattr(d, "coords", None) or (i // 2,)) for i, d in enumerate(row)]
    cores = 2 if count % 2 == 0 and all(where[i] == where[i + 1] for i in range(0, count, 2)) else 1
    chips = where[::cores]
    order = list(range(len(chips)))
    axes = [a for a in range(len(chips[0])) if len({c[a] for c in chips}) > 1]
    if len(axes) == 2:
        short, long = sorted(axes, key=lambda a: len({c[a] for c in chips}))
        low = min(c[short] for c in chips)
        if len({c[short] for c in chips}) == 2:
            order.sort(key=lambda i: (chips[i][short], chips[i][long] if chips[i][short] == low else -chips[i][long]))
    return cores, order


def pack_kernel(experts, tok_ref, routes_ref, gates_ref, out_ref):
    rows, width = tok_ref.shape
    extra = out_ref.shape[1] - width
    lane = lax.broadcasted_iota(jnp.int32, (rows, extra), 1)
    expert, piece = lax.rem(lane, experts), lax.div(lane, experts)
    weight = jnp.zeros((rows, extra), F32)
    for k in range(routes_ref.shape[1]):
        weight += jnp.where(routes_ref[:, k : k + 1] == expert, gates_ref[:, k : k + 1], 0.0)
    high = weight.astype(BF16).astype(F32)
    middle = (weight - high).astype(BF16).astype(F32)
    low = weight - high - middle
    table = jnp.where(piece == 0, high, jnp.where(piece == 1, middle, jnp.where(piece == 2, low, 0.0)))
    out_ref[:, :width] = tok_ref[...]
    out_ref[:, width:] = table.astype(BF16)


def pack(tokens, routes, gates, experts):
    rows, width = tokens.shape
    extra = pl.cdiv(3 * experts, 128) * 128
    return pl.pallas_call(
        functools.partial(pack_kernel, experts),
        out_shape=jax.ShapeDtypeStruct((rows, width + extra), BF16),
    )(tokens, routes, gates)


def ffn_kernel(count, rows, experts, n_ff, me_ref, *refs):
    blocks, (gate_ref, up_ref, down_ref, mine_ref, other_ref, x_ref, w_ref, h_ref) = refs[:count], refs[count:]
    i = pl.program_id(0)
    width = x_ref.shape[1]
    half = mine_ref.shape[0]

    @pl.when(i == 0)
    def _():
        for at, ref in enumerate(blocks):
            x_ref[at * rows : (at + 1) * rows, :] = ref[:, :width]
            table = ref[:, width:].astype(F32)
            lane = lax.broadcasted_iota(jnp.int32, table.shape, 1)
            own = lax.rem(lane, experts) == me_ref[0]
            w_ref[at * rows : (at + 1) * rows, :] = jnp.sum(jnp.where(own, table, 0.0), axis=1, keepdims=True)

    @pl.when(i < n_ff)
    def _():
        x = x_ref[...]
        gate = jnp.dot(x, gate_ref[0], preferred_element_type=F32)
        upper = jnp.dot(x, up_ref[0], preferred_element_type=F32)
        h_ref[jnp.minimum(i, n_ff - 1)] = (gate / (1.0 + jnp.exp(-gate)) * upper).astype(BF16)

    @pl.when(i >= n_ff)
    def _():
        tile = h_ref.shape[2]
        out = jnp.dot(h_ref[0], down_ref[0, :tile], preferred_element_type=F32)
        for j in range(1, n_ff):
            out += jnp.dot(h_ref[j], down_ref[0, j * tile : (j + 1) * tile], preferred_element_type=F32)
        out = out * w_ref[...]
        mine_ref[...] = out[:half]
        if count * rows > half:
            other_ref[...] = out[half:].astype(BF16)


def ffn(blocks, mine, me, experts, w_gate, w_up, w_down):
    count, rows = len(blocks), blocks[0].shape[0]
    _, width, ff = w_gate.shape
    tile_ff = 256 if ff % 256 == 0 else ff
    tile_d = next(t for t in (512, 256, 128, width) if width % t == 0)
    n_ff, n_d = ff // tile_ff, width // tile_d
    total, half = count * rows, mine * rows
    first = lambda i: (0, 0, jnp.minimum(i, n_ff - 1))
    second = lambda i: (0, jnp.maximum(i - n_ff, 0))
    return pl.pallas_call(
        functools.partial(ffn_kernel, count, rows, experts, n_ff),
        grid=(n_ff + n_d,),
        out_shape=[
            jax.ShapeDtypeStruct((half, width), F32),
            jax.ShapeDtypeStruct((total - half, width), BF16),
        ],
        in_specs=[pl.BlockSpec(memory_space=pltpu.SMEM)]
        + [pl.BlockSpec(b.shape, lambda i: (0, 0)) for b in blocks]
        + [
            pl.BlockSpec((1, width, tile_ff), first),
            pl.BlockSpec((1, width, tile_ff), first),
            pl.BlockSpec((1, ff, tile_d), lambda i: (0, 0, jnp.maximum(i - n_ff, 0))),
        ],
        out_specs=[pl.BlockSpec((half, tile_d), second), pl.BlockSpec((total - half, tile_d), second)],
        scratch_shapes=[
            pltpu.VMEM((total, width), BF16),
            pltpu.VMEM((total, 1), F32),
            pltpu.VMEM((n_ff, total, tile_ff), BF16),
        ],
        compiler_params=pltpu.CompilerParams(vmem_limit_bytes=40 * 2**20),
        cost_estimate=pl.CostEstimate(
            flops=6 * total * width * ff, bytes_accessed=6 * width * ff, transcendentals=total * ff
        ),
    )(me, *blocks, w_gate, w_up, w_down)


def local(cores, order, tokens, routes, gates, w_gate, w_up, w_down):
    chips = len(order)
    experts = chips * cores
    rows, width = tokens.shape
    me = lax.axis_index("node").astype(jnp.int32).reshape(1)
    forth = [(order[i] * cores + c, order[(i + 1) % chips] * cores + c) for i in range(chips) for c in range(cores)]
    back = [(b, a) for a, b in forth]
    swap = [(chip * cores + c, chip * cores + 1 - c) for chip in range(chips) for c in range(cores)]
    right = lambda a: lax.ppermute(a, "node", forth)
    left = lambda a: lax.ppermute(a, "node", back)
    sibling = lambda a: lax.ppermute(a, "node", swap)

    own = pack(tokens, routes, gates, experts)
    far = chips // 2
    cut = rows // 2
    got = {0: own}
    for d in range(1, far):
        got[-d] = right(got[-(d - 1)])
        got[d] = left(got[d - 1])
    ends = (right(got[1 - far][:cut]), left(got[far - 1][cut:]))
    got[far] = jnp.concatenate(ends, axis=0)
    twin = {d: sibling(got[d]) for d in got}

    run = lambda at: ffn([got[d] for d in at] + [twin[d] for d in at], len(at), me, experts, w_gate, w_up, w_down)
    late = [far] + [s * (far - 1) for s in (1, -1)]
    early = [d for d in sorted(got, key=abs) if d not in late]
    mine, theirs = {}, {}
    for at in (early, late):
        kept, sent = run(at)
        sent = sibling(sent)
        for j, d in enumerate(at):
            mine[d] = kept[j * rows : (j + 1) * rows]
            theirs[d] = sent[j * rows : (j + 1) * rows]

    both = lambda d: mine[d] + theirs[d].astype(F32)
    end = both(far).astype(BF16)
    a, b = right(end[:cut]), left(end[cut:])
    for d in range(far - 1, 0, -1):
        up, down = both(d), both(-d)
        if d == far - 1:
            up = jnp.concatenate([up[:cut] + a.astype(F32), up[cut:]], axis=0)
            down = jnp.concatenate([down[:cut], down[cut:] + b.astype(F32)], axis=0)
        else:
            up, down = up + a.astype(F32), down + b.astype(F32)
        a, b = right(up.astype(BF16)), left(down.astype(BF16))
    return (both(0) + a.astype(F32) + b.astype(F32)).astype(BF16)


def solution(mesh):
    cores, order = chip_layout(mesh)
    in_specs = (
        P(("groups", "node"), None),
        P(("groups", "node"), None),
        P(("groups", "node"), None),
        P("node", None, None),
        P("node", None, None),
        P("node", None, None),
    )
    out_specs = P(("groups", "node"), None)
    body = functools.partial(local, cores, order)
    return jax.shard_map(body, mesh=mesh, in_specs=in_specs, out_specs=out_specs, check_vma=False)
```

```python
import functools

import jax
import jax.numpy as jnp
from jax import lax
from jax.experimental import pallas as pl
from jax.experimental.pallas import tpu as pltpu
from jax.sharding import PartitionSpec as P

F32, BF16 = jnp.float32, jnp.bfloat16
SCRATCH = 16 * 2**20


def chip_layout(mesh):
    names = list(mesh.axis_names)
    count = mesh.shape["node"]
    row = mesh.devices.transpose([names.index(n) for n in names if n != "node"] + [names.index("node")])
    row = list(row.reshape(-1, count)[0])
    where = [tuple(getattr(d, "coords", None) or (i // 2,)) for i, d in enumerate(row)]
    cores = 2 if count % 2 == 0 and all(where[i] == where[i + 1] for i in range(0, count, 2)) else 1
    chips = where[::cores]
    order = list(range(len(chips)))
    axes = [a for a in range(len(chips[0])) if len({c[a] for c in chips}) > 1]
    if len(axes) == 2:
        short, long = sorted(axes, key=lambda a: len({c[a] for c in chips}))
        low = min(c[short] for c in chips)
        if len({c[short] for c in chips}) == 2:
            order.sort(key=lambda i: (chips[i][short], chips[i][long] if chips[i][short] == low else -chips[i][long]))
    return cores, order


def pack_kernel(experts, tok_hbm, routes_hbm, gates_hbm, out_ref, routes_ref, gates_ref, sems):
    rows, width = tok_hbm.shape
    extra = out_ref.shape[1] - width
    moves = [
        pltpu.make_async_copy(routes_hbm, routes_ref, sems.at[0]),
        pltpu.make_async_copy(gates_hbm, gates_ref, sems.at[1]),
        pltpu.make_async_copy(tok_hbm, out_ref.at[:, :width], sems.at[2]),
    ]
    for move in moves:
        move.start()
    for move in moves[:2]:
        move.wait()
    lane = lax.broadcasted_iota(jnp.int32, (extra, rows), 0)
    expert, piece = lax.rem(lane, experts), lax.div(lane, experts)
    weight = jnp.zeros((extra, rows), F32)
    for k in range(routes_ref.shape[0]):
        weight += jnp.where(routes_ref[k : k + 1] == expert, gates_ref[k : k + 1], 0.0)
    high = weight.astype(BF16).astype(F32)
    middle = (weight - high).astype(BF16).astype(F32)
    low = weight - high - middle
    table = jnp.where(piece == 0, high, jnp.where(piece == 1, middle, jnp.where(piece == 2, low, 0.0)))
    out_ref[:, width:] = table.T.astype(BF16)
    moves[2].wait()


def pack(tokens, routes, gates, experts):
    rows, width = tokens.shape
    extra = pl.cdiv(3 * experts, 128) * 128
    hbm = pl.BlockSpec(memory_space=pltpu.HBM)
    return pl.pallas_call(
        functools.partial(pack_kernel, experts),
        out_shape=jax.ShapeDtypeStruct((rows, width + extra), BF16),
        in_specs=[hbm] * 3,
        out_specs=pl.BlockSpec(memory_space=pltpu.VMEM),
        scratch_shapes=[
            pltpu.VMEM(routes.shape[::-1], routes.dtype),
            pltpu.VMEM(gates.shape[::-1], gates.dtype),
            pltpu.SemaphoreType.DMA((3,)),
        ],
        compiler_params=pltpu.CompilerParams(vmem_limit_bytes=SCRATCH),
        cost_estimate=pl.CostEstimate(flops=40 * 2**30, bytes_accessed=0, transcendentals=0),
    )(tokens, routes.T, gates.T)


def ffn_kernel(count, rows, experts, tile_ff, tile_d, me_ref, *refs):
    blocks, (gate_ref, up_ref, down_ref, mine_ref, other_ref, x_ref, w_ref, h_ref) = refs[:count], refs[count:]
    width = x_ref.shape[1]
    half = mine_ref.shape[0]
    for at, ref in enumerate(blocks):
        x_ref[at * rows : (at + 1) * rows, :] = ref[:, :width]
        table = ref[:, width:].astype(F32)
        lane = lax.broadcasted_iota(jnp.int32, table.shape, 1)
        own = lax.rem(lane, experts) == me_ref[0]
        w_ref[at * rows : (at + 1) * rows, :] = jnp.sum(jnp.where(own, table, 0.0), axis=1, keepdims=True)

    @pl.loop(0, h_ref.shape[1] // tile_ff)
    def _(j):
        at = pl.ds(pl.multiple_of(j * tile_ff, tile_ff), tile_ff)
        gate = jnp.dot(x_ref[...], gate_ref[0, :, at], preferred_element_type=F32)
        upper = jnp.dot(x_ref[...], up_ref[0, :, at], preferred_element_type=F32)
        h_ref[:, at] = (gate / (1.0 + jnp.exp(-gate)) * upper).astype(BF16)

    @pl.loop(0, width // tile_d)
    def _(j):
        at = pl.ds(pl.multiple_of(j * tile_d, tile_d), tile_d)
        out = jnp.dot(h_ref[...], down_ref[0, :, at], preferred_element_type=F32) * w_ref[...]
        mine_ref[:, at] = out[:half]
        other_ref[:, at] = out[half:].astype(BF16)


def ffn(blocks, mine, me, experts, w_gate, w_up, w_down):
    count, rows = len(blocks), blocks[0].shape[0]
    _, width, ff = w_gate.shape
    tile_ff = 256 if ff % 256 == 0 else ff
    tile_d = next(t for t in (512, 256, 128, width) if width % t == 0)
    total, half = count * rows, mine * rows
    vmem = pl.BlockSpec(memory_space=pltpu.VMEM)
    return pl.pallas_call(
        functools.partial(ffn_kernel, count, rows, experts, tile_ff, tile_d),
        out_shape=[
            jax.ShapeDtypeStruct((half, width), F32),
            jax.ShapeDtypeStruct((total - half, width), BF16),
        ],
        in_specs=[pl.BlockSpec(memory_space=pltpu.SMEM)] + [vmem] * (count + 3),
        out_specs=[vmem, vmem],
        scratch_shapes=[
            pltpu.VMEM((total, width), BF16),
            pltpu.VMEM((total, 1), F32),
            pltpu.VMEM((total, ff), BF16),
        ],
        compiler_params=pltpu.CompilerParams(vmem_limit_bytes=SCRATCH),
        cost_estimate=pl.CostEstimate(
            flops=6 * max(total, 256) * width * ff, bytes_accessed=0, transcendentals=total * ff
        ),
    )(me, *blocks, w_gate, w_up, w_down)


def local(cores, order, tokens, routes, gates, w_gate, w_up, w_down):
    chips = len(order)
    experts = chips * cores
    rows, width = tokens.shape
    me = lax.axis_index("node").astype(jnp.int32).reshape(1)
    forth = [(order[i] * cores + c, order[(i + 1) % chips] * cores + c) for i in range(chips) for c in range(cores)]
    back = [(b, a) for a, b in forth]
    swap = [(chip * cores + c, chip * cores + 1 - c) for chip in range(chips) for c in range(cores)]
    right = lambda a: lax.ppermute(a, "node", forth)
    left = lambda a: lax.ppermute(a, "node", back)
    sibling = lambda a: lax.ppermute(a, "node", swap)

    own = pack(tokens, routes, gates, experts)
    far = chips // 2
    cut = rows // 2
    got = {0: own}
    for d in range(1, far):
        got[-d] = right(got[-(d - 1)])
        got[d] = left(got[d - 1])
    ends = (right(got[1 - far][:cut]), left(got[far - 1][cut:]))
    got[far] = jnp.concatenate(ends, axis=0)
    twin = {d: sibling(got[d]) for d in got}

    run = lambda at: ffn([got[d] for d in at] + [twin[d] for d in at], len(at), me, experts, w_gate, w_up, w_down)
    late = [far] + [s * (far - 1) for s in (1, -1)]
    near = [0, 1, -1]
    middle = [d for d in sorted(got, key=abs) if d not in late + near]
    mine, theirs = {}, {}
    for at in (late, middle, near):
        kept, sent = run(at)
        sent = sibling(sent)
        for j, d in enumerate(at):
            mine[d] = kept[j * rows : (j + 1) * rows]
            theirs[d] = sent[j * rows : (j + 1) * rows]

    both = lambda d: mine[d] + theirs[d].astype(F32)
    end = both(far).astype(BF16)
    a, b = right(end[:cut]), left(end[cut:])
    for d in range(far - 1, 0, -1):
        up, down = both(d), both(-d)
        if d == far - 1:
            up = jnp.concatenate([up[:cut] + a.astype(F32), up[cut:]], axis=0)
            down = jnp.concatenate([down[:cut], down[cut:] + b.astype(F32)], axis=0)
        else:
            up, down = up + a.astype(F32), down + b.astype(F32)
        a, b = right(up.astype(BF16)), left(down.astype(BF16))
    return (both(0) + a.astype(F32) + b.astype(F32)).astype(BF16)


def solution(mesh):
    cores, order = chip_layout(mesh)
    in_specs = (
        P(("groups", "node"), None),
        P(("groups", "node"), None),
        P(("groups", "node"), None),
        P("node", None, None),
        P("node", None, None),
        P("node", None, None),
    )
    out_specs = P(("groups", "node"), None)
    body = functools.partial(local, cores, order)
    return jax.shard_map(body, mesh=mesh, in_specs=in_specs, out_specs=out_specs, check_vma=False)
```

```python
import functools

import jax
import jax.numpy as jnp
from jax import lax
from jax.experimental import pallas as pl
from jax.experimental.pallas import tpu as pltpu
from jax.sharding import PartitionSpec as P

F32, BF16 = jnp.float32, jnp.bfloat16
SCRATCH = 16 * 2**20


def chip_layout(mesh):
    names = list(mesh.axis_names)
    count = mesh.shape["node"]
    row = mesh.devices.transpose([names.index(n) for n in names if n != "node"] + [names.index("node")])
    row = list(row.reshape(-1, count)[0])
    where = [tuple(getattr(d, "coords", None) or (i // 2,)) for i, d in enumerate(row)]
    cores = 2 if count % 2 == 0 and all(where[i] == where[i + 1] for i in range(0, count, 2)) else 1
    chips = where[::cores]
    order = list(range(len(chips)))
    axes = [a for a in range(len(chips[0])) if len({c[a] for c in chips}) > 1]
    if len(axes) == 2:
        short, long = sorted(axes, key=lambda a: len({c[a] for c in chips}))
        low = min(c[short] for c in chips)
        if len({c[short] for c in chips}) == 2:
            order.sort(key=lambda i: (chips[i][short], chips[i][long] if chips[i][short] == low else -chips[i][long]))
    return cores, order


def pack_kernel(experts, tok_hbm, routes_hbm, gates_hbm, out_ref, routes_ref, gates_ref, sems):
    rows, width = tok_hbm.shape
    extra = out_ref.shape[1] - width
    moves = [
        pltpu.make_async_copy(routes_hbm, routes_ref, sems.at[0]),
        pltpu.make_async_copy(gates_hbm, gates_ref, sems.at[1]),
        pltpu.make_async_copy(tok_hbm, out_ref.at[:, :width], sems.at[2]),
    ]
    for move in moves:
        move.start()
    for move in moves[:2]:
        move.wait()
    lane = lax.broadcasted_iota(jnp.int32, (extra, rows), 0)
    expert, piece = lax.rem(lane, experts), lax.div(lane, experts)
    weight = jnp.zeros((extra, rows), F32)
    for k in range(routes_ref.shape[0]):
        weight += jnp.where(routes_ref[k : k + 1] == expert, gates_ref[k : k + 1], 0.0)
    high = weight.astype(BF16).astype(F32)
    middle = (weight - high).astype(BF16).astype(F32)
    low = weight - high - middle
    table = jnp.where(piece == 0, high, jnp.where(piece == 1, middle, jnp.where(piece == 2, low, 0.0)))
    out_ref[:, width:] = table.T.astype(BF16)
    moves[2].wait()


def pack(tokens, routes, gates, experts):
    rows, width = tokens.shape
    extra = pl.cdiv(3 * experts, 128) * 128
    hbm = pl.BlockSpec(memory_space=pltpu.HBM)
    return pl.pallas_call(
        functools.partial(pack_kernel, experts),
        out_shape=jax.ShapeDtypeStruct((rows, width + extra), BF16),
        in_specs=[hbm] * 3,
        out_specs=pl.BlockSpec(memory_space=pltpu.VMEM),
        scratch_shapes=[
            pltpu.VMEM(routes.shape[::-1], routes.dtype),
            pltpu.VMEM(gates.shape[::-1], gates.dtype),
            pltpu.SemaphoreType.DMA((3,)),
        ],
        compiler_params=pltpu.CompilerParams(vmem_limit_bytes=SCRATCH),
        cost_estimate=pl.CostEstimate(flops=10 * 2**30, bytes_accessed=0, transcendentals=0),
    )(*(pltpu.with_memory_space_constraint(a, pltpu.HBM) for a in (tokens, routes.T, gates.T)))


def ffn_kernel(count, rows, experts, tile_ff, tile_d, me_ref, *refs):
    blocks, (gate_ref, up_ref, down_ref, mine_ref, other_ref, x_ref, w_ref, h_ref) = refs[:count], refs[count:]
    width = x_ref.shape[1]
    half = mine_ref.shape[0]
    for at, ref in enumerate(blocks):
        x_ref[at * rows : (at + 1) * rows, :] = ref[:, :width]
        table = ref[:, width:].astype(F32)
        lane = lax.broadcasted_iota(jnp.int32, table.shape, 1)
        own = lax.rem(lane, experts) == me_ref[0]
        w_ref[at * rows : (at + 1) * rows, :] = jnp.sum(jnp.where(own, table, 0.0), axis=1, keepdims=True)

    @pl.loop(0, h_ref.shape[1] // tile_ff)
    def _(j):
        at = pl.ds(pl.multiple_of(j * tile_ff, tile_ff), tile_ff)
        gate = jnp.dot(x_ref[...], gate_ref[0, :, at], preferred_element_type=F32)
        upper = jnp.dot(x_ref[...], up_ref[0, :, at], preferred_element_type=F32)
        h_ref[:, at] = (gate / (1.0 + jnp.exp(-gate)) * upper).astype(BF16)

    @pl.loop(0, width // tile_d)
    def _(j):
        at = pl.ds(pl.multiple_of(j * tile_d, tile_d), tile_d)
        out = jnp.dot(h_ref[...], down_ref[0, :, at], preferred_element_type=F32) * w_ref[...]
        mine_ref[:, at] = out[:half]
        other_ref[:, at] = out[half:].astype(BF16)


def ffn(blocks, mine, me, experts, w_gate, w_up, w_down):
    count, rows = len(blocks), blocks[0].shape[0]
    _, width, ff = w_gate.shape
    tile_ff = 256 if ff % 256 == 0 else ff
    tile_d = next(t for t in (512, 256, 128, width) if width % t == 0)
    total, half = count * rows, mine * rows
    vmem = pl.BlockSpec(memory_space=pltpu.VMEM)
    return pl.pallas_call(
        functools.partial(ffn_kernel, count, rows, experts, tile_ff, tile_d),
        out_shape=[
            jax.ShapeDtypeStruct((half, width), F32),
            jax.ShapeDtypeStruct((total - half, width), BF16),
        ],
        in_specs=[pl.BlockSpec(memory_space=pltpu.SMEM)] + [vmem] * (count + 3),
        out_specs=[vmem, vmem],
        scratch_shapes=[
            pltpu.VMEM((total, width), BF16),
            pltpu.VMEM((total, 1), F32),
            pltpu.VMEM((total, ff), BF16),
        ],
        compiler_params=pltpu.CompilerParams(vmem_limit_bytes=SCRATCH),
        cost_estimate=pl.CostEstimate(
            flops=6 * max(total, 256) * width * ff, bytes_accessed=0, transcendentals=total * ff
        ),
    )(me, *blocks, w_gate, w_up, w_down)


def local(cores, order, tokens, routes, gates, w_gate, w_up, w_down):
    chips = len(order)
    experts = chips * cores
    rows, width = tokens.shape
    me = lax.axis_index("node").astype(jnp.int32).reshape(1)
    forth = [(order[i] * cores + c, order[(i + 1) % chips] * cores + c) for i in range(chips) for c in range(cores)]
    back = [(b, a) for a, b in forth]
    swap = [(chip * cores + c, chip * cores + 1 - c) for chip in range(chips) for c in range(cores)]
    right = lambda a: lax.ppermute(a, "node", forth)
    left = lambda a: lax.ppermute(a, "node", back)
    sibling = lambda a: lax.ppermute(a, "node", swap)

    own = pack(tokens, routes, gates, experts)
    far = chips // 2
    cut = rows // 2
    got = {0: own}
    for d in range(1, far):
        got[-d] = right(got[-(d - 1)])
        got[d] = left(got[d - 1])
    ends = (right(got[1 - far][:cut]), left(got[far - 1][cut:]))
    got[far] = jnp.concatenate(ends, axis=0)
    twin = {d: sibling(got[d]) for d in got}

    run = lambda at: ffn([got[d] for d in at] + [twin[d] for d in at], len(at), me, experts, w_gate, w_up, w_down)
    late = [far] + [s * (far - 1) for s in (1, -1)]
    near = [0, 1, -1]
    middle = [d for d in sorted(got, key=abs) if d not in late + near]
    mine, theirs = {}, {}
    for at in (late, middle, near):
        kept, sent = run(at)
        sent = sibling(sent)
        for j, d in enumerate(at):
            mine[d] = kept[j * rows : (j + 1) * rows]
            theirs[d] = sent[j * rows : (j + 1) * rows]

    both = lambda d: mine[d] + theirs[d].astype(F32)
    end = both(far).astype(BF16)
    a, b = right(end[:cut]), left(end[cut:])
    for d in range(far - 1, 0, -1):
        up, down = both(d), both(-d)
        if d == far - 1:
            up = jnp.concatenate([up[:cut] + a.astype(F32), up[cut:]], axis=0)
            down = jnp.concatenate([down[:cut], down[cut:] + b.astype(F32)], axis=0)
        else:
            up, down = up + a.astype(F32), down + b.astype(F32)
        a, b = right(up.astype(BF16)), left(down.astype(BF16))
    return (both(0) + a.astype(F32) + b.astype(F32)).astype(BF16)


def solution(mesh):
    cores, order = chip_layout(mesh)
    in_specs = (
        P(("groups", "node"), None),
        P(("groups", "node"), None),
        P(("groups", "node"), None),
        P("node", None, None),
        P("node", None, None),
        P("node", None, None),
    )
    out_specs = P(("groups", "node"), None)
    body = functools.partial(local, cores, order)
    return jax.shard_map(body, mesh=mesh, in_specs=in_specs, out_specs=out_specs, check_vma=False)
```

```python
import functools

import jax
import jax.numpy as jnp
from jax import lax
from jax.experimental import pallas as pl
from jax.experimental.pallas import tpu as pltpu
from jax.sharding import PartitionSpec as P

F32, BF16 = jnp.float32, jnp.bfloat16
SCRATCH = 16 * 2**20


def chip_layout(mesh):
    names = list(mesh.axis_names)
    count = mesh.shape["node"]
    row = mesh.devices.transpose([names.index(n) for n in names if n != "node"] + [names.index("node")])
    row = list(row.reshape(-1, count)[0])
    where = [tuple(getattr(d, "coords", None) or (i // 2,)) for i, d in enumerate(row)]
    cores = 2 if count % 2 == 0 and all(where[i] == where[i + 1] for i in range(0, count, 2)) else 1
    chips = where[::cores]
    order = list(range(len(chips)))
    axes = [a for a in range(len(chips[0])) if len({c[a] for c in chips}) > 1]
    if len(axes) == 2:
        short, long = sorted(axes, key=lambda a: len({c[a] for c in chips}))
        low = min(c[short] for c in chips)
        if len({c[short] for c in chips}) == 2:
            order.sort(key=lambda i: (chips[i][short], chips[i][long] if chips[i][short] == low else -chips[i][long]))
    return cores, order


def pack_kernel(experts, tok_hbm, routes_hbm, gates_hbm, out_ref, routes_ref, gates_ref, sems):
    rows, width = tok_hbm.shape
    extra = out_ref.shape[1] - width
    moves = [
        pltpu.make_async_copy(routes_hbm, routes_ref, sems.at[0]),
        pltpu.make_async_copy(gates_hbm, gates_ref, sems.at[1]),
        pltpu.make_async_copy(tok_hbm, out_ref.at[:, :width], sems.at[2]),
    ]
    for move in moves:
        move.start()
    for move in moves[:2]:
        move.wait()
    lane = lax.broadcasted_iota(jnp.int32, (extra, rows), 0)
    expert, piece = lax.rem(lane, experts), lax.div(lane, experts)
    weight = jnp.zeros((extra, rows), F32)
    for k in range(routes_ref.shape[0]):
        weight += jnp.where(routes_ref[k : k + 1] == expert, gates_ref[k : k + 1], 0.0)
    high = weight.astype(BF16).astype(F32)
    middle = (weight - high).astype(BF16).astype(F32)
    low = weight - high - middle
    table = jnp.where(piece == 0, high, jnp.where(piece == 1, middle, jnp.where(piece == 2, low, 0.0)))
    out_ref[:, width:] = table.T.astype(BF16)
    moves[2].wait()


def pack(tokens, routes, gates, experts):
    rows, width = tokens.shape
    extra = pl.cdiv(3 * experts, 128) * 128
    there = pl.BlockSpec(memory_space=pltpu.HBM)
    return pl.pallas_call(
        functools.partial(pack_kernel, experts),
        out_shape=pltpu.VMEM((rows, width + extra), BF16),
        in_specs=[there] * 3,
        out_specs=pl.BlockSpec(memory_space=pltpu.VMEM),
        scratch_shapes=[
            pltpu.VMEM(routes.shape[::-1], routes.dtype),
            pltpu.VMEM(gates.shape[::-1], gates.dtype),
            pltpu.SemaphoreType.DMA((3,)),
        ],
        compiler_params=pltpu.CompilerParams(vmem_limit_bytes=SCRATCH),
    )(hbm(tokens), hbm(routes.T), hbm(gates.T))


def hbm(a):
    return pltpu.with_memory_space_constraint(a, pltpu.HBM)


def vmem(a):
    return pltpu.with_memory_space_constraint(a, pltpu.VMEM)


def fetches(parts, source, target, sems):
    step = target.shape[2] // parts
    moves = []
    for i in range(parts):
        at = (slice(None), slice(None), slice(i * step, (i + 1) * step))
        moves.append(pltpu.make_async_copy(source.at[at], target.at[at], sems.at[i]))
        moves[-1].start()
    return moves


def load_kernel(parts, source, after, target, sems):
    step = target.shape[1] // parts
    moves = [
        pltpu.make_async_copy(
            source.at[:, i * step : (i + 1) * step], target.at[:, i * step : (i + 1) * step], sems.at[i]
        )
        for i in range(parts)
    ]
    for move in moves:
        move.start()
    for move in moves:
        move.wait()


def load(weight, after):
    parts = 8 if weight.shape[1] % 128 == 0 else 1
    return pl.pallas_call(
        functools.partial(load_kernel, parts),
        out_shape=pltpu.VMEM(weight.shape, weight.dtype),
        in_specs=[pl.BlockSpec(memory_space=pltpu.HBM), pl.BlockSpec(memory_space=pl.ANY)],
        out_specs=pl.BlockSpec(memory_space=pltpu.VMEM),
        scratch_shapes=[pltpu.SemaphoreType.DMA((parts,))],
        compiler_params=pltpu.CompilerParams(vmem_limit_bytes=SCRATCH),
        cost_estimate=pl.CostEstimate(flops=0, bytes_accessed=2 * weight.size, transcendentals=0),
    )(hbm(weight), after)


def gather_rows(blocks, x_ref):
    rows, width = blocks[0].shape[0], x_ref.shape[1]
    for at, ref in enumerate(blocks):
        x_ref[at * rows : (at + 1) * rows, :] = ref[:, :width]


def gather_weights(experts, me_ref, blocks, width, w_ref):
    rows = blocks[0].shape[0]
    for at, ref in enumerate(blocks):
        table = ref[:, width:].astype(F32)
        lane = lax.broadcasted_iota(jnp.int32, table.shape, 1)
        own = lax.rem(lane, experts) == me_ref[0]
        w_ref[at * rows : (at + 1) * rows, :] = jnp.sum(jnp.where(own, table, 0.0), axis=1, keepdims=True)


def first_half(x_ref, gate_ref, up_ref, h_ref, tile, begin, end):
    @pl.loop(begin // tile, end // tile)
    def _(j):
        at = pl.ds(pl.multiple_of(j * tile, tile), tile)
        gate = jnp.dot(x_ref[...], gate_ref[0, :, at], preferred_element_type=F32)
        upper = jnp.dot(x_ref[...], up_ref[0, :, at], preferred_element_type=F32)
        h_ref[:, at] = (gate / (1.0 + jnp.exp(-gate)) * upper).astype(BF16)


def second_half(h_ref, down_ref, w_ref, mine_ref, other_ref, tile, begin, end):
    half = mine_ref.shape[0]

    @pl.loop(begin // tile, end // tile)
    def _(j):
        at = pl.ds(pl.multiple_of(j * tile, tile), tile)
        out = jnp.dot(h_ref[...], down_ref[0, :, at], preferred_element_type=F32) * w_ref[...]
        mine_ref[:, at] = out[:half]
        other_ref[:, at] = out[half:].astype(BF16)


def tiles(width, ff):
    return (256 if ff % 256 == 0 else ff), next(t for t in (512, 256, 128, width) if width % t == 0)


def hidden_kernel(count, tile, parts, *refs):
    blocks, (gate_ref, source, h_ref, *rest) = refs[:count], refs[count:]
    if parts:
        up_ref, x_ref, sems = rest
        moves = fetches(parts, source, up_ref, sems)
    else:
        up_ref, (x_ref,), moves = source, rest, []
    gather_rows(blocks, x_ref)
    ff = h_ref.shape[1]
    for i in range(max(parts, 1)):
        if parts:
            moves[i].wait()
        first_half(x_ref, gate_ref, up_ref, h_ref, tile, i * ff // max(parts, 1), (i + 1) * ff // max(parts, 1))


def hidden(blocks, w_gate, w_up, fetch):
    count, rows = len(blocks), blocks[0].shape[0]
    _, width, ff = w_gate.shape
    tile, _ = tiles(width, ff)
    parts = (2 if ff % (2 * tile) == 0 else 1) if fetch else 0
    here = pl.BlockSpec(memory_space=pltpu.VMEM)
    return pl.pallas_call(
        functools.partial(hidden_kernel, count, tile, parts),
        out_shape=[pltpu.VMEM((count * rows, ff), BF16)] + [pltpu.VMEM(w_up.shape, BF16)] * fetch,
        in_specs=[here] * (count + 1) + [pl.BlockSpec(memory_space=pltpu.HBM if fetch else pltpu.VMEM)],
        out_specs=[here] * (1 + fetch),
        scratch_shapes=[pltpu.VMEM((count * rows, width), BF16)] + [pltpu.SemaphoreType.DMA((parts,))] * fetch,
        compiler_params=pltpu.CompilerParams(vmem_limit_bytes=SCRATCH),
        cost_estimate=pl.CostEstimate(
            flops=4 * max(count * rows, 256) * width * ff, bytes_accessed=0, transcendentals=count * rows * ff
        ),
    )(*blocks, vmem(w_gate), hbm(w_up) if fetch else vmem(w_up))


def output_kernel(count, experts, tile, parts, me_ref, *refs):
    blocks, (h_ref, source, mine_ref, other_ref, *rest) = refs[:count], refs[count:]
    if parts:
        down_ref, w_ref, sems = rest
        moves = fetches(parts, source, down_ref, sems)
    else:
        down_ref, (w_ref,), moves = source, rest, []
    width = mine_ref.shape[1]
    gather_weights(experts, me_ref, blocks, width, w_ref)
    for i in range(max(parts, 1)):
        if parts:
            moves[i].wait()
        begin, end = i * width // max(parts, 1), (i + 1) * width // max(parts, 1)
        second_half(h_ref, down_ref, w_ref, mine_ref, other_ref, tile, begin, end)


def output(blocks, mine, me, experts, h, w_down, fetch):
    count, rows = len(blocks), blocks[0].shape[0]
    _, ff, width = w_down.shape
    _, tile = tiles(width, ff)
    parts = width // tile if fetch else 0
    here = pl.BlockSpec(memory_space=pltpu.VMEM)
    return pl.pallas_call(
        functools.partial(output_kernel, count, experts, tile, parts),
        out_shape=[pltpu.VMEM((mine * rows, width), F32), pltpu.VMEM(((count - mine) * rows, width), BF16)]
        + [pltpu.VMEM(w_down.shape, BF16)] * fetch,
        in_specs=[pl.BlockSpec(memory_space=pltpu.SMEM)]
        + [here] * (count + 1)
        + [pl.BlockSpec(memory_space=pltpu.HBM if fetch else pltpu.VMEM)],
        out_specs=[here] * (2 + fetch),
        scratch_shapes=[pltpu.VMEM((count * rows, 1), F32)] + [pltpu.SemaphoreType.DMA((parts,))] * fetch,
        compiler_params=pltpu.CompilerParams(vmem_limit_bytes=SCRATCH),
        cost_estimate=pl.CostEstimate(
            flops=2 * max(count * rows, 256) * width * ff, bytes_accessed=0, transcendentals=0
        ),
    )(me, *blocks, h, hbm(w_down) if fetch else vmem(w_down))


def expert_kernel(count, experts, tile_ff, tile_d, me_ref, *refs):
    blocks, (gate_ref, up_ref, down_ref, mine_ref, other_ref, x_ref, w_ref, h_ref) = refs[:count], refs[count:]
    gather_rows(blocks, x_ref)
    gather_weights(experts, me_ref, blocks, x_ref.shape[1], w_ref)
    first_half(x_ref, gate_ref, up_ref, h_ref, tile_ff, 0, h_ref.shape[1])
    second_half(h_ref, down_ref, w_ref, mine_ref, other_ref, tile_d, 0, x_ref.shape[1])


def expert(blocks, mine, me, experts, w_gate, w_up, w_down):
    count, rows = len(blocks), blocks[0].shape[0]
    _, width, ff = w_gate.shape
    total = count * rows
    here = pl.BlockSpec(memory_space=pltpu.VMEM)
    return pl.pallas_call(
        functools.partial(expert_kernel, count, experts, *tiles(width, ff)),
        out_shape=[pltpu.VMEM((mine * rows, width), F32), pltpu.VMEM((total - mine * rows, width), BF16)],
        in_specs=[pl.BlockSpec(memory_space=pltpu.SMEM)] + [here] * (count + 3),
        out_specs=[here] * 2,
        scratch_shapes=[pltpu.VMEM((total, width), BF16), pltpu.VMEM((total, 1), F32), pltpu.VMEM((total, ff), BF16)],
        compiler_params=pltpu.CompilerParams(vmem_limit_bytes=SCRATCH),
        cost_estimate=pl.CostEstimate(
            flops=6 * max(total, 256) * width * ff, bytes_accessed=0, transcendentals=total * ff
        ),
    )(me, *blocks, vmem(w_gate), vmem(w_up), vmem(w_down))


def local(cores, order, tokens, routes, gates, w_gate, w_up, w_down):
    chips = len(order)
    experts = chips * cores
    rows, width = tokens.shape
    me = lax.axis_index("node").astype(jnp.int32).reshape(1)
    forth = [(order[i] * cores + c, order[(i + 1) % chips] * cores + c) for i in range(chips) for c in range(cores)]
    back = [(b, a) for a, b in forth]
    swap = [(chip * cores + c, chip * cores + 1 - c) for chip in range(chips) for c in range(cores)]
    right = lambda a: lax.ppermute(a, "node", forth)
    left = lambda a: lax.ppermute(a, "node", back)
    sibling = lambda a: lax.ppermute(a, "node", swap)
    together = lax.optimization_barrier

    far, cut = chips // 2, rows // 2
    own = pack(tokens, routes, gates, experts)
    got, twin = {0: own}, {}
    middle = [s * d for d in range(2, far - 1) for s in (1, -1)]
    late = [far, far - 1, 1 - far]
    for d in range(1, far):
        a, b = left(got[d - 1]), right(got[1 - d])
        new = {e: sibling(got[e]) for e in {d - 1, 1 - d}}
        if d == 1:
            w_gate, new, a, b = together((load(w_gate, own), new, a, b))
        elif d == 2:
            near = [got[0], got[1], got[-1], twin[0]]
            (h_near, w_up), new, a, b = together((hidden(near, w_gate, w_up, True), new, a, b))
        elif d == 3:
            (*near_out, w_down), new, a, b = together((output(near, 3, me, experts, h_near, w_down, True), new, a, b))
        else:
            new, a, b = together((new, a, b))
        got[d], got[-d] = a, b
        twin.update(new)
    ends = right(got[1 - far][:cut]), left(got[far - 1][cut:])
    new = {e: sibling(got[e]) for e in (far - 1, 1 - far)}
    rest = [got[d] for d in middle] + [twin[1], twin[-1]] + [twin[d] for d in middle]
    (h_rest,), ends, new, near_sent = together((hidden(rest, w_gate, w_up, False), ends, new, sibling(near_out[1])))
    twin.update(new)
    got[far] = jnp.concatenate(ends, axis=0)
    rest_out, twin[far] = together((output(rest, len(middle), me, experts, h_rest, w_down, False), sibling(got[far])))
    late_out = expert([got[d] for d in late] + [twin[d] for d in late], len(late), me, experts, w_gate, w_up, w_down)

    block = lambda a, j: a[j * rows : (j + 1) * rows]
    mine, theirs = {}, {0: near_sent}
    for j, d in enumerate((0, 1, -1)):
        mine[d] = block(near_out[0], j)
    rest_sent, late_sent = sibling(rest_out[1]), sibling(late_out[1])
    for j, d in enumerate(middle):
        mine[d] = block(rest_out[0], j)
    for j, d in enumerate([1, -1] + middle):
        theirs[d] = block(rest_sent, j)
    for j, d in enumerate(late):
        mine[d], theirs[d] = block(late_out[0], j), block(late_sent, j)

    split = width // 256 * 128
    spans = [slice(0, split), slice(split, width)] if split else [slice(0, width)]
    both = lambda d, s: mine[d][:, s] + theirs[d][:, s].astype(F32)
    ends = [both(far, s).astype(BF16) for s in spans]
    flow = [(right(end[:cut]), left(end[cut:])) for end in ends]
    added = None
    for d in range(far - 1, 0, -1):
        for i, s in enumerate(spans):
            a, b = flow[i]
            if added is not None:
                a, b, _ = together((a, b, added))
            up, down = both(d, s), both(-d, s)
            if d == far - 1:
                up = jnp.concatenate([up[:cut] + a.astype(F32), up[cut:]], axis=0)
                down = jnp.concatenate([down[:cut], down[cut:] + b.astype(F32)], axis=0)
            else:
                up, down = up + a.astype(F32), down + b.astype(F32)
            added = up.astype(BF16), down.astype(BF16)
            flow[i] = right(added[0]), left(added[1])
    out = [both(0, s) + flow[i][0].astype(F32) + flow[i][1].astype(F32) for i, s in enumerate(spans)]
    return jnp.concatenate([o.astype(BF16) for o in out], axis=1)


def solution(mesh):
    cores, order = chip_layout(mesh)
    in_specs = (
        P(("groups", "node"), None),
        P(("groups", "node"), None),
        P(("groups", "node"), None),
        P("node", None, None),
        P("node", None, None),
        P("node", None, None),
    )
    out_specs = P(("groups", "node"), None)
    body = functools.partial(local, cores, order)
    return jax.shard_map(body, mesh=mesh, in_specs=in_specs, out_specs=out_specs, check_vma=False)
```

```python
import functools

import jax
import jax.numpy as jnp
from jax import lax
from jax.experimental import pallas as pl
from jax.experimental.pallas import tpu as pltpu
from jax.sharding import PartitionSpec as P

F32, BF16 = jnp.float32, jnp.bfloat16
SCRATCH = 16 * 2**20


def chip_layout(mesh):
    names = list(mesh.axis_names)
    count = mesh.shape["node"]
    row = mesh.devices.transpose([names.index(n) for n in names if n != "node"] + [names.index("node")])
    row = list(row.reshape(-1, count)[0])
    where = [tuple(getattr(d, "coords", None) or (i // 2,)) for i, d in enumerate(row)]
    cores = 2 if count % 2 == 0 and all(where[i] == where[i + 1] for i in range(0, count, 2)) else 1
    chips = where[::cores]
    order = list(range(len(chips)))
    axes = [a for a in range(len(chips[0])) if len({c[a] for c in chips}) > 1]
    if len(axes) == 2:
        short, long = sorted(axes, key=lambda a: len({c[a] for c in chips}))
        low = min(c[short] for c in chips)
        if len({c[short] for c in chips}) == 2:
            order.sort(key=lambda i: (chips[i][short], chips[i][long] if chips[i][short] == low else -chips[i][long]))
    return cores, order


def pack_kernel(experts, tok_hbm, routes_hbm, gates_hbm, out_ref, routes_ref, gates_ref, sems):
    rows, width = tok_hbm.shape
    extra = out_ref.shape[1] - width
    moves = [
        pltpu.make_async_copy(routes_hbm, routes_ref, sems.at[0]),
        pltpu.make_async_copy(gates_hbm, gates_ref, sems.at[1]),
        pltpu.make_async_copy(tok_hbm, out_ref.at[:, :width], sems.at[2]),
    ]
    for move in moves:
        move.start()
    for move in moves[:2]:
        move.wait()
    lane = lax.broadcasted_iota(jnp.int32, (extra, rows), 0)
    expert, piece = lax.rem(lane, experts), lax.div(lane, experts)
    weight = jnp.zeros((extra, rows), F32)
    for k in range(routes_ref.shape[0]):
        weight += jnp.where(routes_ref[k : k + 1] == expert, gates_ref[k : k + 1], 0.0)
    high = weight.astype(BF16).astype(F32)
    middle = (weight - high).astype(BF16).astype(F32)
    low = weight - high - middle
    table = jnp.where(piece == 0, high, jnp.where(piece == 1, middle, jnp.where(piece == 2, low, 0.0)))
    out_ref[:, width:] = table.T.astype(BF16)
    moves[2].wait()


def pack(tokens, routes, gates, experts):
    rows, width = tokens.shape
    extra = pl.cdiv(3 * experts, 128) * 128
    there = pl.BlockSpec(memory_space=pltpu.HBM)
    return pl.pallas_call(
        functools.partial(pack_kernel, experts),
        out_shape=pltpu.VMEM((rows, width + extra), BF16),
        in_specs=[there] * 3,
        out_specs=pl.BlockSpec(memory_space=pltpu.VMEM),
        scratch_shapes=[
            pltpu.VMEM(routes.shape[::-1], routes.dtype),
            pltpu.VMEM(gates.shape[::-1], gates.dtype),
            pltpu.SemaphoreType.DMA((3,)),
        ],
        compiler_params=pltpu.CompilerParams(vmem_limit_bytes=SCRATCH),
    )(hbm(tokens), hbm(routes.T), hbm(gates.T))


def hbm(a):
    return pltpu.with_memory_space_constraint(a, pltpu.HBM)


def vmem(a):
    return pltpu.with_memory_space_constraint(a, pltpu.VMEM)


def fetches(parts, source, target, sems):
    step = target.shape[2] // parts
    moves = []
    for i in range(parts):
        at = (slice(None), slice(None), slice(i * step, (i + 1) * step))
        moves.append(pltpu.make_async_copy(source.at[at], target.at[at], sems.at[i]))
        moves[-1].start()
    return moves


def load_kernel(parts, source, after, target, sems):
    step = target.shape[1] // parts
    moves = [
        pltpu.make_async_copy(
            source.at[:, i * step : (i + 1) * step], target.at[:, i * step : (i + 1) * step], sems.at[i]
        )
        for i in range(parts)
    ]
    for move in moves:
        move.start()
    for move in moves:
        move.wait()


def load(weight, after):
    parts = 8 if weight.shape[1] % 128 == 0 else 1
    return pl.pallas_call(
        functools.partial(load_kernel, parts),
        out_shape=pltpu.VMEM(weight.shape, weight.dtype),
        in_specs=[pl.BlockSpec(memory_space=pltpu.HBM), pl.BlockSpec(memory_space=pl.ANY)],
        out_specs=pl.BlockSpec(memory_space=pltpu.VMEM),
        scratch_shapes=[pltpu.SemaphoreType.DMA((parts,))],
        compiler_params=pltpu.CompilerParams(vmem_limit_bytes=SCRATCH),
        cost_estimate=pl.CostEstimate(flops=0, bytes_accessed=2 * weight.size, transcendentals=0),
    )(hbm(weight), after)


def gather_rows(blocks, x_ref):
    rows, width = blocks[0].shape[0], x_ref.shape[1]
    for at, ref in enumerate(blocks):
        x_ref[at * rows : (at + 1) * rows, :] = ref[:, :width]


def gather_weights(experts, blocks, width, w_ref):
    me = lax.axis_index("node")
    rows = blocks[0].shape[0]
    for at, ref in enumerate(blocks):
        table = ref[:, width:].astype(F32)
        lane = lax.broadcasted_iota(jnp.int32, table.shape, 1)
        own = lax.rem(lane, experts) == me
        w_ref[at * rows : (at + 1) * rows, :] = jnp.sum(jnp.where(own, table, 0.0), axis=1, keepdims=True)


def first_half(x_ref, gate_ref, up_ref, h_ref, tile, begin, end):
    @pl.loop(begin // tile, end // tile)
    def _(j):
        at = pl.ds(pl.multiple_of(j * tile, tile), tile)
        gate = jnp.dot(x_ref[...], gate_ref[0, :, at], preferred_element_type=F32)
        upper = jnp.dot(x_ref[...], up_ref[0, :, at], preferred_element_type=F32)
        h_ref[:, at] = (gate / (1.0 + jnp.exp(-gate)) * upper).astype(BF16)


def second_half(h_ref, down_ref, w_ref, mine_ref, other_ref, tile, begin, end):
    half = mine_ref.shape[0]

    @pl.loop(begin // tile, end // tile)
    def _(j):
        at = pl.ds(pl.multiple_of(j * tile, tile), tile)
        out = jnp.dot(h_ref[...], down_ref[0, :, at], preferred_element_type=F32) * w_ref[...]
        mine_ref[:, at] = out[:half]
        other_ref[:, at] = out[half:].astype(BF16)


def tiles(width, ff):
    return (256 if ff % 256 == 0 else ff), next(t for t in (512, 256, 128, width) if width % t == 0)


def hidden_kernel(count, tile, parts, *refs):
    blocks, (gate_ref, source, h_ref, *rest) = refs[:count], refs[count:]
    if parts:
        up_ref, x_ref, sems = rest
        moves = fetches(parts, source, up_ref, sems)
    else:
        up_ref, (x_ref,), moves = source, rest, []
    gather_rows(blocks, x_ref)
    ff = h_ref.shape[1]
    for i in range(max(parts, 1)):
        if parts:
            moves[i].wait()
        first_half(x_ref, gate_ref, up_ref, h_ref, tile, i * ff // max(parts, 1), (i + 1) * ff // max(parts, 1))


def hidden(blocks, w_gate, w_up, fetch):
    count, rows = len(blocks), blocks[0].shape[0]
    _, width, ff = w_gate.shape
    tile, _ = tiles(width, ff)
    parts = (2 if ff % (2 * tile) == 0 else 1) if fetch else 0
    here = pl.BlockSpec(memory_space=pltpu.VMEM)
    return pl.pallas_call(
        functools.partial(hidden_kernel, count, tile, parts),
        out_shape=[pltpu.VMEM((count * rows, ff), BF16)] + [pltpu.VMEM(w_up.shape, BF16)] * fetch,
        in_specs=[here] * (count + 1) + [pl.BlockSpec(memory_space=pltpu.HBM if fetch else pltpu.VMEM)],
        out_specs=[here] * (1 + fetch),
        scratch_shapes=[pltpu.VMEM((count * rows, width), BF16)] + [pltpu.SemaphoreType.DMA((parts,))] * fetch,
        compiler_params=pltpu.CompilerParams(vmem_limit_bytes=SCRATCH),
        cost_estimate=pl.CostEstimate(
            flops=4 * max(count * rows, 256) * width * ff, bytes_accessed=0, transcendentals=count * rows * ff
        ),
    )(*blocks, vmem(w_gate), hbm(w_up) if fetch else vmem(w_up))


def output_kernel(count, experts, tile, parts, *refs):
    blocks, (h_ref, source, mine_ref, other_ref, *rest) = refs[:count], refs[count:]
    if parts:
        down_ref, w_ref, sems = rest
        moves = fetches(parts, source, down_ref, sems)
    else:
        down_ref, (w_ref,), moves = source, rest, []
    width = mine_ref.shape[1]
    gather_weights(experts, blocks, width, w_ref)
    for i in range(max(parts, 1)):
        if parts:
            moves[i].wait()
        begin, end = i * width // max(parts, 1), (i + 1) * width // max(parts, 1)
        second_half(h_ref, down_ref, w_ref, mine_ref, other_ref, tile, begin, end)


def output(blocks, mine, experts, h, w_down, fetch):
    count, rows = len(blocks), blocks[0].shape[0]
    _, ff, width = w_down.shape
    _, tile = tiles(width, ff)
    parts = width // tile if fetch else 0
    here = pl.BlockSpec(memory_space=pltpu.VMEM)
    return pl.pallas_call(
        functools.partial(output_kernel, count, experts, tile, parts),
        out_shape=[pltpu.VMEM((mine * rows, width), F32), pltpu.VMEM(((count - mine) * rows, width), BF16)]
        + [pltpu.VMEM(w_down.shape, BF16)] * fetch,
        in_specs=[here] * (count + 1)
        + [pl.BlockSpec(memory_space=pltpu.HBM if fetch else pltpu.VMEM)],
        out_specs=[here] * (2 + fetch),
        scratch_shapes=[pltpu.VMEM((count * rows, 1), F32)] + [pltpu.SemaphoreType.DMA((parts,))] * fetch,
        compiler_params=pltpu.CompilerParams(vmem_limit_bytes=SCRATCH),
        cost_estimate=pl.CostEstimate(
            flops=2 * max(count * rows, 256) * width * ff, bytes_accessed=0, transcendentals=0
        ),
    )(*blocks, h, hbm(w_down) if fetch else vmem(w_down))


def expert_kernel(count, experts, tile_ff, tile_d, *refs):
    blocks, (gate_ref, up_ref, down_ref, mine_ref, other_ref, x_ref, w_ref, h_ref) = refs[:count], refs[count:]
    gather_rows(blocks, x_ref)
    gather_weights(experts, blocks, x_ref.shape[1], w_ref)
    first_half(x_ref, gate_ref, up_ref, h_ref, tile_ff, 0, h_ref.shape[1])
    second_half(h_ref, down_ref, w_ref, mine_ref, other_ref, tile_d, 0, x_ref.shape[1])


def expert(blocks, mine, experts, w_gate, w_up, w_down):
    count, rows = len(blocks), blocks[0].shape[0]
    _, width, ff = w_gate.shape
    total = count * rows
    here = pl.BlockSpec(memory_space=pltpu.VMEM)
    return pl.pallas_call(
        functools.partial(expert_kernel, count, experts, *tiles(width, ff)),
        out_shape=[pltpu.VMEM((mine * rows, width), F32), pltpu.VMEM((total - mine * rows, width), BF16)],
        in_specs=[here] * (count + 3),
        out_specs=[here] * 2,
        scratch_shapes=[pltpu.VMEM((total, width), BF16), pltpu.VMEM((total, 1), F32), pltpu.VMEM((total, ff), BF16)],
        compiler_params=pltpu.CompilerParams(vmem_limit_bytes=SCRATCH),
        cost_estimate=pl.CostEstimate(
            flops=6 * max(total, 256) * width * ff, bytes_accessed=0, transcendentals=total * ff
        ),
    )(*blocks, vmem(w_gate), vmem(w_up), vmem(w_down))


def local(cores, order, tokens, routes, gates, w_gate, w_up, w_down):
    chips = len(order)
    experts = chips * cores
    rows, width = tokens.shape
    forth = [(order[i] * cores + c, order[(i + 1) % chips] * cores + c) for i in range(chips) for c in range(cores)]
    back = [(b, a) for a, b in forth]
    swap = [(chip * cores + c, chip * cores + 1 - c) for chip in range(chips) for c in range(cores)]
    right = lambda a: lax.ppermute(a, "node", forth)
    left = lambda a: lax.ppermute(a, "node", back)
    sibling = lambda a: lax.ppermute(a, "node", swap)
    together = lax.optimization_barrier

    far, cut = chips // 2, rows // 2
    own = pack(tokens, routes, gates, experts)
    got, twin = {0: own}, {}
    middle = [s * d for d in range(2, far - 1) for s in (1, -1)]
    late = [far, far - 1, 1 - far]
    for d in range(1, far):
        a, b = left(got[d - 1]), right(got[1 - d])
        new = {e: sibling(got[e]) for e in {d - 1, 1 - d}}
        if d == 1:
            w_gate, new, a, b = together((load(w_gate, own), new, a, b))
        elif d == 2:
            near = [got[0], got[1], got[-1], twin[0]]
            (h_near, w_up), new, a, b = together((hidden(near, w_gate, w_up, True), new, a, b))
        elif d == 3:
            (*near_out, w_down), new, a, b = together((output(near, 3, experts, h_near, w_down, True), new, a, b))
        else:
            new, a, b = together((new, a, b))
        got[d], got[-d] = a, b
        twin.update(new)
    ends = right(got[1 - far][:cut]), left(got[far - 1][cut:])
    new = {e: sibling(got[e]) for e in (far - 1, 1 - far)}
    rest = [got[d] for d in middle] + [twin[1], twin[-1]] + [twin[d] for d in middle]
    (h_rest,), ends, new, near_sent = together((hidden(rest, w_gate, w_up, False), ends, new, sibling(near_out[1])))
    twin.update(new)
    got[far] = jnp.concatenate(ends, axis=0)
    rest_out, twin[far] = together((output(rest, len(middle), experts, h_rest, w_down, False), sibling(got[far])))
    late_out = expert([got[d] for d in late] + [twin[d] for d in late], len(late), experts, w_gate, w_up, w_down)

    block = lambda a, j: a[j * rows : (j + 1) * rows]
    mine, theirs = {}, {0: near_sent}
    for j, d in enumerate((0, 1, -1)):
        mine[d] = block(near_out[0], j)
    rest_sent, late_sent = sibling(rest_out[1]), sibling(late_out[1])
    for j, d in enumerate(middle):
        mine[d] = block(rest_out[0], j)
    for j, d in enumerate([1, -1] + middle):
        theirs[d] = block(rest_sent, j)
    for j, d in enumerate(late):
        mine[d], theirs[d] = block(late_out[0], j), block(late_sent, j)

    split = width // 256 * 128
    spans = [slice(0, split), slice(split, width)] if split else [slice(0, width)]
    both = lambda d, s: mine[d][:, s] + theirs[d][:, s].astype(F32)
    ends = [both(far, s).astype(BF16) for s in spans]
    flow = [(right(end[:cut]), left(end[cut:])) for end in ends]
    added = None
    for d in range(far - 1, 0, -1):
        for i, s in enumerate(spans):
            a, b = flow[i]
            if added is not None:
                a, b, _ = together((a, b, added))
            up, down = both(d, s), both(-d, s)
            if d == far - 1:
                up = jnp.concatenate([up[:cut] + a.astype(F32), up[cut:]], axis=0)
                down = jnp.concatenate([down[:cut], down[cut:] + b.astype(F32)], axis=0)
            else:
                up, down = up + a.astype(F32), down + b.astype(F32)
            added = up.astype(BF16), down.astype(BF16)
            flow[i] = right(added[0]), left(added[1])
    out = [both(0, s) + flow[i][0].astype(F32) + flow[i][1].astype(F32) for i, s in enumerate(spans)]
    return jnp.concatenate([o.astype(BF16) for o in out], axis=1)


def solution(mesh):
    cores, order = chip_layout(mesh)
    in_specs = (
        P(("groups", "node"), None),
        P(("groups", "node"), None),
        P(("groups", "node"), None),
        P("node", None, None),
        P("node", None, None),
        P("node", None, None),
    )
    out_specs = P(("groups", "node"), None)
    body = functools.partial(local, cores, order)
    return jax.shard_map(body, mesh=mesh, in_specs=in_specs, out_specs=out_specs, check_vma=False)
```

```python
import functools

import jax
import jax.numpy as jnp
from jax import lax
from jax.experimental import pallas as pl
from jax.experimental.pallas import tpu as pltpu
from jax.sharding import PartitionSpec as P

F32, BF16 = jnp.float32, jnp.bfloat16
SCRATCH = 16 * 2**20


def chip_layout(mesh):
    names = list(mesh.axis_names)
    count = mesh.shape["node"]
    row = mesh.devices.transpose([names.index(n) for n in names if n != "node"] + [names.index("node")])
    row = list(row.reshape(-1, count)[0])
    where = [tuple(getattr(d, "coords", None) or (i // 2,)) for i, d in enumerate(row)]
    cores = 2 if count % 2 == 0 and all(where[i] == where[i + 1] for i in range(0, count, 2)) else 1
    chips = where[::cores]
    order = list(range(len(chips)))
    axes = [a for a in range(len(chips[0])) if len({c[a] for c in chips}) > 1]
    if len(axes) == 2:
        short, long = sorted(axes, key=lambda a: len({c[a] for c in chips}))
        low = min(c[short] for c in chips)
        if len({c[short] for c in chips}) == 2:
            order.sort(key=lambda i: (chips[i][short], chips[i][long] if chips[i][short] == low else -chips[i][long]))
    return cores, order


def pack_kernel(experts, tok_hbm, routes_hbm, gates_hbm, out_ref, routes_ref, gates_ref, sems):
    rows, width = tok_hbm.shape
    extra = out_ref.shape[1] - width
    moves = [
        pltpu.make_async_copy(routes_hbm, routes_ref, sems.at[0]),
        pltpu.make_async_copy(gates_hbm, gates_ref, sems.at[1]),
        pltpu.make_async_copy(tok_hbm, out_ref.at[:, :width], sems.at[2]),
    ]
    for move in moves:
        move.start()
    for move in moves[:2]:
        move.wait()
    lane = lax.broadcasted_iota(jnp.int32, (extra, rows), 0)
    expert, piece = lax.rem(lane, experts), lax.div(lane, experts)
    weight = jnp.zeros((extra, rows), F32)
    for k in range(routes_ref.shape[0]):
        weight += jnp.where(routes_ref[k : k + 1] == expert, gates_ref[k : k + 1], 0.0)
    high = weight.astype(BF16).astype(F32)
    middle = (weight - high).astype(BF16).astype(F32)
    low = weight - high - middle
    table = jnp.where(piece == 0, high, jnp.where(piece == 1, middle, jnp.where(piece == 2, low, 0.0)))
    out_ref[:, width:] = table.T.astype(BF16)
    moves[2].wait()


def pack(tokens, routes, gates, experts):
    rows, width = tokens.shape
    extra = pl.cdiv(3 * experts, 128) * 128
    there = pl.BlockSpec(memory_space=pltpu.HBM)
    return pl.pallas_call(
        functools.partial(pack_kernel, experts),
        out_shape=pltpu.VMEM((rows, width + extra), BF16),
        in_specs=[there] * 3,
        out_specs=pl.BlockSpec(memory_space=pltpu.VMEM),
        scratch_shapes=[
            pltpu.VMEM(routes.shape[::-1], routes.dtype),
            pltpu.VMEM(gates.shape[::-1], gates.dtype),
            pltpu.SemaphoreType.DMA((3,)),
        ],
        compiler_params=pltpu.CompilerParams(vmem_limit_bytes=SCRATCH),
    )(hbm(tokens), hbm(routes.T), hbm(gates.T))


def hbm(a):
    return pltpu.with_memory_space_constraint(a, pltpu.HBM)


def vmem(a):
    return pltpu.with_memory_space_constraint(a, pltpu.VMEM)


def fetches(parts, source, target, sems):
    step = target.shape[2] // parts
    moves = []
    for i in range(parts):
        at = (slice(None), slice(None), slice(i * step, (i + 1) * step))
        moves.append(pltpu.make_async_copy(source.at[at], target.at[at], sems.at[i]))
        moves[-1].start()
    return moves


def load_kernel(parts, source, after, target, sems):
    step = target.shape[1] // parts
    moves = [
        pltpu.make_async_copy(
            source.at[:, i * step : (i + 1) * step], target.at[:, i * step : (i + 1) * step], sems.at[i]
        )
        for i in range(parts)
    ]
    for move in moves:
        move.start()
    for move in moves:
        move.wait()


def load(weight, after):
    parts = 8 if weight.shape[1] % 128 == 0 else 1
    return pl.pallas_call(
        functools.partial(load_kernel, parts),
        out_shape=pltpu.VMEM(weight.shape, weight.dtype),
        in_specs=[pl.BlockSpec(memory_space=pltpu.HBM), pl.BlockSpec(memory_space=pl.ANY)],
        out_specs=pl.BlockSpec(memory_space=pltpu.VMEM),
        scratch_shapes=[pltpu.SemaphoreType.DMA((parts,))],
        compiler_params=pltpu.CompilerParams(vmem_limit_bytes=SCRATCH),
        cost_estimate=pl.CostEstimate(flops=0, bytes_accessed=2 * weight.size, transcendentals=0),
    )(hbm(weight), after)


def gather_rows(blocks, x_ref):
    rows, width = blocks[0].shape[0], x_ref.shape[1]
    for at, ref in enumerate(blocks):
        x_ref[at * rows : (at + 1) * rows, :] = ref[:, :width]


def gather_weights(experts, blocks, width, w_ref):
    me = lax.axis_index("node")
    rows = blocks[0].shape[0]
    for at, ref in enumerate(blocks):
        table = ref[:, width:].astype(F32)
        lane = lax.broadcasted_iota(jnp.int32, table.shape, 1)
        own = lax.rem(lane, experts) == me
        w_ref[at * rows : (at + 1) * rows, :] = jnp.sum(jnp.where(own, table, 0.0), axis=1, keepdims=True)


def first_half(x_ref, gate_ref, up_ref, h_ref, tile, begin, end):
    for j in range(begin // tile, end // tile):
        at = slice(j * tile, (j + 1) * tile)
        gate = jnp.dot(x_ref[...], gate_ref[0, :, at], preferred_element_type=F32)
        upper = jnp.dot(x_ref[...], up_ref[0, :, at], preferred_element_type=F32)
        h_ref[:, at] = (gate / (1.0 + jnp.exp(-gate)) * upper).astype(BF16)


def second_half(h_ref, down_ref, w_ref, out_refs, tile, begin, end):
    for j in range(begin // tile, end // tile):
        at = slice(j * tile, (j + 1) * tile)
        out = jnp.dot(h_ref[...], down_ref[0, :, at], preferred_element_type=F32) * w_ref[...]
        row = 0
        for ref in out_refs:
            ref[:, at] = out[row : row + ref.shape[0]].astype(ref.dtype)
            row += ref.shape[0]


def tiles(width, ff):
    return (256 if ff % 256 == 0 else ff), next(t for t in (512, 256, 128, width) if width % t == 0)


def hidden_kernel(count, tile, parts, *refs):
    blocks, (gate_ref, source, h_ref, *rest) = refs[:count], refs[count:]
    if parts:
        up_ref, x_ref, sems = rest
        moves = fetches(parts, source, up_ref, sems)
    else:
        up_ref, (x_ref,), moves = source, rest, []
    gather_rows(blocks, x_ref)
    ff = h_ref.shape[1]
    for i in range(max(parts, 1)):
        if parts:
            moves[i].wait()
        first_half(x_ref, gate_ref, up_ref, h_ref, tile, i * ff // max(parts, 1), (i + 1) * ff // max(parts, 1))


def hidden(blocks, w_gate, w_up, fetch):
    count, rows = len(blocks), blocks[0].shape[0]
    _, width, ff = w_gate.shape
    tile, _ = tiles(width, ff)
    parts = (2 if ff % (2 * tile) == 0 else 1) if fetch else 0
    here = pl.BlockSpec(memory_space=pltpu.VMEM)
    return pl.pallas_call(
        functools.partial(hidden_kernel, count, tile, parts),
        out_shape=[pltpu.VMEM((count * rows, ff), BF16)] + [pltpu.VMEM(w_up.shape, BF16)] * fetch,
        in_specs=[here] * (count + 1) + [pl.BlockSpec(memory_space=pltpu.HBM if fetch else pltpu.VMEM)],
        out_specs=[here] * (1 + fetch),
        scratch_shapes=[pltpu.VMEM((count * rows, width), BF16)] + [pltpu.SemaphoreType.DMA((parts,))] * fetch,
        compiler_params=pltpu.CompilerParams(vmem_limit_bytes=SCRATCH),
        cost_estimate=pl.CostEstimate(
            flops=4 * max(count * rows, 256) * width * ff, bytes_accessed=0, transcendentals=count * rows * ff
        ),
    )(*blocks, vmem(w_gate), hbm(w_up) if fetch else vmem(w_up))


def output_kernel(count, experts, tile, parts, *refs):
    blocks, (h_ref, source, mine_ref, other_ref, *rest) = refs[:count], refs[count:]
    if parts:
        down_ref, w_ref, sems = rest
        moves = fetches(parts, source, down_ref, sems)
    else:
        down_ref, (w_ref,), moves = source, rest, []
    width = mine_ref.shape[1]
    gather_weights(experts, blocks, width, w_ref)
    for i in range(max(parts, 1)):
        if parts:
            moves[i].wait()
        begin, end = i * width // max(parts, 1), (i + 1) * width // max(parts, 1)
        second_half(h_ref, down_ref, w_ref, [mine_ref, other_ref], tile, begin, end)


def output(blocks, mine, experts, h, w_down, fetch):
    count, rows = len(blocks), blocks[0].shape[0]
    _, ff, width = w_down.shape
    _, tile = tiles(width, ff)
    parts = width // tile if fetch else 0
    here = pl.BlockSpec(memory_space=pltpu.VMEM)
    return pl.pallas_call(
        functools.partial(output_kernel, count, experts, tile, parts),
        out_shape=[pltpu.VMEM((mine * rows, width), F32), pltpu.VMEM(((count - mine) * rows, width), BF16)]
        + [pltpu.VMEM(w_down.shape, BF16)] * fetch,
        in_specs=[here] * (count + 1)
        + [pl.BlockSpec(memory_space=pltpu.HBM if fetch else pltpu.VMEM)],
        out_specs=[here] * (2 + fetch),
        scratch_shapes=[pltpu.VMEM((count * rows, 1), F32)] + [pltpu.SemaphoreType.DMA((parts,))] * fetch,
        compiler_params=pltpu.CompilerParams(vmem_limit_bytes=SCRATCH),
        cost_estimate=pl.CostEstimate(
            flops=2 * max(count * rows, 256) * width * ff, bytes_accessed=0, transcendentals=0
        ),
    )(*blocks, h, hbm(w_down) if fetch else vmem(w_down))


def expert_kernel(count, experts, tile_ff, tile_d, *refs):
    blocks, (gate_ref, up_ref, down_ref, mine_ref, first_ref, other_ref, x_ref, w_ref, h_ref) = refs[:count], refs[count:]
    gather_rows(blocks, x_ref)
    gather_weights(experts, blocks, x_ref.shape[1], w_ref)
    first_half(x_ref, gate_ref, up_ref, h_ref, tile_ff, 0, h_ref.shape[1])
    second_half(h_ref, down_ref, w_ref, [mine_ref, first_ref, other_ref], tile_d, 0, x_ref.shape[1])


def expert(blocks, mine, experts, w_gate, w_up, w_down):
    count, rows = len(blocks), blocks[0].shape[0]
    _, width, ff = w_gate.shape
    total = count * rows
    here = pl.BlockSpec(memory_space=pltpu.VMEM)
    return pl.pallas_call(
        functools.partial(expert_kernel, count, experts, *tiles(width, ff)),
        out_shape=[
            pltpu.VMEM((mine * rows, width), F32),
            pltpu.VMEM((rows, width), BF16),
            pltpu.VMEM((total - (mine + 1) * rows, width), BF16),
        ],
        in_specs=[here] * (count + 3),
        out_specs=[here] * 3,
        scratch_shapes=[pltpu.VMEM((total, width), BF16), pltpu.VMEM((total, 1), F32), pltpu.VMEM((total, ff), BF16)],
        compiler_params=pltpu.CompilerParams(vmem_limit_bytes=SCRATCH),
        cost_estimate=pl.CostEstimate(
            flops=6 * max(total, 256) * width * ff, bytes_accessed=0, transcendentals=total * ff
        ),
    )(*blocks, vmem(w_gate), vmem(w_up), vmem(w_down))


def local(cores, order, tokens, routes, gates, w_gate, w_up, w_down):
    chips = len(order)
    experts = chips * cores
    rows, width = tokens.shape
    forth = [(order[i] * cores + c, order[(i + 1) % chips] * cores + c) for i in range(chips) for c in range(cores)]
    back = [(b, a) for a, b in forth]
    swap = [(chip * cores + c, chip * cores + 1 - c) for chip in range(chips) for c in range(cores)]
    right = lambda a: lax.ppermute(a, "node", forth)
    left = lambda a: lax.ppermute(a, "node", back)
    sibling = lambda a: lax.ppermute(a, "node", swap)
    together = lax.optimization_barrier

    far, cut = chips // 2, rows // 2
    own = pack(tokens, routes, gates, experts)
    got, twin = {0: own}, {}
    middle = [s * d for d in range(2, far - 1) for s in (1, -1)]
    late = [far, far - 1, 1 - far]
    for d in range(1, far):
        a, b = left(got[d - 1]), right(got[1 - d])
        new = {e: sibling(got[e]) for e in {d - 1, 1 - d}}
        if d == 1:
            w_gate, new, a, b = together((load(w_gate, own), new, a, b))
        elif d == 2:
            near = [got[0], got[1], got[-1], twin[0]]
            (h_near, w_up), new, a, b = together((hidden(near, w_gate, w_up, True), new, a, b))
        elif d == 3:
            (*near_out, w_down), new, a, b = together((output(near, 3, experts, h_near, w_down, True), new, a, b))
        else:
            new, a, b = together((new, a, b))
        got[d], got[-d] = a, b
        twin.update(new)
    ends = right(got[1 - far][:cut]), left(got[far - 1][cut:])
    new = {e: sibling(got[e]) for e in (far - 1, 1 - far)}
    rest = [got[d] for d in middle] + [twin[1], twin[-1]] + [twin[d] for d in middle]
    (h_rest,), ends, new, near_sent = together((hidden(rest, w_gate, w_up, False), ends, new, sibling(near_out[1])))
    twin.update(new)
    got[far] = jnp.concatenate(ends, axis=0)
    rest_out, twin[far] = together((output(rest, len(middle), experts, h_rest, w_down, False), sibling(got[far])))
    late_out = expert([got[d] for d in late] + [twin[d] for d in late], len(late), experts, w_gate, w_up, w_down)

    block = lambda a, j: a[j * rows : (j + 1) * rows]
    mine, theirs = {}, {0: near_sent}
    for j, d in enumerate((0, 1, -1)):
        mine[d] = block(near_out[0], j)
    mine[far], theirs[far] = block(late_out[0], 0), sibling(late_out[1])
    end = (mine[far] + theirs[far].astype(F32)).astype(BF16)
    late_sent, rest_sent, _ = together((sibling(late_out[2]), sibling(rest_out[1]), end))
    for j, d in enumerate(middle):
        mine[d] = block(rest_out[0], j)
    for j, d in enumerate([1, -1] + middle):
        theirs[d] = block(rest_sent, j)
    for j, d in enumerate(late[1:]):
        mine[d], theirs[d] = block(late_out[0], j + 1), block(late_sent, j)

    both = lambda d: mine[d] + theirs[d].astype(F32)
    a, b = right(end[:cut]), left(end[cut:])
    for d in range(far - 1, 0, -1):
        up = both(d)
        up = jnp.concatenate([up[:cut] + a.astype(F32), up[cut:]], axis=0) if d == far - 1 else up + a.astype(F32)
        up = up.astype(BF16)
        b, _ = together((b, up))
        down = both(-d)
        down = jnp.concatenate([down[:cut], down[cut:] + b.astype(F32)], axis=0) if d == far - 1 else down + b.astype(F32)
        down = down.astype(BF16)
        a, _ = together((right(up), down))
        b = left(down)
    return (both(0) + a.astype(F32) + b.astype(F32)).astype(BF16)


def solution(mesh):
    cores, order = chip_layout(mesh)
    in_specs = (
        P(("groups", "node"), None),
        P(("groups", "node"), None),
        P(("groups", "node"), None),
        P("node", None, None),
        P("node", None, None),
        P("node", None, None),
    )
    out_specs = P(("groups", "node"), None)
    body = functools.partial(local, cores, order)
    return jax.shard_map(body, mesh=mesh, in_specs=in_specs, out_specs=out_specs, check_vma=False)
```

```python
import functools

import jax
import jax.numpy as jnp
from jax import lax
from jax.experimental import pallas as pl
from jax.experimental.pallas import tpu as pltpu
from jax.sharding import PartitionSpec as P

F32, BF16 = jnp.float32, jnp.bfloat16
SCRATCH = 16 * 2**20


def chip_layout(mesh):
    names = list(mesh.axis_names)
    count = mesh.shape["node"]
    row = mesh.devices.transpose([names.index(n) for n in names if n != "node"] + [names.index("node")])
    row = list(row.reshape(-1, count)[0])
    where = [tuple(getattr(d, "coords", None) or (i // 2,)) for i, d in enumerate(row)]
    cores = 2 if count % 2 == 0 and all(where[i] == where[i + 1] for i in range(0, count, 2)) else 1
    chips = where[::cores]
    order = list(range(len(chips)))
    axes = [a for a in range(len(chips[0])) if len({c[a] for c in chips}) > 1]
    if len(axes) == 2:
        short, long = sorted(axes, key=lambda a: len({c[a] for c in chips}))
        low = min(c[short] for c in chips)
        if len({c[short] for c in chips}) == 2:
            order.sort(key=lambda i: (chips[i][short], chips[i][long] if chips[i][short] == low else -chips[i][long]))
    return cores, order


def pack_kernel(experts, tok_hbm, routes_hbm, gates_hbm, out_ref, routes_ref, gates_ref, sems):
    rows, width = tok_hbm.shape
    extra = out_ref.shape[1] - width
    moves = [
        pltpu.make_async_copy(routes_hbm, routes_ref, sems.at[0]),
        pltpu.make_async_copy(gates_hbm, gates_ref, sems.at[1]),
        pltpu.make_async_copy(tok_hbm, out_ref.at[:, :width], sems.at[2]),
    ]
    for move in moves:
        move.start()
    for move in moves[:2]:
        move.wait()
    lane = lax.broadcasted_iota(jnp.int32, (extra, rows), 0)
    expert, piece = lax.rem(lane, experts), lax.div(lane, experts)
    weight = jnp.zeros((extra, rows), F32)
    for k in range(routes_ref.shape[0]):
        weight += jnp.where(routes_ref[k : k + 1] == expert, gates_ref[k : k + 1], 0.0)
    high = weight.astype(BF16).astype(F32)
    middle = (weight - high).astype(BF16).astype(F32)
    low = weight - high - middle
    table = jnp.where(piece == 0, high, jnp.where(piece == 1, middle, jnp.where(piece == 2, low, 0.0)))
    out_ref[:, width:] = table.T.astype(BF16)
    moves[2].wait()


def pack(tokens, routes, gates, experts):
    rows, width = tokens.shape
    extra = pl.cdiv(3 * experts, 128) * 128
    there = pl.BlockSpec(memory_space=pltpu.HBM)
    return pl.pallas_call(
        functools.partial(pack_kernel, experts),
        out_shape=pltpu.VMEM((rows, width + extra), BF16),
        in_specs=[there] * 3,
        out_specs=pl.BlockSpec(memory_space=pltpu.VMEM),
        scratch_shapes=[
            pltpu.VMEM(routes.shape[::-1], routes.dtype),
            pltpu.VMEM(gates.shape[::-1], gates.dtype),
            pltpu.SemaphoreType.DMA((3,)),
        ],
        compiler_params=pltpu.CompilerParams(vmem_limit_bytes=SCRATCH),
    )(hbm(tokens), hbm(routes.T), hbm(gates.T))


def hbm(a):
    return pltpu.with_memory_space_constraint(a, pltpu.HBM)


def vmem(a):
    return pltpu.with_memory_space_constraint(a, pltpu.VMEM)


def fetches(parts, source, target, sems):
    step = target.shape[2] // parts
    moves = []
    for i in range(parts):
        at = (slice(None), slice(None), slice(i * step, (i + 1) * step))
        moves.append(pltpu.make_async_copy(source.at[at], target.at[at], sems.at[i]))
        moves[-1].start()
    return moves


def load_kernel(parts, source, after, target, sems):
    step = target.shape[1] // parts
    moves = [
        pltpu.make_async_copy(
            source.at[:, i * step : (i + 1) * step], target.at[:, i * step : (i + 1) * step], sems.at[i]
        )
        for i in range(parts)
    ]
    for move in moves:
        move.start()
    for move in moves:
        move.wait()


def load(weight, after):
    parts = 8 if weight.shape[1] % 128 == 0 else 1
    return pl.pallas_call(
        functools.partial(load_kernel, parts),
        out_shape=pltpu.VMEM(weight.shape, weight.dtype),
        in_specs=[pl.BlockSpec(memory_space=pltpu.HBM), pl.BlockSpec(memory_space=pl.ANY)],
        out_specs=pl.BlockSpec(memory_space=pltpu.VMEM),
        scratch_shapes=[pltpu.SemaphoreType.DMA((parts,))],
        compiler_params=pltpu.CompilerParams(vmem_limit_bytes=SCRATCH),
        cost_estimate=pl.CostEstimate(flops=0, bytes_accessed=2 * weight.size, transcendentals=0),
    )(hbm(weight), after)


def gather_rows(blocks, x_ref):
    rows, width = blocks[0].shape[0], x_ref.shape[1]
    for at, ref in enumerate(blocks):
        x_ref[at * rows : (at + 1) * rows, :] = ref[:, :width]


def gather_weights(experts, blocks, width, w_ref):
    me = lax.axis_index("node")
    rows = blocks[0].shape[0]
    for at, ref in enumerate(blocks):
        table = ref[:, width:].astype(F32)
        lane = lax.broadcasted_iota(jnp.int32, table.shape, 1)
        own = lax.rem(lane, experts) == me
        w_ref[at * rows : (at + 1) * rows, :] = jnp.sum(jnp.where(own, table, 0.0), axis=1, keepdims=True)


def first_half(x_ref, gate_ref, up_ref, h_ref, tile, begin, end):
    for j in range(begin // tile, end // tile):
        at = slice(j * tile, (j + 1) * tile)
        gate = jnp.dot(x_ref[...], gate_ref[0, :, at], preferred_element_type=F32)
        upper = jnp.dot(x_ref[...], up_ref[0, :, at], preferred_element_type=F32)
        h_ref[:, at] = (gate / (1.0 + jnp.exp(-gate)) * upper).astype(BF16)


def second_half(h_ref, down_ref, w_ref, out_refs, tile, begin, end):
    for j in range(begin // tile, end // tile):
        at = slice(j * tile, (j + 1) * tile)
        out = jnp.dot(h_ref[...], down_ref[0, :, at], preferred_element_type=F32) * w_ref[...]
        row = 0
        for ref in out_refs:
            ref[:, at] = out[row : row + ref.shape[0]].astype(ref.dtype)
            row += ref.shape[0]


def tiles(width, ff):
    return (256 if ff % 256 == 0 else ff), next(t for t in (512, 256, 128, width) if width % t == 0)


def hidden_kernel(count, tile, parts, *refs):
    blocks, (gate_ref, source, h_ref, *rest) = refs[:count], refs[count:]
    if parts:
        up_ref, x_ref, sems = rest
        moves = fetches(parts, source, up_ref, sems)
    else:
        up_ref, (x_ref,), moves = source, rest, []
    gather_rows(blocks, x_ref)
    ff = h_ref.shape[1]
    for i in range(max(parts, 1)):
        if parts:
            moves[i].wait()
        first_half(x_ref, gate_ref, up_ref, h_ref, tile, i * ff // max(parts, 1), (i + 1) * ff // max(parts, 1))


def hidden(blocks, w_gate, w_up, fetch):
    count, rows = len(blocks), blocks[0].shape[0]
    _, width, ff = w_gate.shape
    tile, _ = tiles(width, ff)
    parts = (2 if ff % (2 * tile) == 0 else 1) if fetch else 0
    here = pl.BlockSpec(memory_space=pltpu.VMEM)
    return pl.pallas_call(
        functools.partial(hidden_kernel, count, tile, parts),
        out_shape=[pltpu.VMEM((count * rows, ff), BF16)] + [pltpu.VMEM(w_up.shape, BF16)] * fetch,
        in_specs=[here] * (count + 1) + [pl.BlockSpec(memory_space=pltpu.HBM if fetch else pltpu.VMEM)],
        out_specs=[here] * (1 + fetch),
        scratch_shapes=[pltpu.VMEM((count * rows, width), BF16)] + [pltpu.SemaphoreType.DMA((parts,))] * fetch,
        compiler_params=pltpu.CompilerParams(vmem_limit_bytes=SCRATCH),
        cost_estimate=pl.CostEstimate(
            flops=4 * max(count * rows, 256) * width * ff, bytes_accessed=0, transcendentals=count * rows * ff
        ),
    )(*blocks, vmem(w_gate), hbm(w_up) if fetch else vmem(w_up))


def output_kernel(count, experts, tile, parts, *refs):
    blocks, (h_ref, source, mine_ref, other_ref, *rest) = refs[:count], refs[count:]
    if parts:
        down_ref, w_ref, sems = rest
        moves = fetches(parts, source, down_ref, sems)
    else:
        down_ref, (w_ref,), moves = source, rest, []
    width = mine_ref.shape[1]
    gather_weights(experts, blocks, width, w_ref)
    for i in range(max(parts, 1)):
        if parts:
            moves[i].wait()
        begin, end = i * width // max(parts, 1), (i + 1) * width // max(parts, 1)
        second_half(h_ref, down_ref, w_ref, [mine_ref, other_ref], tile, begin, end)


def output(blocks, mine, experts, h, w_down, fetch):
    count, rows = len(blocks), blocks[0].shape[0]
    _, ff, width = w_down.shape
    _, tile = tiles(width, ff)
    parts = width // tile if fetch else 0
    here = pl.BlockSpec(memory_space=pltpu.VMEM)
    return pl.pallas_call(
        functools.partial(output_kernel, count, experts, tile, parts),
        out_shape=[pltpu.VMEM((mine * rows, width), F32), pltpu.VMEM(((count - mine) * rows, width), BF16)]
        + [pltpu.VMEM(w_down.shape, BF16)] * fetch,
        in_specs=[here] * (count + 1)
        + [pl.BlockSpec(memory_space=pltpu.HBM if fetch else pltpu.VMEM)],
        out_specs=[here] * (2 + fetch),
        scratch_shapes=[pltpu.VMEM((count * rows, 1), F32)] + [pltpu.SemaphoreType.DMA((parts,))] * fetch,
        compiler_params=pltpu.CompilerParams(vmem_limit_bytes=SCRATCH),
        cost_estimate=pl.CostEstimate(
            flops=2 * max(count * rows, 256) * width * ff, bytes_accessed=0, transcendentals=0
        ),
    )(*blocks, h, hbm(w_down) if fetch else vmem(w_down))


def expert_kernel(count, experts, tile_ff, tile_d, *refs):
    blocks, (gate_ref, up_ref, down_ref, mine_ref, first_ref, other_ref, x_ref, w_ref, h_ref) = refs[:count], refs[count:]
    gather_rows(blocks, x_ref)
    gather_weights(experts, blocks, x_ref.shape[1], w_ref)
    first_half(x_ref, gate_ref, up_ref, h_ref, tile_ff, 0, h_ref.shape[1])
    second_half(h_ref, down_ref, w_ref, [mine_ref, first_ref, other_ref], tile_d, 0, x_ref.shape[1])


def expert(blocks, mine, experts, w_gate, w_up, w_down):
    count, rows = len(blocks), blocks[0].shape[0]
    _, width, ff = w_gate.shape
    total = count * rows
    here = pl.BlockSpec(memory_space=pltpu.VMEM)
    return pl.pallas_call(
        functools.partial(expert_kernel, count, experts, *tiles(width, ff)),
        out_shape=[
            pltpu.VMEM((mine * rows, width), F32),
            pltpu.VMEM((rows, width), BF16),
            pltpu.VMEM((total - (mine + 1) * rows, width), BF16),
        ],
        in_specs=[here] * (count + 3),
        out_specs=[here] * 3,
        scratch_shapes=[pltpu.VMEM((total, width), BF16), pltpu.VMEM((total, 1), F32), pltpu.VMEM((total, ff), BF16)],
        compiler_params=pltpu.CompilerParams(vmem_limit_bytes=SCRATCH),
        cost_estimate=pl.CostEstimate(
            flops=6 * max(total, 256) * width * ff, bytes_accessed=0, transcendentals=total * ff
        ),
    )(*blocks, vmem(w_gate), vmem(w_up), vmem(w_down))


def local(cores, order, tokens, routes, gates, w_gate, w_up, w_down):
    chips = len(order)
    experts = chips * cores
    rows, width = tokens.shape
    forth = [(order[i] * cores + c, order[(i + 1) % chips] * cores + c) for i in range(chips) for c in range(cores)]
    back = [(b, a) for a, b in forth]
    swap = [(chip * cores + c, chip * cores + 1 - c) for chip in range(chips) for c in range(cores)]
    right = lambda a: lax.ppermute(a, "node", forth)
    left = lambda a: lax.ppermute(a, "node", back)
    sibling = lambda a: lax.ppermute(a, "node", swap)
    together = lax.optimization_barrier

    far, cut = chips // 2, rows // 2
    own = pack(tokens, routes, gates, experts)
    got, twin = {0: own}, {}
    middle = [s * d for d in range(2, far - 1) for s in (1, -1)]
    late = [far, far - 1, 1 - far]
    exchanged = {}
    for d in range(1, far):
        a, b = left(got[d - 1]), right(got[1 - d])
        if d == 1:
            done = (load(w_gate, own),)
        elif d == 2:
            near = [got[0], got[1], got[-1], twin[0]]
            done = hidden(near, w_gate, w_up, True)
        elif d == 3:
            done = output(near, 3, experts, h_near, w_down, True)
        else:
            done = None
        ready, done = together(({e: got[e] for e in {d - 1, 1 - d}}, done))
        started = {e: sibling(ready[e]) for e in ready}
        if d == 1:
            a, b, (w_gate,), started = together((a, b, done, started))
            twin.update(started)
            started = {}
        else:
            a, b, done, exchanged = together((a, b, done, exchanged))
        if d == 2:
            h_near, w_up = done
        if d == 3:
            *near_out, w_down = done
        twin.update(exchanged)
        exchanged = started
        got[d], got[-d] = a, b
    ends = right(got[1 - far][:cut]), left(got[far - 1][cut:])
    exchanged = together(exchanged)
    twin.update(exchanged)
    rest = [got[d] for d in middle] + [twin[1], twin[-1]] + [twin[d] for d in middle]
    (h_rest,) = hidden(rest, w_gate, w_up, False)
    ready, h_rest = together(({e: got[e] for e in (far - 1, 1 - far)}, h_rest))
    exchanged = {e: sibling(ready[e]) for e in ready}
    ends, h_rest = together((ends, h_rest))
    got[far] = jnp.concatenate(ends, axis=0)
    rest_out, twin[far], exchanged, near_sent = together(
        (
            output(rest, len(middle), experts, h_rest, w_down, False),
            sibling(got[far]),
            exchanged,
            sibling(near_out[1]),
        )
    )
    twin.update(exchanged)
    late_out = expert([got[d] for d in late] + [twin[d] for d in late], len(late), experts, w_gate, w_up, w_down)

    block = lambda a, j: a[j * rows : (j + 1) * rows]
    mine, theirs = {}, {0: near_sent}
    for j, d in enumerate((0, 1, -1)):
        mine[d] = block(near_out[0], j)
    mine[far], theirs[far] = block(late_out[0], 0), sibling(late_out[1])
    end = (mine[far] + theirs[far].astype(F32)).astype(BF16)
    late_sent, rest_sent, _ = together((sibling(late_out[2]), sibling(rest_out[1]), end))
    for j, d in enumerate(middle):
        mine[d] = block(rest_out[0], j)
    for j, d in enumerate([1, -1] + middle):
        theirs[d] = block(rest_sent, j)
    for j, d in enumerate(late[1:]):
        mine[d], theirs[d] = block(late_out[0], j + 1), block(late_sent, j)

    both = lambda d: mine[d] + theirs[d].astype(F32)
    a, b = right(end[:cut]), left(end[cut:])
    for d in range(far - 1, 0, -1):
        up = both(d)
        up = jnp.concatenate([up[:cut] + a.astype(F32), up[cut:]], axis=0) if d == far - 1 else up + a.astype(F32)
        up = up.astype(BF16)
        b, _ = together((b, up))
        down = both(-d)
        down = jnp.concatenate([down[:cut], down[cut:] + b.astype(F32)], axis=0) if d == far - 1 else down + b.astype(F32)
        down = down.astype(BF16)
        a, _ = together((right(up), down))
        b = left(down)
    return (both(0) + a.astype(F32) + b.astype(F32)).astype(BF16)


def solution(mesh):
    cores, order = chip_layout(mesh)
    in_specs = (
        P(("groups", "node"), None),
        P(("groups", "node"), None),
        P(("groups", "node"), None),
        P("node", None, None),
        P("node", None, None),
        P("node", None, None),
    )
    out_specs = P(("groups", "node"), None)
    body = functools.partial(local, cores, order)
    return jax.shard_map(body, mesh=mesh, in_specs=in_specs, out_specs=out_specs, check_vma=False)
```

```python
import functools

import jax
import jax.numpy as jnp
from jax import lax
from jax.experimental import pallas as pl
from jax.experimental.pallas import tpu as pltpu
from jax.sharding import PartitionSpec as P

F32, BF16 = jnp.float32, jnp.bfloat16
SCRATCH = 16 * 2**20


def chip_layout(mesh):
    names = list(mesh.axis_names)
    count = mesh.shape["node"]
    row = mesh.devices.transpose([names.index(n) for n in names if n != "node"] + [names.index("node")])
    row = list(row.reshape(-1, count)[0])
    where = [tuple(getattr(d, "coords", None) or (i // 2,)) for i, d in enumerate(row)]
    cores = 2 if count % 2 == 0 and all(where[i] == where[i + 1] for i in range(0, count, 2)) else 1
    chips = where[::cores]
    order = list(range(len(chips)))
    axes = [a for a in range(len(chips[0])) if len({c[a] for c in chips}) > 1]
    if len(axes) == 2:
        short, long = sorted(axes, key=lambda a: len({c[a] for c in chips}))
        low = min(c[short] for c in chips)
        if len({c[short] for c in chips}) == 2:
            order.sort(key=lambda i: (chips[i][short], chips[i][long] if chips[i][short] == low else -chips[i][long]))
    return cores, order


def pack_kernel(experts, tok_hbm, routes_hbm, gates_hbm, out_ref, routes_ref, gates_ref, sems):
    rows, width = tok_hbm.shape
    extra = out_ref.shape[1] - width
    moves = [
        pltpu.make_async_copy(routes_hbm, routes_ref, sems.at[0]),
        pltpu.make_async_copy(gates_hbm, gates_ref, sems.at[1]),
        pltpu.make_async_copy(tok_hbm, out_ref.at[:, :width], sems.at[2]),
    ]
    for move in moves:
        move.start()
    for move in moves[:2]:
        move.wait()
    lane = lax.broadcasted_iota(jnp.int32, (extra, rows), 0)
    expert, piece = lax.rem(lane, experts), lax.div(lane, experts)
    weight = jnp.zeros((extra, rows), F32)
    for k in range(routes_ref.shape[0]):
        weight += jnp.where(routes_ref[k : k + 1] == expert, gates_ref[k : k + 1], 0.0)
    high = weight.astype(BF16).astype(F32)
    middle = (weight - high).astype(BF16).astype(F32)
    low = weight - high - middle
    table = jnp.where(piece == 0, high, jnp.where(piece == 1, middle, jnp.where(piece == 2, low, 0.0)))
    out_ref[:, width:] = table.T.astype(BF16)
    moves[2].wait()


def pack(tokens, routes, gates, experts):
    rows, width = tokens.shape
    extra = pl.cdiv(3 * experts, 128) * 128
    there = pl.BlockSpec(memory_space=pltpu.HBM)
    return pl.pallas_call(
        functools.partial(pack_kernel, experts),
        out_shape=pltpu.VMEM((rows, width + extra), BF16),
        in_specs=[there] * 3,
        out_specs=pl.BlockSpec(memory_space=pltpu.VMEM),
        scratch_shapes=[
            pltpu.VMEM(routes.shape[::-1], routes.dtype),
            pltpu.VMEM(gates.shape[::-1], gates.dtype),
            pltpu.SemaphoreType.DMA((3,)),
        ],
        compiler_params=pltpu.CompilerParams(vmem_limit_bytes=SCRATCH),
        cost_estimate=pl.CostEstimate(flops=10 * 2**30, bytes_accessed=0, transcendentals=0),
    )(hbm(tokens), hbm(routes.T), hbm(gates.T))


def hbm(a):
    return pltpu.with_memory_space_constraint(a, pltpu.HBM)


def gather_rows(blocks, x_ref):
    rows, width = blocks[0].shape[0], x_ref.shape[1]
    for at, ref in enumerate(blocks):
        x_ref[at * rows : (at + 1) * rows, :] = ref[:, :width]


def gather_weights(experts, blocks, width, w_ref):
    me = lax.axis_index("node")
    rows = blocks[0].shape[0]
    for at, ref in enumerate(blocks):
        table = ref[:, width:].astype(F32)
        lane = lax.broadcasted_iota(jnp.int32, table.shape, 1)
        own = lax.rem(lane, experts) == me
        w_ref[at * rows : (at + 1) * rows, :] = jnp.sum(jnp.where(own, table, 0.0), axis=1, keepdims=True)


def first_half(x_ref, gate_ref, up_ref, h_ref, tile, begin, end):
    for j in range(begin // tile, end // tile):
        at = slice(j * tile, (j + 1) * tile)
        gate = jnp.dot(x_ref[...], gate_ref[0, :, at], preferred_element_type=F32)
        upper = jnp.dot(x_ref[...], up_ref[0, :, at], preferred_element_type=F32)
        h_ref[:, at] = (gate / (1.0 + jnp.exp(-gate)) * upper).astype(BF16)


def second_half(h_ref, down_ref, w_ref, out_refs, tile, begin, end):
    for j in range(begin // tile, end // tile):
        at = slice(j * tile, (j + 1) * tile)
        out = jnp.dot(h_ref[...], down_ref[0, :, at], preferred_element_type=F32) * w_ref[...]
        row = 0
        for ref in out_refs:
            ref[:, at] = out[row : row + ref.shape[0]].astype(ref.dtype)
            row += ref.shape[0]


def tiles(width, ff):
    return (256 if ff % 256 == 0 else ff), next(t for t in (512, 256, 128, width) if width % t == 0)


def hidden_kernel(count, tile, *refs):
    blocks, (gate_ref, up_ref, h_ref, x_ref) = refs[:count], refs[count:]
    gather_rows(blocks, x_ref)
    first_half(x_ref, gate_ref, up_ref, h_ref, tile, 0, h_ref.shape[1])


def hidden(blocks, w_gate, w_up):
    count, rows = len(blocks), blocks[0].shape[0]
    _, width, ff = w_gate.shape
    here = pl.BlockSpec(memory_space=pltpu.VMEM)
    return pl.pallas_call(
        functools.partial(hidden_kernel, count, tiles(width, ff)[0]),
        out_shape=pltpu.VMEM((count * rows, ff), BF16),
        in_specs=[here] * (count + 2),
        out_specs=here,
        scratch_shapes=[pltpu.VMEM((count * rows, width), BF16)],
        compiler_params=pltpu.CompilerParams(vmem_limit_bytes=SCRATCH),
        cost_estimate=pl.CostEstimate(
            flops=4 * max(count * rows, 256) * width * ff, bytes_accessed=0, transcendentals=count * rows * ff
        ),
    )(*blocks, w_gate, w_up)


def output_kernel(count, experts, tile, *refs):
    blocks, (h_ref, down_ref, mine_ref, other_ref, w_ref) = refs[:count], refs[count:]
    width = mine_ref.shape[1]
    gather_weights(experts, blocks, width, w_ref)
    second_half(h_ref, down_ref, w_ref, [mine_ref, other_ref], tile, 0, width)


def output(blocks, mine, experts, h, w_down):
    count, rows = len(blocks), blocks[0].shape[0]
    _, ff, width = w_down.shape
    here = pl.BlockSpec(memory_space=pltpu.VMEM)
    return pl.pallas_call(
        functools.partial(output_kernel, count, experts, tiles(width, ff)[1]),
        out_shape=[pltpu.VMEM((mine * rows, width), F32), pltpu.VMEM(((count - mine) * rows, width), BF16)],
        in_specs=[here] * (count + 2),
        out_specs=[here] * 2,
        scratch_shapes=[pltpu.VMEM((count * rows, 1), F32)],
        compiler_params=pltpu.CompilerParams(vmem_limit_bytes=SCRATCH),
        cost_estimate=pl.CostEstimate(
            flops=2 * max(count * rows, 256) * width * ff, bytes_accessed=0, transcendentals=0
        ),
    )(*blocks, h, w_down)


def expert_kernel(count, experts, tile_ff, tile_d, *refs):
    blocks, (gate_ref, up_ref, down_ref, mine_ref, first_ref, other_ref, x_ref, w_ref, h_ref) = refs[:count], refs[count:]
    gather_rows(blocks, x_ref)
    gather_weights(experts, blocks, x_ref.shape[1], w_ref)
    first_half(x_ref, gate_ref, up_ref, h_ref, tile_ff, 0, h_ref.shape[1])
    second_half(h_ref, down_ref, w_ref, [mine_ref, first_ref, other_ref], tile_d, 0, x_ref.shape[1])


def expert(blocks, mine, experts, w_gate, w_up, w_down):
    count, rows = len(blocks), blocks[0].shape[0]
    _, width, ff = w_gate.shape
    total = count * rows
    here = pl.BlockSpec(memory_space=pltpu.VMEM)
    return pl.pallas_call(
        functools.partial(expert_kernel, count, experts, *tiles(width, ff)),
        out_shape=[
            pltpu.VMEM((mine * rows, width), F32),
            pltpu.VMEM((rows, width), BF16),
            pltpu.VMEM((total - (mine + 1) * rows, width), BF16),
        ],
        in_specs=[here] * (count + 3),
        out_specs=[here] * 3,
        scratch_shapes=[pltpu.VMEM((total, width), BF16), pltpu.VMEM((total, 1), F32), pltpu.VMEM((total, ff), BF16)],
        compiler_params=pltpu.CompilerParams(vmem_limit_bytes=SCRATCH),
        cost_estimate=pl.CostEstimate(
            flops=6 * max(total, 256) * width * ff, bytes_accessed=0, transcendentals=total * ff
        ),
    )(*blocks, w_gate, w_up, w_down)


def local(cores, order, tokens, routes, gates, w_gate, w_up, w_down):
    chips = len(order)
    experts = chips * cores
    rows, width = tokens.shape
    forth = [(order[i] * cores + c, order[(i + 1) % chips] * cores + c) for i in range(chips) for c in range(cores)]
    back = [(b, a) for a, b in forth]
    swap = [(chip * cores + c, chip * cores + 1 - c) for chip in range(chips) for c in range(cores)]
    right = lambda a: lax.ppermute(a, "node", forth)
    left = lambda a: lax.ppermute(a, "node", back)
    sibling = lambda a: lax.ppermute(a, "node", swap)
    together = lax.optimization_barrier

    far, cut = chips // 2, rows // 2
    own = pack(tokens, routes, gates, experts)
    got, twin = {0: own}, {}
    middle = [s * d for d in range(2, far - 1) for s in (1, -1)]
    late = [far, far - 1, 1 - far]
    exchanged = {}
    for d in range(1, far):
        a, b = left(got[d - 1]), right(got[1 - d])
        if d == 1:
            done = None
        elif d == 2:
            near = [got[0], got[1], got[-1], twin[0]]
            done = hidden(near, w_gate, w_up)
        elif d == 3:
            done = output(near, 3, experts, h_near, w_down)
        else:
            done = None
        ready, done = together(({e: got[e] for e in {d - 1, 1 - d}}, done))
        started = {e: sibling(ready[e]) for e in ready}
        if d == 1:
            a, b, started = together((a, b, started))
            twin.update(started)
            started = {}
        else:
            a, b, done, exchanged = together((a, b, done, exchanged))
        if d == 2:
            h_near = done
        if d == 3:
            near_out = done
        twin.update(exchanged)
        exchanged = started
        got[d], got[-d] = a, b
    ends = right(got[1 - far][:cut]), left(got[far - 1][cut:])
    exchanged = together(exchanged)
    twin.update(exchanged)
    rest = [got[d] for d in middle] + [twin[1], twin[-1]] + [twin[d] for d in middle]
    h_rest = hidden(rest, w_gate, w_up)
    ready, h_rest = together(({e: got[e] for e in (far - 1, 1 - far)}, h_rest))
    exchanged = {e: sibling(ready[e]) for e in ready}
    ends, h_rest = together((ends, h_rest))
    got[far] = jnp.concatenate(ends, axis=0)
    rest_out, twin[far], exchanged, near_sent = together(
        (
            output(rest, len(middle), experts, h_rest, w_down),
            sibling(got[far]),
            exchanged,
            sibling(near_out[1]),
        )
    )
    twin.update(exchanged)
    late_out = expert([got[d] for d in late] + [twin[d] for d in late], len(late), experts, w_gate, w_up, w_down)

    block = lambda a, j: a[j * rows : (j + 1) * rows]
    mine, theirs = {}, {0: near_sent}
    for j, d in enumerate((0, 1, -1)):
        mine[d] = block(near_out[0], j)
    mine[far], theirs[far] = block(late_out[0], 0), sibling(late_out[1])
    end = (mine[far] + theirs[far].astype(F32)).astype(BF16)
    late_sent, rest_sent, _ = together((sibling(late_out[2]), sibling(rest_out[1]), end))
    for j, d in enumerate(middle):
        mine[d] = block(rest_out[0], j)
    for j, d in enumerate([1, -1] + middle):
        theirs[d] = block(rest_sent, j)
    for j, d in enumerate(late[1:]):
        mine[d], theirs[d] = block(late_out[0], j + 1), block(late_sent, j)

    split = width // 256 * 128
    spans = [slice(0, split), slice(split, width)] if split else [slice(0, width)]
    both = lambda d, s: mine[d][:, s] + theirs[d][:, s].astype(F32)
    flow = [(right(end[:cut, s]), left(end[cut:, s])) for s in spans]
    last = end
    for d in range(far - 1, 0, -1):
        for i, s in enumerate(spans):
            up, down = both(d, s), both(-d, s)
            a, _ = together((flow[i][0], last))
            up = jnp.concatenate([up[:cut] + a.astype(F32), up[cut:]], axis=0) if d == far - 1 else up + a.astype(F32)
            up = up.astype(BF16)
            b, _ = together((flow[i][1], up))
            down = jnp.concatenate([down[:cut], down[cut:] + b.astype(F32)], axis=0) if d == far - 1 else down + b.astype(F32)
            last = down.astype(BF16)
            flow[i] = right(up), left(last)
    out = []
    for (a, b), s in zip(flow, spans):
        a, _ = together((a, last))
        total = both(0, s) + a.astype(F32)
        b, total = together((b, total))
        last = (total + b.astype(F32)).astype(BF16)
        out.append(last)
    return jnp.concatenate(out, axis=1)


def solution(mesh):
    cores, order = chip_layout(mesh)
    in_specs = (
        P(("groups", "node"), None),
        P(("groups", "node"), None),
        P(("groups", "node"), None),
        P("node", None, None),
        P("node", None, None),
        P("node", None, None),
    )
    out_specs = P(("groups", "node"), None)
    body = functools.partial(local, cores, order)
    return jax.shard_map(body, mesh=mesh, in_specs=in_specs, out_specs=out_specs, check_vma=False)
```

```python
import functools

import jax
import jax.numpy as jnp
from jax import lax
from jax.experimental import pallas as pl
from jax.experimental.pallas import tpu as pltpu
from jax.sharding import PartitionSpec as P

F32, BF16 = jnp.float32, jnp.bfloat16
SCRATCH = 20 * 2**20
GROUP = 8


def chip_order(mesh):
    names = list(mesh.axis_names)
    count = mesh.shape["node"]
    row = mesh.devices.transpose([names.index(n) for n in names if n != "node"] + [names.index("node")])
    row = list(row.reshape(-1, count)[0])
    chips = [tuple(getattr(d, "coords", None) or (i // 2,)) for i, d in enumerate(row)][::2]
    order = list(range(len(chips)))
    axes = [a for a in range(len(chips[0])) if len({c[a] for c in chips}) > 1]
    if len(axes) == 2:
        short, long = sorted(axes, key=lambda a: len({c[a] for c in chips}))
        low = min(c[short] for c in chips)
        if len({c[short] for c in chips}) == 2:
            order.sort(key=lambda i: (chips[i][short], chips[i][long] if chips[i][short] == low else -chips[i][long]))
    return order


def pack_kernel(experts, tok_hbm, routes_hbm, gates_hbm, out_ref, routes_ref, gates_ref, sems):
    rows, width = tok_hbm.shape
    extra = out_ref.shape[1] - width
    moves = [
        pltpu.make_async_copy(routes_hbm, routes_ref, sems.at[0]),
        pltpu.make_async_copy(gates_hbm, gates_ref, sems.at[1]),
        pltpu.make_async_copy(tok_hbm, out_ref.at[:, :width], sems.at[2]),
    ]
    for move in moves:
        move.start()
    for move in moves[:2]:
        move.wait()
    lane = lax.broadcasted_iota(jnp.int32, (extra, rows), 0)
    expert, piece = lax.rem(lane, experts), lax.div(lane, experts)
    weight = jnp.zeros((extra, rows), F32)
    for k in range(routes_ref.shape[0]):
        weight += jnp.where(routes_ref[k : k + 1] == expert, gates_ref[k : k + 1], 0.0)
    high = weight.astype(BF16).astype(F32)
    middle = (weight - high).astype(BF16).astype(F32)
    low = weight - high - middle
    table = jnp.where(piece == 0, high, jnp.where(piece == 1, middle, jnp.where(piece == 2, low, 0.0)))
    out_ref[:, width:] = table.T.astype(BF16)
    moves[2].wait()


def pack(tokens, routes, gates, experts):
    rows, width = tokens.shape
    extra = pl.cdiv(3 * experts, 128) * 128
    there = pl.BlockSpec(memory_space=pltpu.HBM)
    return pl.pallas_call(
        functools.partial(pack_kernel, experts),
        out_shape=pltpu.VMEM((rows, width + extra), BF16),
        in_specs=[there] * 3,
        out_specs=pl.BlockSpec(memory_space=pltpu.VMEM),
        scratch_shapes=[
            pltpu.VMEM(routes.shape[::-1], routes.dtype),
            pltpu.VMEM(gates.shape[::-1], gates.dtype),
            pltpu.SemaphoreType.DMA((3,)),
        ],
        compiler_params=pltpu.CompilerParams(vmem_limit_bytes=SCRATCH),
        cost_estimate=pl.CostEstimate(flops=10 * 2**30, bytes_accessed=0, transcendentals=0),
    )(hbm(tokens), hbm(routes.T), hbm(gates.T))


def hbm(a):
    return pltpu.with_memory_space_constraint(a, pltpu.HBM)


def gather_rows(blocks, x_ref):
    rows, width = blocks[0].shape[0], x_ref.shape[1]
    for at, ref in enumerate(blocks):
        x_ref[at * rows : (at + 1) * rows, :] = ref[:, :width]


def gather_weights(experts, blocks, width, w_ref):
    me = lax.axis_index("node")
    rows = blocks[0].shape[0]
    for at, ref in enumerate(blocks):
        table = ref[:, width:].astype(F32)
        lane = lax.broadcasted_iota(jnp.int32, table.shape, 1)
        own = lax.rem(lane, experts) == me
        w_ref[at * rows : (at + 1) * rows, :] = jnp.sum(jnp.where(own, table, 0.0), axis=1, keepdims=True)


def first_half(x_ref, gate_ref, up_ref, h_ref, tile, begin, end):
    for j in range(begin // tile, end // tile):
        at = slice(j * tile, (j + 1) * tile)
        gate = jnp.dot(x_ref[...], gate_ref[0, :, at], preferred_element_type=F32)
        upper = jnp.dot(x_ref[...], up_ref[0, :, at], preferred_element_type=F32)
        h_ref[:, at] = (gate / (1.0 + jnp.exp(-gate)) * upper).astype(BF16)


def second_half(h_ref, down_ref, w_ref, out_refs, tile, begin, end):
    for j in range(begin // tile, end // tile):
        at = slice(j * tile, (j + 1) * tile)
        out = jnp.dot(h_ref[...], down_ref[0, :, at], preferred_element_type=F32) * w_ref[...]
        row = 0
        for ref in out_refs:
            ref[:, at] = out[row : row + ref.shape[0]].astype(ref.dtype)
            row += ref.shape[0]


def tiles(width, ff):
    return (256 if ff % 256 == 0 else ff), next(t for t in (512, 256, 128, width) if width % t == 0)


def expert_kernel(count, experts, tile_ff, tile_d, *refs):
    blocks, (gate_ref, up_ref, down_ref, *out_refs) = refs[:count], refs[count:]
    out_refs, (x_ref, w_ref, h_ref) = out_refs[:-3], out_refs[-3:]
    gather_rows(blocks, x_ref)
    gather_weights(experts, blocks, x_ref.shape[1], w_ref)
    first_half(x_ref, gate_ref, up_ref, h_ref, tile_ff, 0, h_ref.shape[1])
    second_half(h_ref, down_ref, w_ref, out_refs, tile_d, 0, x_ref.shape[1])


def expert(blocks, pieces, experts, w_gate, w_up, w_down):
    count, rows = len(blocks), blocks[0].shape[0]
    _, width, ff = w_gate.shape
    total = count * rows
    here = pl.BlockSpec(memory_space=pltpu.VMEM)
    return pl.pallas_call(
        functools.partial(expert_kernel, count, experts, *tiles(width, ff)),
        out_shape=[pltpu.VMEM((n * rows, width), kind) for n, kind in pieces],
        in_specs=[here] * (count + 3),
        out_specs=[here] * len(pieces),
        scratch_shapes=[pltpu.VMEM((total, width), BF16), pltpu.VMEM((total, 1), F32), pltpu.VMEM((total, ff), BF16)],
        compiler_params=pltpu.CompilerParams(vmem_limit_bytes=SCRATCH),
        cost_estimate=pl.CostEstimate(
            flops=6 * max(total, 256) * width * ff, bytes_accessed=0, transcendentals=total * ff
        ),
    )(*blocks, w_gate, w_up, w_down)


def local(order, tokens, routes, gates, w_gate, w_up, w_down):
    chips = len(order)
    experts = 2 * chips
    rows, width = tokens.shape
    forth = [(2 * order[i], 2 * order[(i + 1) % chips]) for i in range(chips)]
    spin = forth + [(b + 1, a + 1) for a, b in forth]
    swap = [(i, i ^ 1) for i in range(experts)]
    send = lambda a: lax.ppermute(a, "node", spin)
    sibling = lambda a: lax.ppermute(a, "node", swap)
    together = lax.optimization_barrier
    block = lambda a, j: a[j * rows : (j + 1) * rows]

    far = chips // 2
    own = pack(tokens, routes, gates, experts)
    up, up_twin, down, down_twin = {0: own}, {0: sibling(own)}, {}, {}
    for k in range(1, far):
        up[k] = send(up[k - 1])
        up_twin[k] = send(up_twin[k - 1])
        down_twin[k], down[k] = sibling(up[k]), sibling(up_twin[k])
    up[far] = send(up[far - 1])
    far_twin = sibling(up[far])

    kept, given = [up[far]], [far_twin]
    for k in range(far - 1, 0, -1):
        kept += [down_twin[k], down[k]]
        given += [up[k], up_twin[k]]
    kept, given = kept + [own], given + [up_twin[0]]
    mine, theirs = [], []
    for at in range(0, len(kept), GROUP):
        some = slice(at, at + GROUP)
        n = len(kept[some])
        sizes = [m for m in (min(n, 2), min(n - 2, 2), n - 4) if m > 0]
        out = expert(kept[some] + given[some], [(n, F32)] + [(m, BF16) for m in sizes], experts, w_gate, w_up, w_down)
        mine += [block(out[0], j) for j in range(n)]
        for m, piece in zip(sizes, out[1:]):
            piece = sibling(piece)
            theirs += [(piece, j) for j in range(m)]

    def add(j, *arrived):
        nonlocal last
        piece, at = theirs[j]
        (piece, *arrived), _ = together(((piece, *arrived), last))
        total = mine[j] + block(piece, at).astype(F32)
        for a in arrived:
            total = total + a.astype(F32)
        last = total.astype(BF16)
        return last

    last = mine[0]
    sums = send(add(0))
    sums_twin = []
    for j in range(1, len(mine) - 1, 2):
        sums_twin = [send(add(j, *sums_twin))]
        sums = send(add(j + 1, sums))
    end = len(mine) - 1
    piece, sums = together((theirs[end][0], sums))
    total = mine[end] + block(piece, theirs[end][1]).astype(F32) + sums.astype(F32)
    for a in sums_twin:
        a, total = together((sibling(a), total))
        total = total + a.astype(F32)
    return total.astype(BF16)


def solution(mesh):
    order = chip_order(mesh)
    in_specs = (
        P(("groups", "node"), None),
        P(("groups", "node"), None),
        P(("groups", "node"), None),
        P("node", None, None),
        P("node", None, None),
        P("node", None, None),
    )
    out_specs = P(("groups", "node"), None)
    body = functools.partial(local, order)
    return jax.shard_map(body, mesh=mesh, in_specs=in_specs, out_specs=out_specs, check_vma=False)
```

```python
import functools

import jax
import jax.numpy as jnp
from jax import lax
from jax.experimental import pallas as pl
from jax.experimental.pallas import tpu as pltpu
from jax.sharding import PartitionSpec as P

F32, BF16 = jnp.float32, jnp.bfloat16
SCRATCH = 16 * 2**20


def chip_order(mesh):
    names = list(mesh.axis_names)
    count = mesh.shape["node"]
    row = mesh.devices.transpose([names.index(n) for n in names if n != "node"] + [names.index("node")])
    row = list(row.reshape(-1, count)[0])
    chips = [tuple(getattr(d, "coords", None) or (i // 2,)) for i, d in enumerate(row)][::2]
    order = list(range(len(chips)))
    axes = [a for a in range(len(chips[0])) if len({c[a] for c in chips}) > 1]
    if len(axes) == 2:
        short, long = sorted(axes, key=lambda a: len({c[a] for c in chips}))
        low = min(c[short] for c in chips)
        if len({c[short] for c in chips}) == 2:
            order.sort(key=lambda i: (chips[i][short], chips[i][long] if chips[i][short] == low else -chips[i][long]))
    return order


def pack_kernel(experts, tok_hbm, routes_hbm, gates_hbm, out_ref, routes_ref, gates_ref, sems):
    rows, width = tok_hbm.shape
    extra = out_ref.shape[1] - width
    moves = [
        pltpu.make_async_copy(routes_hbm, routes_ref, sems.at[0]),
        pltpu.make_async_copy(gates_hbm, gates_ref, sems.at[1]),
        pltpu.make_async_copy(tok_hbm, out_ref.at[:, :width], sems.at[2]),
    ]
    for move in moves:
        move.start()
    for move in moves[:2]:
        move.wait()
    lane = lax.broadcasted_iota(jnp.int32, (extra, rows), 0)
    expert, piece = lax.rem(lane, experts), lax.div(lane, experts)
    weight = jnp.zeros((extra, rows), F32)
    for k in range(routes_ref.shape[0]):
        weight += jnp.where(routes_ref[k : k + 1] == expert, gates_ref[k : k + 1], 0.0)
    high = weight.astype(BF16).astype(F32)
    middle = (weight - high).astype(BF16).astype(F32)
    low = weight - high - middle
    table = jnp.where(piece == 0, high, jnp.where(piece == 1, middle, jnp.where(piece == 2, low, 0.0)))
    out_ref[:, width:] = table.T.astype(BF16)
    moves[2].wait()


def pack(tokens, routes, gates, experts):
    rows, width = tokens.shape
    extra = pl.cdiv(3 * experts, 128) * 128
    there = pl.BlockSpec(memory_space=pltpu.HBM)
    return pl.pallas_call(
        functools.partial(pack_kernel, experts),
        out_shape=pltpu.VMEM((rows, width + extra), BF16),
        in_specs=[there] * 3,
        out_specs=pl.BlockSpec(memory_space=pltpu.VMEM),
        scratch_shapes=[
            pltpu.VMEM(routes.shape[::-1], routes.dtype),
            pltpu.VMEM(gates.shape[::-1], gates.dtype),
            pltpu.SemaphoreType.DMA((3,)),
        ],
        compiler_params=pltpu.CompilerParams(vmem_limit_bytes=SCRATCH),
        cost_estimate=pl.CostEstimate(flops=10 * 2**30, bytes_accessed=0, transcendentals=0),
    )(hbm(tokens), hbm(routes.T), hbm(gates.T))


def hbm(a):
    return pltpu.with_memory_space_constraint(a, pltpu.HBM)


def gather_rows(blocks, x_ref):
    rows, width = blocks[0].shape[0], x_ref.shape[1]
    for at, ref in enumerate(blocks):
        x_ref[at * rows : (at + 1) * rows, :] = ref[:, :width]


def gather_weights(experts, blocks, width, w_ref):
    me = lax.axis_index("node")
    rows = blocks[0].shape[0]
    for at, ref in enumerate(blocks):
        table = ref[:, width:].astype(F32)
        lane = lax.broadcasted_iota(jnp.int32, table.shape, 1)
        own = lax.rem(lane, experts) == me
        w_ref[at * rows : (at + 1) * rows, :] = jnp.sum(jnp.where(own, table, 0.0), axis=1, keepdims=True)


def first_half(x_ref, gate_ref, up_ref, h_ref, tile, begin, end):
    for j in range(begin // tile, end // tile):
        at = slice(j * tile, (j + 1) * tile)
        gate = jnp.dot(x_ref[...], gate_ref[0, :, at], preferred_element_type=F32)
        upper = jnp.dot(x_ref[...], up_ref[0, :, at], preferred_element_type=F32)
        h_ref[:, at] = (gate / (1.0 + jnp.exp(-gate)) * upper).astype(BF16)


def second_half(h_ref, down_ref, w_ref, out_refs, tile, begin, end):
    for j in range(begin // tile, end // tile):
        at = slice(j * tile, (j + 1) * tile)
        out = jnp.dot(h_ref[...], down_ref[0, :, at], preferred_element_type=F32) * w_ref[...]
        row = 0
        for ref in out_refs:
            ref[:, at] = out[row : row + ref.shape[0]].astype(ref.dtype)
            row += ref.shape[0]


def tiles(width, ff):
    return (256 if ff % 256 == 0 else ff), next(t for t in (512, 256, 128, width) if width % t == 0)


def expert_kernel(count, experts, tile_ff, tile_d, *refs):
    blocks, (gate_ref, up_ref, down_ref, *out_refs) = refs[:count], refs[count:]
    out_refs, (x_ref, w_ref, h_ref) = out_refs[:-3], out_refs[-3:]
    gather_rows(blocks, x_ref)
    gather_weights(experts, blocks, x_ref.shape[1], w_ref)
    first_half(x_ref, gate_ref, up_ref, h_ref, tile_ff, 0, h_ref.shape[1])
    second_half(h_ref, down_ref, w_ref, out_refs, tile_d, 0, x_ref.shape[1])


def expert(blocks, pieces, experts, w_gate, w_up, w_down):
    count, rows = len(blocks), blocks[0].shape[0]
    _, width, ff = w_gate.shape
    total = count * rows
    here = pl.BlockSpec(memory_space=pltpu.VMEM)
    return pl.pallas_call(
        functools.partial(expert_kernel, count, experts, *tiles(width, ff)),
        out_shape=[pltpu.VMEM((n * rows, width), kind) for n, kind in pieces],
        in_specs=[here] * (count + 3),
        out_specs=[here] * len(pieces),
        scratch_shapes=[pltpu.VMEM((total, width), BF16), pltpu.VMEM((total, 1), F32), pltpu.VMEM((total, ff), BF16)],
        compiler_params=pltpu.CompilerParams(vmem_limit_bytes=SCRATCH),
        cost_estimate=pl.CostEstimate(
            flops=6 * max(total, 256) * width * ff, bytes_accessed=0, transcendentals=total * ff
        ),
    )(*blocks, w_gate, w_up, w_down)


def local(order, tokens, routes, gates, w_gate, w_up, w_down):
    chips = len(order)
    experts = 2 * chips
    rows, width = tokens.shape
    forth = [(2 * order[i], 2 * order[(i + 1) % chips]) for i in range(chips)]
    spin = forth + [(b + 1, a + 1) for a, b in forth]
    swap = [(i, i ^ 1) for i in range(experts)]
    send = lambda a: lax.ppermute(a, "node", spin)
    sibling = lambda a: lax.ppermute(a, "node", swap)
    together = lax.optimization_barrier
    block = lambda a, j: a[j * rows : (j + 1) * rows]

    far = chips // 2
    own = pack(tokens, routes, gates, experts)
    up, up_twin, down, down_twin = {0: own}, {0: sibling(own)}, {}, {}
    for k in range(1, far):
        up[k] = send(up[k - 1])
        up_twin[k] = send(up_twin[k - 1])
        down_twin[k], down[k] = sibling(up[k]), sibling(up_twin[k])
    up[far] = send(up[far - 1])
    far_twin = sibling(up[far])

    mine, theirs = {}, {}
    weights = w_gate, w_up, w_down

    def compute(places, heads):
        kept = [up[k] if k >= 0 else down[-k] for k in places]
        given = [far_twin if k == far else (down_twin[k] if k > 0 else up_twin[-k]) for k in places]
        sizes = [n for n in (heads, len(places) - heads) if n]
        return expert(kept + given, [(len(kept), F32)] + [(n, BF16) for n in sizes], experts, *weights)

    def note(places, out, pieces):
        at = [(piece, j) for piece in pieces for j in range(piece.shape[0] // rows)]
        for j, k in enumerate(places):
            mine[k], theirs[k] = (out, j), at[j]

    def add(k, last, *arrived):
        piece, at = theirs[k]
        (piece, *arrived), _ = together(((piece, *arrived), last))
        total = block(mine[k][0], mine[k][1]) + block(piece, at).astype(F32)
        for a in arrived:
            total = total + a.astype(F32)
        return total

    up, up_twin, down, down_twin, far_twin = together((up, up_twin, down, down_twin, far_twin))
    late = [far, far - 1, 1 - far]
    out, first, other = compute(late, 1)
    first = sibling(first)
    note(late[:1], out, [first])
    last = add(far, first).astype(BF16)
    other, _ = together((sibling(other), last))
    note(late[1:], None, [other])
    for j, k in enumerate(late):
        mine[k] = out, j

    cut = rows // 2
    return_send = lambda a: lax.ppermute(a, "node", [(b, a) for a, b in spin])
    ahead, astern = send(last[:cut]), return_send(last[cut:])
    tasks = [[s * k for k in range(2, far - 1) for s in (1, -1)], [1, -1], [0]]
    computed = None
    for d in range(far - 1, -1, -1):
        exchanged, computed = computed, None
        if exchanged is not None:
            places, out, piece = exchanged
            piece, _ = together((piece, last))
            exchanged = places, out, sibling(piece)
        if tasks:
            places = tasks.pop(0)
            saved = up, down, up_twin, down_twin
            up, down, up_twin, down_twin, _ = together((*saved, last))
            out, piece = compute(places, 0)
            out, piece, ahead = together((out, piece, ahead))
            up, down, up_twin, down_twin = saved
            computed = places, out, piece
        if exchanged is not None:
            places, out, piece = exchanged
            piece, ahead = together((piece, ahead))
            note(places, out, [piece])
        if d == far - 1:
            pad = jnp.zeros_like(ahead)
            ahead = jnp.concatenate([ahead, pad], axis=0)
            astern = jnp.concatenate([pad, astern], axis=0)
        if d:
            last = add(-d, last, ahead).astype(BF16)
            ahead = send(last)
            last = add(d, last, astern).astype(BF16)
            astern = return_send(last)
    total = add(0, last, ahead)
    astern, total = together((astern, total))
    return (total + astern.astype(F32)).astype(BF16)


def solution(mesh):
    order = chip_order(mesh)
    in_specs = (
        P(("groups", "node"), None),
        P(("groups", "node"), None),
        P(("groups", "node"), None),
        P("node", None, None),
        P("node", None, None),
        P("node", None, None),
    )
    out_specs = P(("groups", "node"), None)
    body = functools.partial(local, order)
    return jax.shard_map(body, mesh=mesh, in_specs=in_specs, out_specs=out_specs, check_vma=False)
```

```python
import functools

import jax
import jax.numpy as jnp
from jax import lax
from jax.experimental import pallas as pl
from jax.experimental.pallas import tpu as pltpu
from jax.sharding import PartitionSpec as P

F32, BF16 = jnp.float32, jnp.bfloat16
SCRATCH = 16 * 2**20


def chip_order(mesh):
    names = list(mesh.axis_names)
    count = mesh.shape["node"]
    row = mesh.devices.transpose([names.index(n) for n in names if n != "node"] + [names.index("node")])
    row = list(row.reshape(-1, count)[0])
    chips = [tuple(getattr(d, "coords", None) or (i // 2,)) for i, d in enumerate(row)][::2]
    order = list(range(len(chips)))
    axes = [a for a in range(len(chips[0])) if len({c[a] for c in chips}) > 1]
    if len(axes) == 2:
        short, long = sorted(axes, key=lambda a: len({c[a] for c in chips}))
        low = min(c[short] for c in chips)
        if len({c[short] for c in chips}) == 2:
            order.sort(key=lambda i: (chips[i][short], chips[i][long] if chips[i][short] == low else -chips[i][long]))
    return order


def pack_kernel(experts, tok_hbm, routes_hbm, gates_hbm, out_ref, routes_ref, gates_ref, sems):
    rows, width = tok_hbm.shape
    extra = out_ref.shape[1] - width
    moves = [
        pltpu.make_async_copy(routes_hbm, routes_ref, sems.at[0]),
        pltpu.make_async_copy(gates_hbm, gates_ref, sems.at[1]),
        pltpu.make_async_copy(tok_hbm, out_ref.at[:, :width], sems.at[2]),
    ]
    for move in moves:
        move.start()
    for move in moves[:2]:
        move.wait()
    lane = lax.broadcasted_iota(jnp.int32, (extra, rows), 0)
    expert, piece = lax.rem(lane, experts), lax.div(lane, experts)
    weight = jnp.zeros((extra, rows), F32)
    for k in range(routes_ref.shape[0]):
        weight += jnp.where(routes_ref[k : k + 1] == expert, gates_ref[k : k + 1], 0.0)
    high = weight.astype(BF16).astype(F32)
    middle = (weight - high).astype(BF16).astype(F32)
    low = weight - high - middle
    table = jnp.where(piece == 0, high, jnp.where(piece == 1, middle, jnp.where(piece == 2, low, 0.0)))
    out_ref[:, width:] = table.T.astype(BF16)
    moves[2].wait()


def pack(tokens, routes, gates, experts):
    rows, width = tokens.shape
    extra = pl.cdiv(3 * experts, 128) * 128
    there = pl.BlockSpec(memory_space=pltpu.HBM)
    return pl.pallas_call(
        functools.partial(pack_kernel, experts),
        out_shape=pltpu.VMEM((rows, width + extra), BF16),
        in_specs=[there] * 3,
        out_specs=pl.BlockSpec(memory_space=pltpu.VMEM),
        scratch_shapes=[
            pltpu.VMEM(routes.shape[::-1], routes.dtype),
            pltpu.VMEM(gates.shape[::-1], gates.dtype),
            pltpu.SemaphoreType.DMA((3,)),
        ],
        compiler_params=pltpu.CompilerParams(vmem_limit_bytes=SCRATCH),
        cost_estimate=pl.CostEstimate(flops=10 * 2**30, bytes_accessed=0, transcendentals=0),
    )(hbm(tokens), hbm(routes.T), hbm(gates.T))


def hbm(a):
    return pltpu.with_memory_space_constraint(a, pltpu.HBM)


def gather_rows(blocks, x_ref):
    rows, width = blocks[0].shape[0], x_ref.shape[1]
    for at, ref in enumerate(blocks):
        x_ref[at * rows : (at + 1) * rows, :] = ref[:, :width]


def gather_weights(experts, blocks, width, w_ref):
    me = lax.axis_index("node")
    rows = blocks[0].shape[0]
    for at, ref in enumerate(blocks):
        table = ref[:, width:].astype(F32)
        lane = lax.broadcasted_iota(jnp.int32, table.shape, 1)
        own = lax.rem(lane, experts) == me
        w_ref[at * rows : (at + 1) * rows, :] = jnp.sum(jnp.where(own, table, 0.0), axis=1, keepdims=True)


def first_half(x_ref, gate_ref, up_ref, h_ref, tile, begin, end):
    for j in range(begin // tile, end // tile):
        at = slice(j * tile, (j + 1) * tile)
        gate = jnp.dot(x_ref[...], gate_ref[0, :, at], preferred_element_type=F32)
        upper = jnp.dot(x_ref[...], up_ref[0, :, at], preferred_element_type=F32)
        h_ref[:, at] = (gate / (1.0 + jnp.exp(-gate)) * upper).astype(BF16)


def second_half(h_ref, down_ref, w_ref, out_refs, tile, begin, end):
    for j in range(begin // tile, end // tile):
        at = slice(j * tile, (j + 1) * tile)
        out = jnp.dot(h_ref[...], down_ref[0, :, at], preferred_element_type=F32) * w_ref[...]
        row = 0
        for ref in out_refs:
            ref[:, at] = out[row : row + ref.shape[0]].astype(ref.dtype)
            row += ref.shape[0]


def tiles(width, ff):
    return (256 if ff % 256 == 0 else ff), next(t for t in (512, 256, 128, width) if width % t == 0)


def expert_kernel(count, experts, tile_ff, tile_d, *refs):
    blocks, (gate_ref, up_ref, down_ref, *out_refs) = refs[:count], refs[count:]
    out_refs, (x_ref, w_ref, h_ref) = out_refs[:-3], out_refs[-3:]
    gather_rows(blocks, x_ref)
    gather_weights(experts, blocks, x_ref.shape[1], w_ref)
    first_half(x_ref, gate_ref, up_ref, h_ref, tile_ff, 0, h_ref.shape[1])
    second_half(h_ref, down_ref, w_ref, out_refs, tile_d, 0, x_ref.shape[1])


def expert(blocks, pieces, experts, w_gate, w_up, w_down):
    count, rows = len(blocks), blocks[0].shape[0]
    _, width, ff = w_gate.shape
    total = count * rows
    here = pl.BlockSpec(memory_space=pltpu.VMEM)
    return pl.pallas_call(
        functools.partial(expert_kernel, count, experts, *tiles(width, ff)),
        out_shape=[pltpu.VMEM((n * rows, width), kind) for n, kind in pieces],
        in_specs=[here] * (count + 3),
        out_specs=[here] * len(pieces),
        scratch_shapes=[pltpu.VMEM((total, width), BF16), pltpu.VMEM((total, 1), F32), pltpu.VMEM((total, ff), BF16)],
        compiler_params=pltpu.CompilerParams(vmem_limit_bytes=SCRATCH),
        cost_estimate=pl.CostEstimate(
            flops=6 * max(total, 256) * width * ff, bytes_accessed=0, transcendentals=total * ff
        ),
    )(*blocks, w_gate, w_up, w_down)


def local(order, tokens, routes, gates, w_gate, w_up, w_down):
    chips = len(order)
    experts = 2 * chips
    rows, width = tokens.shape
    forth = [(2 * order[i], 2 * order[(i + 1) % chips]) for i in range(chips)]
    spin = forth + [(b + 1, a + 1) for a, b in forth]
    swap = [(i, i ^ 1) for i in range(experts)]
    turn = dict(spin)
    spin_two = [(a, turn[b]) for a, b in spin]
    reverse = lambda pairs: [(b, a) for a, b in pairs]
    send = lambda a: lax.ppermute(a, "node", spin)
    send_two = lambda a: lax.ppermute(a, "node", spin_two)
    return_send = lambda a: lax.ppermute(a, "node", reverse(spin))
    return_two = lambda a: lax.ppermute(a, "node", reverse(spin_two))
    sibling = lambda a: lax.ppermute(a, "node", swap)
    together = lax.optimization_barrier
    block = lambda a, j: a[j * rows : (j + 1) * rows]

    far = chips // 2
    own = pack(tokens, routes, gates, experts)
    up, up_twin, down, down_twin = {0: own}, {0: sibling(own)}, {}, {}
    for k in range(1, far):
        up[k] = send(up[k - 1])
        up_twin[k] = send(up_twin[k - 1])
        down_twin[k], down[k] = sibling(up[k]), sibling(up_twin[k])
    up[far] = send_two(up[far - 2])
    far_twin = sibling(up[far])

    mine, theirs = {}, {}
    weights = w_gate, w_up, w_down

    def compute(places, heads):
        kept = [up[k] if k >= 0 else down[-k] for k in places]
        given = [far_twin if k == far else (down_twin[k] if k > 0 else up_twin[-k]) for k in places]
        sizes = [n for n in (heads, len(places) - heads) if n]
        return expert(kept + given, [(len(kept), F32)] + [(n, BF16) for n in sizes], experts, *weights)

    def note(places, out, pieces):
        at = [(piece, j) for piece in pieces for j in range(piece.shape[0] // rows)]
        for j, k in enumerate(places):
            mine[k], theirs[k] = (out, j), at[j]

    def add(k, last, *arrived):
        piece, at = theirs[k]
        (piece, *arrived), _ = together(((piece, *arrived), last))
        total = block(mine[k][0], mine[k][1]) + block(piece, at).astype(F32)
        for a in arrived:
            total = total + a.astype(F32)
        return total

    up, up_twin, down, down_twin, far_twin = together((up, up_twin, down, down_twin, far_twin))
    late = [far] + [s * k for k in (far - 1, far - 2) for s in (1, -1)]
    out, first, other = compute(late, 3)
    note(late, out, [sibling(first), sibling(other)])

    cut = rows // 2
    last = add(far, out).astype(BF16)
    ahead_two, astern_two = send_two(last[:cut]), return_two(last[cut:])
    last = add(1 - far, last).astype(BF16)
    ahead = send(last)
    last = add(far - 1, last).astype(BF16)
    astern = return_send(last)
    tasks = [[s * k for k in range(2, far - 2) for s in (1, -1)], [0, 1, -1]]
    tasks = [places for places in tasks if places]
    computed = None
    for d in range(far - 2, -1, -1):
        exchanged, computed = computed, None
        if exchanged is not None:
            places, out, piece = exchanged
            piece, _ = together((piece, last))
            exchanged = places, out, sibling(piece)
        if tasks:
            places = tasks.pop(0)
            saved = up, down, up_twin, down_twin
            up, down, up_twin, down_twin, _ = together((*saved, last))
            out, piece = compute(places, 0)
            out, piece, ahead = together((out, piece, ahead))
            up, down, up_twin, down_twin = saved
            computed = places, out, piece
        if exchanged is not None:
            places, out, piece = exchanged
            piece, ahead = together((piece, ahead))
            note(places, out, [piece])
        if d:
            ahead_all, astern_all = [ahead], [astern]
            if d == far - 2:
                pad = jnp.zeros_like(ahead_two)
                ahead_all.append(jnp.concatenate([ahead_two, pad], axis=0))
                astern_all.append(jnp.concatenate([pad, astern_two], axis=0))
            last = add(-d, last, *ahead_all).astype(BF16)
            ahead = send(last)
            last = add(d, last, *astern_all).astype(BF16)
            astern = return_send(last)
    total = add(0, last, ahead)
    astern, total = together((astern, total))
    return (total + astern.astype(F32)).astype(BF16)


def solution(mesh):
    order = chip_order(mesh)
    in_specs = (
        P(("groups", "node"), None),
        P(("groups", "node"), None),
        P(("groups", "node"), None),
        P("node", None, None),
        P("node", None, None),
        P("node", None, None),
    )
    out_specs = P(("groups", "node"), None)
    body = functools.partial(local, order)
    return jax.shard_map(body, mesh=mesh, in_specs=in_specs, out_specs=out_specs, check_vma=False)
```

```python
import functools

import jax
import jax.numpy as jnp
from jax import lax
from jax.experimental import pallas as pl
from jax.experimental.pallas import tpu as pltpu
from jax.sharding import PartitionSpec as P

F32, BF16 = jnp.float32, jnp.bfloat16
SCRATCH = 16 * 2**20


def chip_order(mesh):
    names = list(mesh.axis_names)
    count = mesh.shape["node"]
    row = mesh.devices.transpose([names.index(n) for n in names if n != "node"] + [names.index("node")])
    row = list(row.reshape(-1, count)[0])
    chips = [tuple(getattr(d, "coords", None) or (i // 2,)) for i, d in enumerate(row)][::2]
    order = list(range(len(chips)))
    axes = [a for a in range(len(chips[0])) if len({c[a] for c in chips}) > 1]
    if len(axes) == 2:
        short, long = sorted(axes, key=lambda a: len({c[a] for c in chips}))
        low = min(c[short] for c in chips)
        if len({c[short] for c in chips}) == 2:
            order.sort(key=lambda i: (chips[i][short], chips[i][long] if chips[i][short] == low else -chips[i][long]))
    return order


def pack_kernel(experts, tok_hbm, routes_hbm, gates_hbm, out_ref, routes_ref, gates_ref, sems):
    rows, width = tok_hbm.shape
    extra = out_ref.shape[1] - width
    moves = [
        pltpu.make_async_copy(routes_hbm, routes_ref, sems.at[0]),
        pltpu.make_async_copy(gates_hbm, gates_ref, sems.at[1]),
        pltpu.make_async_copy(tok_hbm, out_ref.at[:, :width], sems.at[2]),
    ]
    for move in moves:
        move.start()
    for move in moves[:2]:
        move.wait()
    lane = lax.broadcasted_iota(jnp.int32, (extra, rows), 0)
    expert, piece = lax.rem(lane, experts), lax.div(lane, experts)
    weight = jnp.zeros((extra, rows), F32)
    for k in range(routes_ref.shape[0]):
        weight += jnp.where(routes_ref[k : k + 1] == expert, gates_ref[k : k + 1], 0.0)
    high = weight.astype(BF16).astype(F32)
    middle = (weight - high).astype(BF16).astype(F32)
    low = weight - high - middle
    table = jnp.where(piece == 0, high, jnp.where(piece == 1, middle, jnp.where(piece == 2, low, 0.0)))
    out_ref[:, width:] = table.T.astype(BF16)
    moves[2].wait()


def pack(tokens, routes, gates, experts):
    rows, width = tokens.shape
    extra = pl.cdiv(3 * experts, 128) * 128
    there = pl.BlockSpec(memory_space=pltpu.HBM)
    return pl.pallas_call(
        functools.partial(pack_kernel, experts),
        out_shape=pltpu.VMEM((rows, width + extra), BF16),
        in_specs=[there] * 3,
        out_specs=pl.BlockSpec(memory_space=pltpu.VMEM),
        scratch_shapes=[
            pltpu.VMEM(routes.shape[::-1], routes.dtype),
            pltpu.VMEM(gates.shape[::-1], gates.dtype),
            pltpu.SemaphoreType.DMA((3,)),
        ],
        compiler_params=pltpu.CompilerParams(vmem_limit_bytes=SCRATCH),
        cost_estimate=pl.CostEstimate(flops=10 * 2**30, bytes_accessed=0, transcendentals=0),
    )(hbm(tokens), hbm(routes.T), hbm(gates.T))


def hbm(a):
    return pltpu.with_memory_space_constraint(a, pltpu.HBM)


def gather_rows(blocks, x_ref):
    rows, width = blocks[0].shape[0], x_ref.shape[1]
    for at, ref in enumerate(blocks):
        x_ref[at * rows : (at + 1) * rows, :] = ref[:, :width]


def gather_weights(experts, blocks, width, w_ref):
    me = lax.axis_index("node")
    rows = blocks[0].shape[0]
    for at, ref in enumerate(blocks):
        table = ref[:, width:].astype(F32)
        lane = lax.broadcasted_iota(jnp.int32, table.shape, 1)
        own = lax.rem(lane, experts) == me
        w_ref[at * rows : (at + 1) * rows, :] = jnp.sum(jnp.where(own, table, 0.0), axis=1, keepdims=True)


def first_half(x_ref, gate_ref, up_ref, h_ref, tile, begin, end):
    for j in range(begin // tile, end // tile):
        at = slice(j * tile, (j + 1) * tile)
        gate = jnp.dot(x_ref[...], gate_ref[0, :, at], preferred_element_type=F32)
        upper = jnp.dot(x_ref[...], up_ref[0, :, at], preferred_element_type=F32)
        h_ref[:, at] = (gate / (1.0 + jnp.exp(-gate)) * upper).astype(BF16)


def second_half(h_ref, down_ref, w_ref, out_refs, tile, begin, end):
    for j in range(begin // tile, end // tile):
        at = slice(j * tile, (j + 1) * tile)
        out = jnp.dot(h_ref[...], down_ref[0, :, at], preferred_element_type=F32) * w_ref[...]
        row = 0
        for ref in out_refs:
            ref[:, at] = out[row : row + ref.shape[0]].astype(ref.dtype)
            row += ref.shape[0]


def tiles(width, ff):
    return (256 if ff % 256 == 0 else ff), next(t for t in (512, 256, 128, width) if width % t == 0)


def expert_kernel(count, experts, tile_ff, tile_d, *refs):
    blocks, (gate_ref, up_ref, down_ref, *out_refs) = refs[:count], refs[count:]
    out_refs, (x_ref, w_ref, h_ref) = out_refs[:-3], out_refs[-3:]
    gather_rows(blocks, x_ref)
    gather_weights(experts, blocks, x_ref.shape[1], w_ref)
    first_half(x_ref, gate_ref, up_ref, h_ref, tile_ff, 0, h_ref.shape[1])
    second_half(h_ref, down_ref, w_ref, out_refs, tile_d, 0, x_ref.shape[1])


def expert(blocks, pieces, experts, w_gate, w_up, w_down):
    count, rows = len(blocks), blocks[0].shape[0]
    _, width, ff = w_gate.shape
    total = count * rows
    here = pl.BlockSpec(memory_space=pltpu.VMEM)
    return pl.pallas_call(
        functools.partial(expert_kernel, count, experts, *tiles(width, ff)),
        out_shape=[pltpu.VMEM((n * rows, width), kind) for n, kind in pieces],
        in_specs=[here] * (count + 3),
        out_specs=[here] * len(pieces),
        scratch_shapes=[pltpu.VMEM((total, width), BF16), pltpu.VMEM((total, 1), F32), pltpu.VMEM((total, ff), BF16)],
        compiler_params=pltpu.CompilerParams(vmem_limit_bytes=SCRATCH),
        cost_estimate=pl.CostEstimate(
            flops=6 * max(total, 256) * width * ff, bytes_accessed=0, transcendentals=total * ff
        ),
    )(*blocks, w_gate, w_up, w_down)


def local(order, tokens, routes, gates, w_gate, w_up, w_down):
    chips = len(order)
    experts = 2 * chips
    rows, width = tokens.shape
    forth = [(2 * order[i], 2 * order[(i + 1) % chips]) for i in range(chips)]
    spin = forth + [(b + 1, a + 1) for a, b in forth]
    swap = [(i, i ^ 1) for i in range(experts)]
    send = lambda a: lax.ppermute(a, "node", spin)
    sibling = lambda a: lax.ppermute(a, "node", swap)
    together = lax.optimization_barrier
    block = lambda a, j: a[j * rows : (j + 1) * rows]

    far = chips // 2
    own = pack(tokens, routes, gates, experts)
    up, up_twin, down, down_twin = {0: own}, {0: sibling(own)}, {}, {}
    for k in range(1, far):
        up[k] = send(up[k - 1])
        up_twin[k] = send(up_twin[k - 1])
        down_twin[k], down[k] = sibling(up[k]), sibling(up_twin[k])
    up[far] = send(up[far - 1])
    far_twin = sibling(up[far])

    mine, theirs = {}, {}
    weights = w_gate, w_up, w_down

    def compute(keep, give, sizes):
        kept = [up[k] if k >= 0 else down[-k] for k in keep]
        given = [far_twin if k == far else (down_twin[k] if k > 0 else up_twin[-k]) for k in give]
        sizes = [n for n in sizes if n]
        return expert(kept + given, [(len(kept), F32)] + [(n, BF16) for n in sizes], experts, *weights)

    def add(k, last, *arrived):
        piece, at = theirs[k]
        (piece, *arrived), _ = together(((piece, *arrived), last))
        total = block(mine[k][0], mine[k][1]) + block(piece, at).astype(F32)
        for a in arrived:
            total = total + a.astype(F32)
        return total

    up, up_twin, down, down_twin, far_twin = together((up, up_twin, down, down_twin, far_twin))
    places = [far] + [s * k for k in range(far - 1, 0, -1) for s in (1, -1)] + [0]
    out, *given = compute(places[:3], places, (1, 2, len(places) - 3))
    mine.update({k: (out, j) for j, k in enumerate(places[:3])})
    theirs[far] = sibling(given[0]), 0
    given[1] = sibling(given[1])
    theirs.update({k: (given[1], j) for j, k in enumerate(places[1:3])})
    last = add(far, out).astype(BF16)

    cut = rows // 2
    return_send = lambda a: lax.ppermute(a, "node", [(b, a) for a, b in spin])
    ahead, astern = send(last[:cut]), return_send(last[cut:])
    up, down, rest, _ = together((up, down, given[2], last))
    rest = sibling(rest)
    (out,) = compute(places[3:], [], ())
    out, ahead = together((out, ahead))
    mine.update({k: (out, j) for j, k in enumerate(places[3:])})
    theirs.update({k: (rest, j) for j, k in enumerate(places[3:])})
    pad = jnp.zeros_like(ahead)
    ahead, astern = jnp.concatenate([ahead, pad], axis=0), jnp.concatenate([pad, astern], axis=0)
    for d in range(far - 1, 0, -1):
        last = add(-d, last, ahead).astype(BF16)
        ahead = send(last)
        last = add(d, last, astern).astype(BF16)
        astern = return_send(last)
    total = add(0, last, ahead)
    astern, total = together((astern, total))
    return (total + astern.astype(F32)).astype(BF16)


def solution(mesh):
    order = chip_order(mesh)
    in_specs = (
        P(("groups", "node"), None),
        P(("groups", "node"), None),
        P(("groups", "node"), None),
        P("node", None, None),
        P("node", None, None),
        P("node", None, None),
    )
    out_specs = P(("groups", "node"), None)
    body = functools.partial(local, order)
    return jax.shard_map(body, mesh=mesh, in_specs=in_specs, out_specs=out_specs, check_vma=False)
```

```python
import functools

import jax
import jax.numpy as jnp
from jax import lax
from jax.experimental import pallas as pl
from jax.experimental.pallas import tpu as pltpu
from jax.sharding import PartitionSpec as P

F32, BF16 = jnp.float32, jnp.bfloat16
SCRATCH = 20 * 2**20


def chip_order(mesh):
    names = list(mesh.axis_names)
    count = mesh.shape["node"]
    row = mesh.devices.transpose([names.index(n) for n in names if n != "node"] + [names.index("node")])
    row = list(row.reshape(-1, count)[0])
    chips = [tuple(getattr(d, "coords", None) or (i // 2,)) for i, d in enumerate(row)][::2]
    order = list(range(len(chips)))
    axes = [a for a in range(len(chips[0])) if len({c[a] for c in chips}) > 1]
    if len(axes) == 2:
        short, long = sorted(axes, key=lambda a: len({c[a] for c in chips}))
        low = min(c[short] for c in chips)
        if len({c[short] for c in chips}) == 2:
            order.sort(key=lambda i: (chips[i][short], chips[i][long] if chips[i][short] == low else -chips[i][long]))
    return order


def pack_kernel(experts, tok_hbm, routes_hbm, gates_hbm, out_ref, routes_ref, gates_ref, sems):
    rows, width = tok_hbm.shape
    extra = out_ref.shape[1] - width
    moves = [
        pltpu.make_async_copy(routes_hbm, routes_ref, sems.at[0]),
        pltpu.make_async_copy(gates_hbm, gates_ref, sems.at[1]),
        pltpu.make_async_copy(tok_hbm, out_ref.at[:, :width], sems.at[2]),
    ]
    for move in moves:
        move.start()
    for move in moves[:2]:
        move.wait()
    lane = lax.broadcasted_iota(jnp.int32, (extra, rows), 0)
    expert, piece = lax.rem(lane, experts), lax.div(lane, experts)
    weight = jnp.zeros((extra, rows), F32)
    for k in range(routes_ref.shape[0]):
        weight += jnp.where(routes_ref[k : k + 1] == expert, gates_ref[k : k + 1], 0.0)
    high = weight.astype(BF16).astype(F32)
    middle = (weight - high).astype(BF16).astype(F32)
    low = weight - high - middle
    table = jnp.where(piece == 0, high, jnp.where(piece == 1, middle, jnp.where(piece == 2, low, 0.0)))
    out_ref[:, width:] = table.T.astype(BF16)
    moves[2].wait()


def pack(tokens, routes, gates, experts):
    rows, width = tokens.shape
    extra = pl.cdiv(3 * experts, 128) * 128
    there = pl.BlockSpec(memory_space=pltpu.HBM)
    return pl.pallas_call(
        functools.partial(pack_kernel, experts),
        out_shape=pltpu.VMEM((rows, width + extra), BF16),
        in_specs=[there] * 3,
        out_specs=pl.BlockSpec(memory_space=pltpu.VMEM),
        scratch_shapes=[
            pltpu.VMEM(routes.shape[::-1], routes.dtype),
            pltpu.VMEM(gates.shape[::-1], gates.dtype),
            pltpu.SemaphoreType.DMA((3,)),
        ],
        compiler_params=pltpu.CompilerParams(vmem_limit_bytes=SCRATCH),
        cost_estimate=pl.CostEstimate(flops=10 * 2**30, bytes_accessed=0, transcendentals=0),
    )(hbm(tokens), hbm(routes.T), hbm(gates.T))


def hbm(a):
    return pltpu.with_memory_space_constraint(a, pltpu.HBM)


def gather_rows(blocks, x_ref):
    rows, width = blocks[0].shape[0], x_ref.shape[1]
    for at, ref in enumerate(blocks):
        x_ref[at * rows : (at + 1) * rows, :] = ref[:, :width]


def gather_weights(experts, blocks, width, w_ref):
    me = lax.axis_index("node")
    rows = blocks[0].shape[0]
    for at, ref in enumerate(blocks):
        table = ref[:, width:].astype(F32)
        lane = lax.broadcasted_iota(jnp.int32, table.shape, 1)
        own = lax.rem(lane, experts) == me
        w_ref[at * rows : (at + 1) * rows, :] = jnp.sum(jnp.where(own, table, 0.0), axis=1, keepdims=True)


def first_half(x_ref, gate_ref, up_ref, h_ref, tile, begin, end):
    for j in range(begin // tile, end // tile):
        at = slice(j * tile, (j + 1) * tile)
        gate = jnp.dot(x_ref[...], gate_ref[0, :, at], preferred_element_type=F32)
        upper = jnp.dot(x_ref[...], up_ref[0, :, at], preferred_element_type=F32)
        h_ref[:, at] = (gate / (1.0 + jnp.exp(-gate)) * upper).astype(BF16)


def second_half(h_ref, down_ref, w_ref, out_refs, tile, begin, end):
    for j in range(begin // tile, end // tile):
        at = slice(j * tile, (j + 1) * tile)
        out = jnp.dot(h_ref[...], down_ref[0, :, at], preferred_element_type=F32) * w_ref[...]
        row = 0
        for ref in out_refs:
            ref[:, at] = out[row : row + ref.shape[0]].astype(ref.dtype)
            row += ref.shape[0]


def tiles(width, ff):
    return (256 if ff % 256 == 0 else ff), next(t for t in (512, 256, 128, width) if width % t == 0)


def expert_kernel(count, experts, tile_ff, tile_d, *refs):
    blocks, (gate_ref, up_ref, down_ref, *out_refs) = refs[:count], refs[count:]
    out_refs, (x_ref, w_ref, h_ref) = out_refs[:-3], out_refs[-3:]
    gather_rows(blocks, x_ref)
    gather_weights(experts, blocks, x_ref.shape[1], w_ref)
    first_half(x_ref, gate_ref, up_ref, h_ref, tile_ff, 0, h_ref.shape[1])
    second_half(h_ref, down_ref, w_ref, out_refs, tile_d, 0, x_ref.shape[1])


def expert(blocks, pieces, experts, w_gate, w_up, w_down):
    count, rows = len(blocks), blocks[0].shape[0]
    _, width, ff = w_gate.shape
    total = count * rows
    here = pl.BlockSpec(memory_space=pltpu.VMEM)
    return pl.pallas_call(
        functools.partial(expert_kernel, count, experts, *tiles(width, ff)),
        out_shape=[pltpu.VMEM((n * rows, width), kind) for n, kind in pieces],
        in_specs=[here] * (count + 3),
        out_specs=[here] * len(pieces),
        scratch_shapes=[pltpu.VMEM((total, width), BF16), pltpu.VMEM((total, 1), F32), pltpu.VMEM((total, ff), BF16)],
        compiler_params=pltpu.CompilerParams(vmem_limit_bytes=SCRATCH),
        cost_estimate=pl.CostEstimate(
            flops=6 * max(total, 256) * width * ff, bytes_accessed=0, transcendentals=total * ff
        ),
    )(*blocks, w_gate, w_up, w_down)


def local(order, tokens, routes, gates, w_gate, w_up, w_down):
    chips = len(order)
    experts = 2 * chips
    rows, width = tokens.shape
    forth = [(2 * order[i], 2 * order[(i + 1) % chips]) for i in range(chips)]
    spin = forth + [(b + 1, a + 1) for a, b in forth]
    swap = [(i, i ^ 1) for i in range(experts)]
    send = lambda a: lax.ppermute(a, "node", spin)
    sibling = lambda a: lax.ppermute(a, "node", swap)
    together = lax.optimization_barrier
    block = lambda a, j: a[j * rows : (j + 1) * rows]

    far = chips // 2
    own = pack(tokens, routes, gates, experts)
    up, up_twin, down, down_twin = {0: own}, {0: sibling(own)}, {}, {}
    for k in range(1, far):
        up[k] = send(up[k - 1])
        up_twin[k] = send(up_twin[k - 1])
        down_twin[k], down[k] = sibling(up[k]), sibling(up_twin[k])
    up[far] = send(up[far - 1])
    far_twin = sibling(up[far])

    kept, given = [up[far]], [far_twin]
    for k in range(far - 1, 0, -1):
        kept += [down_twin[k], down[k]]
        given += [up[k], up_twin[k]]
    kept, given = kept + [own], given + [up_twin[0]]
    end = len(kept) - 1
    mine, theirs = {}, {}

    def compute(keep, give, sizes):
        sizes = [n for n in sizes if n]
        blocks = [kept[j] for j in keep] + [given[j] for j in give]
        out, *pieces = expert(blocks, [(len(keep), F32)] + [(n, BF16) for n in sizes], experts, w_gate, w_up, w_down)
        return out, pieces

    def note(keep, out, give, pieces):
        mine.update({j: (out, at) for at, j in enumerate(keep)})
        theirs.update(zip(give, [(piece, at) for piece in pieces for at in range(piece.shape[0] // rows)]))

    keep, give = [end], [end - 2, end - 1, end]
    kept[end], given[end - 2 :], _ = together((kept[end], given[end - 2 :], up[far - 1]))
    out, pieces = compute(keep, give, (3,))
    out, pieces, kept[0], given[2] = together((out, pieces, kept[0], given[2]))
    given[0] = sibling(kept[0])
    kept[2] = sibling(given[2])
    pieces = [sibling(p) for p in pieces]
    note(keep, out, give, pieces)

    keep, give = [end - 2, end - 1], [end - 4, end - 3]
    kept[end - 2 : end], given[end - 4 : end - 2], _ = together((kept[end - 2 : end], given[end - 4 : end - 2], kept[0]))
    out_too, given_too = compute(keep, give, (2,))
    out_too, given_too, given[0], kept[2], pieces = together((out_too, given_too, given[0], kept[2], pieces))
    note([end], out, [end - 2, end - 1, end], pieces)
    sent_too = [sibling(p) for p in given_too]

    keep_last, give_last = list(range(end - 2)), list(range(end - 4))
    out, pieces = compute(keep_last, give_last, (2, len(give_last) - 2))
    out, pieces, sent_too = together((out, pieces, sent_too))
    note(keep, out_too, give, sent_too)
    note(keep_last, out, give_last, [sibling(p) for p in pieces])

    def add(j, *arrived):
        nonlocal last
        piece, at = theirs[j]
        (piece, *arrived), _ = together(((piece, *arrived), last))
        total = block(*mine[j]) + block(piece, at).astype(F32)
        for a in arrived:
            total = total + a.astype(F32)
        last = total.astype(BF16)
        return last

    last = mine[0][0]
    sums = send(add(0))
    sums_twin = []
    for j in range(1, end, 2):
        sums_twin = [send(add(j, *sums_twin))]
        sums = send(add(j + 1, sums))
    piece, sums = together((theirs[end][0], sums))
    total = block(*mine[end]) + block(piece, theirs[end][1]).astype(F32) + sums.astype(F32)
    for a in sums_twin:
        a, total = together((sibling(a), total))
        total = total + a.astype(F32)
    return total.astype(BF16)


def solution(mesh):
    order = chip_order(mesh)
    in_specs = (
        P(("groups", "node"), None),
        P(("groups", "node"), None),
        P(("groups", "node"), None),
        P("node", None, None),
        P("node", None, None),
        P("node", None, None),
    )
    out_specs = P(("groups", "node"), None)
    body = functools.partial(local, order)
    return jax.shard_map(body, mesh=mesh, in_specs=in_specs, out_specs=out_specs, check_vma=False)
```

```python
import functools

import jax
import jax.numpy as jnp
from jax import lax
from jax.experimental import pallas as pl
from jax.experimental.pallas import tpu as pltpu
from jax.sharding import PartitionSpec as P

F32, BF16 = jnp.float32, jnp.bfloat16
SCRATCH = 20 * 2**20


def chip_order(mesh):
    names = list(mesh.axis_names)
    count = mesh.shape["node"]
    row = mesh.devices.transpose([names.index(n) for n in names if n != "node"] + [names.index("node")])
    row = list(row.reshape(-1, count)[0])
    chips = [tuple(getattr(d, "coords", None) or (i // 2,)) for i, d in enumerate(row)][::2]
    order = list(range(len(chips)))
    axes = [a for a in range(len(chips[0])) if len({c[a] for c in chips}) > 1]
    if len(axes) == 2:
        short, long = sorted(axes, key=lambda a: len({c[a] for c in chips}))
        low = min(c[short] for c in chips)
        if len({c[short] for c in chips}) == 2:
            order.sort(key=lambda i: (chips[i][short], chips[i][long] if chips[i][short] == low else -chips[i][long]))
    return order


def pack_kernel(experts, tok_hbm, routes_hbm, gates_hbm, out_ref, routes_ref, gates_ref, sems):
    rows, width = tok_hbm.shape
    extra = out_ref.shape[1] - width
    moves = [
        pltpu.make_async_copy(routes_hbm, routes_ref, sems.at[0]),
        pltpu.make_async_copy(gates_hbm, gates_ref, sems.at[1]),
        pltpu.make_async_copy(tok_hbm, out_ref.at[:, :width], sems.at[2]),
    ]
    for move in moves:
        move.start()
    for move in moves[:2]:
        move.wait()
    lane = lax.broadcasted_iota(jnp.int32, (extra, rows), 0)
    expert, piece = lax.rem(lane, experts), lax.div(lane, experts)
    weight = jnp.zeros((extra, rows), F32)
    for k in range(routes_ref.shape[0]):
        weight += jnp.where(routes_ref[k : k + 1] == expert, gates_ref[k : k + 1], 0.0)
    high = weight.astype(BF16).astype(F32)
    middle = (weight - high).astype(BF16).astype(F32)
    low = weight - high - middle
    table = jnp.where(piece == 0, high, jnp.where(piece == 1, middle, jnp.where(piece == 2, low, 0.0)))
    out_ref[:, width:] = table.T.astype(BF16)
    moves[2].wait()


def pack(tokens, routes, gates, experts):
    rows, width = tokens.shape
    extra = pl.cdiv(3 * experts, 128) * 128
    there = pl.BlockSpec(memory_space=pltpu.HBM)
    return pl.pallas_call(
        functools.partial(pack_kernel, experts),
        out_shape=pltpu.VMEM((rows, width + extra), BF16),
        in_specs=[there] * 3,
        out_specs=pl.BlockSpec(memory_space=pltpu.VMEM),
        scratch_shapes=[
            pltpu.VMEM(routes.shape[::-1], routes.dtype),
            pltpu.VMEM(gates.shape[::-1], gates.dtype),
            pltpu.SemaphoreType.DMA((3,)),
        ],
        compiler_params=pltpu.CompilerParams(vmem_limit_bytes=SCRATCH),
        cost_estimate=pl.CostEstimate(flops=10 * 2**30, bytes_accessed=0, transcendentals=0),
    )(hbm(tokens), hbm(routes.T), hbm(gates.T))


def hbm(a):
    return pltpu.with_memory_space_constraint(a, pltpu.HBM)


def gather_rows(blocks, x_ref):
    rows, width = blocks[0].shape[0], x_ref.shape[1]
    for at, ref in enumerate(blocks):
        x_ref[at * rows : (at + 1) * rows, :] = ref[:, :width]


def gather_weights(experts, blocks, width, w_ref):
    me = lax.axis_index("node")
    rows = blocks[0].shape[0]
    for at, ref in enumerate(blocks):
        table = ref[:, width:].astype(F32)
        lane = lax.broadcasted_iota(jnp.int32, table.shape, 1)
        own = lax.rem(lane, experts) == me
        w_ref[at * rows : (at + 1) * rows, :] = jnp.sum(jnp.where(own, table, 0.0), axis=1, keepdims=True)


def first_half(x_ref, gate_ref, up_ref, h_ref, tile, begin, end):
    for j in range(begin // tile, end // tile):
        at = slice(j * tile, (j + 1) * tile)
        gate = jnp.dot(x_ref[...], gate_ref[0, :, at], preferred_element_type=F32)
        upper = jnp.dot(x_ref[...], up_ref[0, :, at], preferred_element_type=F32)
        h_ref[:, at] = (gate / (1.0 + jnp.exp(-gate)) * upper).astype(BF16)


def second_half(h_ref, down_ref, w_ref, out_refs, tile, begin, end):
    for j in range(begin // tile, end // tile):
        at = slice(j * tile, (j + 1) * tile)
        out = jnp.dot(h_ref[...], down_ref[0, :, at], preferred_element_type=F32) * w_ref[...]
        row = 0
        for ref in out_refs:
            ref[:, at] = out[row : row + ref.shape[0]].astype(ref.dtype)
            row += ref.shape[0]


def tiles(width, ff):
    return (256 if ff % 256 == 0 else ff), next(t for t in (512, 256, 128, width) if width % t == 0)


def expert_kernel(count, experts, tile_ff, tile_d, *refs):
    blocks, (gate_ref, up_ref, down_ref, *out_refs) = refs[:count], refs[count:]
    out_refs, (x_ref, w_ref, h_ref) = out_refs[:-3], out_refs[-3:]
    gather_rows(blocks, x_ref)
    gather_weights(experts, blocks, x_ref.shape[1], w_ref)
    first_half(x_ref, gate_ref, up_ref, h_ref, tile_ff, 0, h_ref.shape[1])
    second_half(h_ref, down_ref, w_ref, out_refs, tile_d, 0, x_ref.shape[1])


def expert(blocks, pieces, experts, w_gate, w_up, w_down):
    count, rows = len(blocks), blocks[0].shape[0]
    _, width, ff = w_gate.shape
    total = count * rows
    here = pl.BlockSpec(memory_space=pltpu.VMEM)
    return pl.pallas_call(
        functools.partial(expert_kernel, count, experts, *tiles(width, ff)),
        out_shape=[pltpu.VMEM((n * rows, width), kind) for n, kind in pieces],
        in_specs=[here] * (count + 3),
        out_specs=[here] * len(pieces),
        scratch_shapes=[pltpu.VMEM((total, width), BF16), pltpu.VMEM((total, 1), F32), pltpu.VMEM((total, ff), BF16)],
        compiler_params=pltpu.CompilerParams(vmem_limit_bytes=SCRATCH),
        cost_estimate=pl.CostEstimate(
            flops=6 * max(total, 256) * width * ff, bytes_accessed=0, transcendentals=total * ff
        ),
    )(*blocks, w_gate, w_up, w_down)


def local(order, tokens, routes, gates, w_gate, w_up, w_down):
    chips = len(order)
    experts = 2 * chips
    rows, width = tokens.shape
    forth = [(2 * order[i], 2 * order[(i + 1) % chips]) for i in range(chips)]
    spin = forth + [(b + 1, a + 1) for a, b in forth]
    swap = [(i, i ^ 1) for i in range(experts)]
    send = lambda a: lax.ppermute(a, "node", spin)
    sibling = lambda a: lax.ppermute(a, "node", swap)
    together = lax.optimization_barrier
    block = lambda a, j: a[j * rows : (j + 1) * rows]

    far = chips // 2
    own = pack(tokens, routes, gates, experts)
    up, up_twin, down, down_twin = {0: own}, {0: sibling(own)}, {}, {}
    for k in range(1, far):
        up[k] = send(up[k - 1])
        up_twin[k] = send(up_twin[k - 1])
        down_twin[k], down[k] = sibling(up[k]), sibling(up_twin[k])
    up[far] = send(up[far - 1])
    far_twin = sibling(up[far])

    kept, given = [up[far]], [far_twin]
    for k in range(far - 1, 0, -1):
        kept += [down_twin[k], down[k]]
        given += [up[k], up_twin[k]]
    kept, given = kept + [own], given + [up_twin[0]]
    end = len(kept) - 1
    mine, theirs = {}, {}

    def compute(keep, give, sizes):
        sizes = [n for n in sizes if n]
        blocks = [kept[j] for j in keep] + [given[j] for j in give]
        out, *pieces = expert(blocks, [(len(keep), F32)] + [(n, BF16) for n in sizes], experts, w_gate, w_up, w_down)
        return out, pieces

    def note(keep, out, give, pieces):
        mine.update({j: (out, at) for at, j in enumerate(keep)})
        theirs.update(zip(give, [(piece, at) for piece in pieces for at in range(piece.shape[0] // rows)]))

    keep, give = [end], [end - 2, end - 1, end]
    out, pieces = compute(keep, give, (3,))
    out, pieces, kept[0], given[2] = together((out, pieces, kept[0], given[2]))
    given[0] = sibling(kept[0])
    kept[2] = sibling(given[2])
    pieces = [sibling(p) for p in pieces]
    note(keep, out, give, pieces)

    keep, give = [end - 2, end - 1], [end - 4, end - 3]
    kept[end - 2 : end], given[end - 4 : end - 2], _ = together((kept[end - 2 : end], given[end - 4 : end - 2], kept[0]))
    out_too, given_too = compute(keep, give, (2,))
    out_too, given_too, given[0], kept[2], pieces = together((out_too, given_too, given[0], kept[2], pieces))
    note([end], out, [end - 2, end - 1, end], pieces)
    sent_too = [sibling(p) for p in given_too]

    keep_last, give_last = list(range(end - 2)), list(range(end - 4))
    out, pieces = compute(keep_last, give_last, (2, len(give_last) - 2))
    out, pieces, sent_too = together((out, pieces, sent_too))
    note(keep, out_too, give, sent_too)
    note(keep_last, out, give_last, [sibling(p) for p in pieces])

    def add(j, *arrived):
        nonlocal last
        piece, at = theirs[j]
        (piece, *arrived), _ = together(((piece, *arrived), last))
        total = block(*mine[j]) + block(piece, at).astype(F32)
        for a in arrived:
            total = total + a.astype(F32)
        last = total.astype(BF16)
        return last

    last = mine[0][0]
    sums = send(add(0))
    sums_twin = []
    for j in range(1, end, 2):
        sums_twin = [send(add(j, *sums_twin))]
        sums = send(add(j + 1, sums))
    piece, sums = together((theirs[end][0], sums))
    total = block(*mine[end]) + block(piece, theirs[end][1]).astype(F32) + sums.astype(F32)
    for a in sums_twin:
        a, total = together((sibling(a), total))
        total = total + a.astype(F32)
    return total.astype(BF16)


def solution(mesh):
    order = chip_order(mesh)
    in_specs = (
        P(("groups", "node"), None),
        P(("groups", "node"), None),
        P(("groups", "node"), None),
        P("node", None, None),
        P("node", None, None),
        P("node", None, None),
    )
    out_specs = P(("groups", "node"), None)
    body = functools.partial(local, order)
    return jax.shard_map(body, mesh=mesh, in_specs=in_specs, out_specs=out_specs, check_vma=False)
```

```python
import functools

import jax
import jax.numpy as jnp
from jax import lax
from jax.experimental import pallas as pl
from jax.experimental.pallas import tpu as pltpu
from jax.sharding import PartitionSpec as P

F32, BF16 = jnp.float32, jnp.bfloat16
SCRATCH = 20 * 2**20


def chip_order(mesh):
    names = list(mesh.axis_names)
    count = mesh.shape["node"]
    row = mesh.devices.transpose([names.index(n) for n in names if n != "node"] + [names.index("node")])
    row = list(row.reshape(-1, count)[0])
    chips = [tuple(getattr(d, "coords", None) or (i // 2,)) for i, d in enumerate(row)][::2]
    order = list(range(len(chips)))
    axes = [a for a in range(len(chips[0])) if len({c[a] for c in chips}) > 1]
    if len(axes) == 2:
        short, long = sorted(axes, key=lambda a: len({c[a] for c in chips}))
        low = min(c[short] for c in chips)
        if len({c[short] for c in chips}) == 2:
            order.sort(key=lambda i: (chips[i][short], chips[i][long] if chips[i][short] == low else -chips[i][long]))
    return order


def pack_kernel(experts, tok_hbm, routes_hbm, gates_hbm, out_ref, routes_ref, gates_ref, sems):
    rows, width = tok_hbm.shape
    extra = out_ref.shape[1] - width
    moves = [
        pltpu.make_async_copy(routes_hbm, routes_ref, sems.at[0]),
        pltpu.make_async_copy(gates_hbm, gates_ref, sems.at[1]),
        pltpu.make_async_copy(tok_hbm, out_ref.at[:, :width], sems.at[2]),
    ]
    for move in moves:
        move.start()
    for move in moves[:2]:
        move.wait()
    lane = lax.broadcasted_iota(jnp.int32, (extra, rows), 0)
    expert, piece = lax.rem(lane, experts), lax.div(lane, experts)
    weight = jnp.zeros((extra, rows), F32)
    for k in range(routes_ref.shape[0]):
        weight += jnp.where(routes_ref[k : k + 1] == expert, gates_ref[k : k + 1], 0.0)
    high = weight.astype(BF16).astype(F32)
    middle = (weight - high).astype(BF16).astype(F32)
    low = weight - high - middle
    table = jnp.where(piece == 0, high, jnp.where(piece == 1, middle, jnp.where(piece == 2, low, 0.0)))
    out_ref[:, width:] = table.T.astype(BF16)
    moves[2].wait()


def pack(tokens, routes, gates, experts):
    rows, width = tokens.shape
    extra = pl.cdiv(3 * experts, 128) * 128
    there = pl.BlockSpec(memory_space=pltpu.HBM)
    return pl.pallas_call(
        functools.partial(pack_kernel, experts),
        out_shape=pltpu.VMEM((rows, width + extra), BF16),
        in_specs=[there] * 3,
        out_specs=pl.BlockSpec(memory_space=pltpu.VMEM),
        scratch_shapes=[
            pltpu.VMEM(routes.shape[::-1], routes.dtype),
            pltpu.VMEM(gates.shape[::-1], gates.dtype),
            pltpu.SemaphoreType.DMA((3,)),
        ],
        compiler_params=pltpu.CompilerParams(vmem_limit_bytes=SCRATCH),
        cost_estimate=pl.CostEstimate(flops=10 * 2**30, bytes_accessed=0, transcendentals=0),
    )(hbm(tokens), hbm(routes.T), hbm(gates.T))


def hbm(a):
    return pltpu.with_memory_space_constraint(a, pltpu.HBM)


def gather_rows(blocks, x_ref):
    rows, width = blocks[0].shape[0], x_ref.shape[1]
    for at, ref in enumerate(blocks):
        x_ref[at * rows : (at + 1) * rows, :] = ref[:, :width]


def gather_weights(experts, blocks, width, w_ref):
    me = lax.axis_index("node")
    rows = blocks[0].shape[0]
    for at, ref in enumerate(blocks):
        table = ref[:, width:].astype(F32)
        lane = lax.broadcasted_iota(jnp.int32, table.shape, 1)
        own = lax.rem(lane, experts) == me
        w_ref[at * rows : (at + 1) * rows, :] = jnp.sum(jnp.where(own, table, 0.0), axis=1, keepdims=True)


def first_half(x_ref, gate_ref, up_ref, h_ref, tile, begin, end):
    for j in range(begin // tile, end // tile):
        at = slice(j * tile, (j + 1) * tile)
        gate = jnp.dot(x_ref[...], gate_ref[0, :, at], preferred_element_type=F32)
        upper = jnp.dot(x_ref[...], up_ref[0, :, at], preferred_element_type=F32)
        h_ref[:, at] = (gate / (1.0 + jnp.exp(-gate)) * upper).astype(BF16)


def second_half(h_ref, down_ref, w_ref, out_refs, tile, begin, end):
    for j in range(begin // tile, end // tile):
        at = slice(j * tile, (j + 1) * tile)
        out = jnp.dot(h_ref[...], down_ref[0, :, at], preferred_element_type=F32) * w_ref[...]
        row = 0
        for ref in out_refs:
            ref[:, at] = out[row : row + ref.shape[0]].astype(ref.dtype)
            row += ref.shape[0]


def tiles(width, ff):
    return (256 if ff % 256 == 0 else ff), next(t for t in (512, 256, 128, width) if width % t == 0)


def expert_kernel(count, experts, tile_ff, tile_d, *refs):
    blocks, (gate_ref, up_ref, down_ref, *out_refs) = refs[:count], refs[count:]
    out_refs, (x_ref, w_ref, h_ref) = out_refs[:-3], out_refs[-3:]
    gather_rows(blocks, x_ref)
    gather_weights(experts, blocks, x_ref.shape[1], w_ref)
    first_half(x_ref, gate_ref, up_ref, h_ref, tile_ff, 0, h_ref.shape[1])
    second_half(h_ref, down_ref, w_ref, out_refs, tile_d, 0, x_ref.shape[1])


def expert(blocks, pieces, experts, w_gate, w_up, w_down):
    count, rows = len(blocks), blocks[0].shape[0]
    _, width, ff = w_gate.shape
    total = count * rows
    here = pl.BlockSpec(memory_space=pltpu.VMEM)
    return pl.pallas_call(
        functools.partial(expert_kernel, count, experts, *tiles(width, ff)),
        out_shape=[pltpu.VMEM((n * rows, width), kind) for n, kind in pieces],
        in_specs=[here] * (count + 3),
        out_specs=[here] * len(pieces),
        scratch_shapes=[pltpu.VMEM((total, width), BF16), pltpu.VMEM((total, 1), F32), pltpu.VMEM((total, ff), BF16)],
        compiler_params=pltpu.CompilerParams(vmem_limit_bytes=SCRATCH),
        cost_estimate=pl.CostEstimate(
            flops=6 * max(total, 256) * width * ff, bytes_accessed=0, transcendentals=total * ff
        ),
    )(*blocks, w_gate, w_up, w_down)


def local(order, tokens, routes, gates, w_gate, w_up, w_down):
    chips = len(order)
    experts = 2 * chips
    rows, width = tokens.shape
    forth = [(2 * order[i], 2 * order[(i + 1) % chips]) for i in range(chips)]
    spin = forth + [(b + 1, a + 1) for a, b in forth]
    swap = [(i, i ^ 1) for i in range(experts)]
    send = lambda a: lax.ppermute(a, "node", spin)
    sibling = lambda a: lax.ppermute(a, "node", swap)
    together = lax.optimization_barrier
    block = lambda a, j: a[j * rows : (j + 1) * rows]

    far = chips // 2
    own = pack(tokens, routes, gates, experts)
    up, up_twin, down, down_twin = {0: own}, {0: sibling(own)}, {}, {}
    for k in range(1, far):
        up[k] = send(up[k - 1])
        up_twin[k] = send(up_twin[k - 1])
        down_twin[k], down[k] = sibling(up[k]), sibling(up_twin[k])
    up[far] = send(up[far - 1])
    far_twin = sibling(up[far])

    kept, given = [up[far]], [far_twin]
    for k in range(far - 1, 0, -1):
        kept += [down_twin[k], down[k]]
        given += [up[k], up_twin[k]]
    kept, given = kept + [own], given + [up_twin[0]]
    end = len(kept) - 1
    mine, theirs = {}, {}

    def compute(keep, give, sizes):
        sizes = [n for n in sizes if n]
        blocks = [kept[j] for j in keep] + [given[j] for j in give]
        out, *pieces = expert(blocks, [(len(keep), F32)] + [(n, BF16) for n in sizes], experts, w_gate, w_up, w_down)
        return out, pieces

    def note(keep, out, give, pieces):
        mine.update({j: (out, at) for at, j in enumerate(keep)})
        theirs.update(zip(give, [(piece, at) for piece in pieces for at in range(piece.shape[0] // rows)]))

    keep, give = [end - 2, end - 1, end], list(range(end - 4, end + 1))
    near, near_given = compute(keep, give, (5,))
    others = kept[1:2] + kept[3 : end - 2]
    near, near_given, kept[0], given[2], others = together((near, near_given, kept[0], given[2], others))
    kept[1], kept[3 : end - 2] = others[0], others[1:]
    given[0], kept[2] = sibling(kept[0]), sibling(given[2])
    given[0], kept[2], near_given = together((given[0], kept[2], near_given))
    near_sent = [sibling(p) for p in near_given]

    keep_last, give_last = list(range(end - 2)), list(range(end - 4))
    out, pieces = compute(keep_last, give_last, (2, len(give_last) - 2))
    out, pieces, near_sent = together((out, pieces, near_sent))
    note(keep, near, give, near_sent)
    note(keep_last, out, give_last, [sibling(p) for p in pieces])

    def add(j, *arrived):
        nonlocal last
        piece, at = theirs[j]
        (piece, *arrived), _ = together(((piece, *arrived), last))
        total = block(*mine[j]) + block(piece, at).astype(F32)
        for a in arrived:
            total = total + a.astype(F32)
        last = total.astype(BF16)
        return last

    last = mine[0][0]
    sums = send(add(0))
    sums_twin = []
    for j in range(1, end, 2):
        sums_twin = [send(add(j, *sums_twin))]
        sums = send(add(j + 1, sums))
    piece, sums = together((theirs[end][0], sums))
    total = block(*mine[end]) + block(piece, theirs[end][1]).astype(F32) + sums.astype(F32)
    for a in sums_twin:
        a, total = together((sibling(a), total))
        total = total + a.astype(F32)
    return total.astype(BF16)


def solution(mesh):
    order = chip_order(mesh)
    in_specs = (
        P(("groups", "node"), None),
        P(("groups", "node"), None),
        P(("groups", "node"), None),
        P("node", None, None),
        P("node", None, None),
        P("node", None, None),
    )
    out_specs = P(("groups", "node"), None)
    body = functools.partial(local, order)
    return jax.shard_map(body, mesh=mesh, in_specs=in_specs, out_specs=out_specs, check_vma=False)
```

```python
import functools

import jax
import jax.numpy as jnp
from jax import lax
from jax.experimental import pallas as pl
from jax.experimental.pallas import tpu as pltpu
from jax.sharding import PartitionSpec as P

F32, BF16 = jnp.float32, jnp.bfloat16
SCRATCH = 20 * 2**20


def chip_order(mesh):
    names = list(mesh.axis_names)
    count = mesh.shape["node"]
    row = mesh.devices.transpose([names.index(n) for n in names if n != "node"] + [names.index("node")])
    row = list(row.reshape(-1, count)[0])
    chips = [tuple(getattr(d, "coords", None) or (i // 2,)) for i, d in enumerate(row)][::2]
    order = list(range(len(chips)))
    axes = [a for a in range(len(chips[0])) if len({c[a] for c in chips}) > 1]
    if len(axes) == 2:
        short, long = sorted(axes, key=lambda a: len({c[a] for c in chips}))
        low = min(c[short] for c in chips)
        if len({c[short] for c in chips}) == 2:
            order.sort(key=lambda i: (chips[i][short], chips[i][long] if chips[i][short] == low else -chips[i][long]))
    return order


def pack_kernel(experts, tok_hbm, routes_hbm, gates_hbm, out_ref, routes_ref, gates_ref, sems):
    rows, width = tok_hbm.shape
    extra = out_ref.shape[1] - width
    moves = [
        pltpu.make_async_copy(routes_hbm, routes_ref, sems.at[0]),
        pltpu.make_async_copy(gates_hbm, gates_ref, sems.at[1]),
        pltpu.make_async_copy(tok_hbm, out_ref.at[:, :width], sems.at[2]),
    ]
    for move in moves:
        move.start()
    for move in moves[:2]:
        move.wait()
    lane = lax.broadcasted_iota(jnp.int32, (extra, rows), 0)
    expert, piece = lax.rem(lane, experts), lax.div(lane, experts)
    weight = jnp.zeros((extra, rows), F32)
    for k in range(routes_ref.shape[0]):
        weight += jnp.where(routes_ref[k : k + 1] == expert, gates_ref[k : k + 1], 0.0)
    high = weight.astype(BF16).astype(F32)
    middle = (weight - high).astype(BF16).astype(F32)
    low = weight - high - middle
    table = jnp.where(piece == 0, high, jnp.where(piece == 1, middle, jnp.where(piece == 2, low, 0.0)))
    out_ref[:, width:] = table.T.astype(BF16)
    moves[2].wait()


def pack(tokens, routes, gates, experts):
    rows, width = tokens.shape
    extra = pl.cdiv(3 * experts, 128) * 128
    there = pl.BlockSpec(memory_space=pltpu.HBM)
    return pl.pallas_call(
        functools.partial(pack_kernel, experts),
        out_shape=pltpu.VMEM((rows, width + extra), BF16),
        in_specs=[there] * 3,
        out_specs=pl.BlockSpec(memory_space=pltpu.VMEM),
        scratch_shapes=[
            pltpu.VMEM(routes.shape[::-1], routes.dtype),
            pltpu.VMEM(gates.shape[::-1], gates.dtype),
            pltpu.SemaphoreType.DMA((3,)),
        ],
        compiler_params=pltpu.CompilerParams(vmem_limit_bytes=SCRATCH),
        cost_estimate=pl.CostEstimate(flops=10 * 2**30, bytes_accessed=0, transcendentals=0),
    )(hbm(tokens), hbm(routes.T), hbm(gates.T))


def hbm(a):
    return pltpu.with_memory_space_constraint(a, pltpu.HBM)


def gather_rows(blocks, x_ref):
    rows, width = blocks[0].shape[0], x_ref.shape[1]
    for at, ref in enumerate(blocks):
        x_ref[at * rows : (at + 1) * rows, :] = ref[:, :width]


def gather_weights(experts, blocks, width, w_ref):
    me = lax.axis_index("node")
    rows = blocks[0].shape[0]
    for at, ref in enumerate(blocks):
        table = ref[:, width:].astype(F32)
        lane = lax.broadcasted_iota(jnp.int32, table.shape, 1)
        own = lax.rem(lane, experts) == me
        w_ref[at * rows : (at + 1) * rows, :] = jnp.sum(jnp.where(own, table, 0.0), axis=1, keepdims=True)


def first_half(x_ref, gate_ref, up_ref, h_ref, tile, begin, end):
    for j in range(begin // tile, end // tile):
        at = slice(j * tile, (j + 1) * tile)
        gate = jnp.dot(x_ref[...], gate_ref[0, :, at], preferred_element_type=F32)
        upper = jnp.dot(x_ref[...], up_ref[0, :, at], preferred_element_type=F32)
        h_ref[:, at] = (gate / (1.0 + jnp.exp(-gate)) * upper).astype(BF16)


def second_half(h_ref, down_ref, w_ref, out_refs, tile, begin, end):
    for j in range(begin // tile, end // tile):
        at = slice(j * tile, (j + 1) * tile)
        out = jnp.dot(h_ref[...], down_ref[0, :, at], preferred_element_type=F32) * w_ref[...]
        row = 0
        for ref in out_refs:
            ref[:, at] = out[row : row + ref.shape[0]].astype(ref.dtype)
            row += ref.shape[0]


def tiles(width, ff):
    return (256 if ff % 256 == 0 else ff), next(t for t in (512, 256, 128, width) if width % t == 0)


def hidden_kernel(count, tile, *refs):
    blocks, (gate_ref, up_ref, h_ref, x_ref) = refs[:count], refs[count:]
    gather_rows(blocks, x_ref)
    first_half(x_ref, gate_ref, up_ref, h_ref, tile, 0, h_ref.shape[1])


def hidden(blocks, w_gate, w_up):
    count, rows = len(blocks), blocks[0].shape[0]
    _, width, ff = w_gate.shape
    here = pl.BlockSpec(memory_space=pltpu.VMEM)
    return pl.pallas_call(
        functools.partial(hidden_kernel, count, tiles(width, ff)[0]),
        out_shape=pltpu.VMEM((count * rows, ff), BF16),
        in_specs=[here] * (count + 2),
        out_specs=here,
        scratch_shapes=[pltpu.VMEM((count * rows, width), BF16)],
        compiler_params=pltpu.CompilerParams(vmem_limit_bytes=SCRATCH),
        cost_estimate=pl.CostEstimate(
            flops=4 * max(count * rows, 256) * width * ff, bytes_accessed=0, transcendentals=count * rows * ff
        ),
    )(*blocks, w_gate, w_up)


def output_kernel(count, experts, tile, begin, *refs):
    blocks, (h_ref, down_ref, *out_refs), w_ref = refs[:count], refs[count:-1], refs[-1]
    width = out_refs[0].shape[1]
    gather_weights(experts, blocks, width, w_ref)
    second_half(h_ref.at[begin : begin + w_ref.shape[0]], down_ref, w_ref, out_refs, tile, 0, width)


def output(blocks, h, first, pieces, experts, w_down):
    count, rows = len(blocks), blocks[0].shape[0]
    _, ff, width = w_down.shape
    here = pl.BlockSpec(memory_space=pltpu.VMEM)
    return pl.pallas_call(
        functools.partial(output_kernel, count, experts, tiles(width, ff)[1], first * rows),
        out_shape=[pltpu.VMEM((n * rows, width), kind) for n, kind in pieces],
        in_specs=[here] * (count + 2),
        out_specs=[here] * len(pieces),
        scratch_shapes=[pltpu.VMEM((count * rows, 1), F32)],
        compiler_params=pltpu.CompilerParams(vmem_limit_bytes=SCRATCH),
        cost_estimate=pl.CostEstimate(
            flops=2 * max(count * rows, 256) * width * ff, bytes_accessed=0, transcendentals=0
        ),
    )(*blocks, h, w_down)


def local(order, tokens, routes, gates, w_gate, w_up, w_down):
    chips = len(order)
    experts = 2 * chips
    rows, width = tokens.shape
    forth = [(2 * order[i], 2 * order[(i + 1) % chips]) for i in range(chips)]
    spin = forth + [(b + 1, a + 1) for a, b in forth]
    swap = [(i, i ^ 1) for i in range(experts)]
    send = lambda a: lax.ppermute(a, "node", spin)
    sibling = lambda a: lax.ppermute(a, "node", swap)
    together = lax.optimization_barrier
    block = lambda a, j: a[j * rows : (j + 1) * rows]

    far = chips // 2
    own = pack(tokens, routes, gates, experts)
    up, up_twin, down, down_twin = {0: own}, {0: sibling(own)}, {}, {}
    for k in range(1, far):
        up[k] = send(up[k - 1])
        up_twin[k] = send(up_twin[k - 1])
        down_twin[k], down[k] = sibling(up[k]), sibling(up_twin[k])
    up[far] = send(up[far - 1])
    far_twin = sibling(up[far])

    kept, given = [up[far]], [far_twin]
    for k in range(far - 1, 0, -1):
        kept += [down_twin[k], down[k]]
        given += [up[k], up_twin[k]]
    kept, given = kept + [own], given + [up_twin[0]]
    end = len(kept) - 1
    mine, theirs = {}, {}

    def note(keep, out, give, pieces):
        mine.update({j: (out, at) for at, j in enumerate(keep)})
        theirs.update(zip(give, [(piece, at) for piece in pieces for at in range(piece.shape[0] // rows)]))

    keep, give = [end - 2, end - 1, end], list(range(end - 4, end + 1))
    blocks = [kept[j] for j in keep] + [given[j] for j in give]
    h = hidden(blocks, w_gate, w_up)
    others = kept[1:2] + kept[3 : end - 2]
    h, kept[0], given[2], others = together((h, kept[0], given[2], others))
    kept[1], kept[3 : end - 2] = others[0], others[1:]
    given[0], kept[2] = sibling(kept[0]), sibling(given[2])
    near, near_given = output(blocks, h, 0, [(3, F32), (5, BF16)], experts, w_down)
    given[0], kept[2], near_given = together((given[0], kept[2], near_given))
    near_sent = sibling(near_given)

    keep_last, give_last = list(range(end - 2)), list(range(end - 4))
    kept_blocks, given_blocks = [kept[j] for j in keep_last], [given[j] for j in give_last]
    h = hidden(given_blocks + kept_blocks, w_gate, w_up)
    pieces = output(given_blocks, h, 0, [(2, BF16), (len(give_last) - 2, BF16)], experts, w_down)
    h, pieces = together((h, pieces))
    sent = [sibling(p) for p in pieces]
    (out,) = output(kept_blocks, h, len(give_last), [(len(keep_last), F32)], experts, w_down)
    out, near_sent = together((out, near_sent))
    note(keep, near, give, [near_sent])
    note(keep_last, out, give_last, sent)

    def add(j, *arrived):
        nonlocal last
        piece, at = theirs[j]
        (piece, *arrived), _ = together(((piece, *arrived), last))
        total = block(*mine[j]) + block(piece, at).astype(F32)
        for a in arrived:
            total = total + a.astype(F32)
        last = total.astype(BF16)
        return last

    last = mine[0][0]
    sums = send(add(0))
    sums_twin = []
    for j in range(1, end, 2):
        sums_twin = [send(add(j, *sums_twin))]
        sums = send(add(j + 1, sums))
    piece, sums = together((theirs[end][0], sums))
    total = block(*mine[end]) + block(piece, theirs[end][1]).astype(F32) + sums.astype(F32)
    for a in sums_twin:
        a, total = together((sibling(a), total))
        total = total + a.astype(F32)
    return total.astype(BF16)


def solution(mesh):
    order = chip_order(mesh)
    in_specs = (
        P(("groups", "node"), None),
        P(("groups", "node"), None),
        P(("groups", "node"), None),
        P("node", None, None),
        P("node", None, None),
        P("node", None, None),
    )
    out_specs = P(("groups", "node"), None)
    body = functools.partial(local, order)
    return jax.shard_map(body, mesh=mesh, in_specs=in_specs, out_specs=out_specs, check_vma=False)
```

```python
import functools

import jax
import jax.numpy as jnp
from jax import lax
from jax.experimental import pallas as pl
from jax.experimental.pallas import tpu as pltpu
from jax.sharding import PartitionSpec as P

F32, BF16 = jnp.float32, jnp.bfloat16
SCRATCH = 20 * 2**20


def chip_order(mesh):
    names = list(mesh.axis_names)
    count = mesh.shape["node"]
    row = mesh.devices.transpose([names.index(n) for n in names if n != "node"] + [names.index("node")])
    row = list(row.reshape(-1, count)[0])
    chips = [tuple(getattr(d, "coords", None) or (i // 2,)) for i, d in enumerate(row)][::2]
    order = list(range(len(chips)))
    axes = [a for a in range(len(chips[0])) if len({c[a] for c in chips}) > 1]
    if len(axes) == 2:
        short, long = sorted(axes, key=lambda a: len({c[a] for c in chips}))
        low = min(c[short] for c in chips)
        if len({c[short] for c in chips}) == 2:
            order.sort(key=lambda i: (chips[i][short], chips[i][long] if chips[i][short] == low else -chips[i][long]))
    return order


def pack_kernel(experts, tok_hbm, routes_hbm, gates_hbm, out_ref, routes_ref, gates_ref, sems):
    rows, width = tok_hbm.shape
    extra = out_ref.shape[1] - width
    moves = [
        pltpu.make_async_copy(routes_hbm, routes_ref, sems.at[0]),
        pltpu.make_async_copy(gates_hbm, gates_ref, sems.at[1]),
        pltpu.make_async_copy(tok_hbm, out_ref.at[:, :width], sems.at[2]),
    ]
    for move in moves:
        move.start()
    for move in moves[:2]:
        move.wait()
    lane = lax.broadcasted_iota(jnp.int32, (extra, rows), 0)
    expert, piece = lax.rem(lane, experts), lax.div(lane, experts)
    weight = jnp.zeros((extra, rows), F32)
    for k in range(routes_ref.shape[0]):
        weight += jnp.where(routes_ref[k : k + 1] == expert, gates_ref[k : k + 1], 0.0)
    high = weight.astype(BF16).astype(F32)
    middle = (weight - high).astype(BF16).astype(F32)
    low = weight - high - middle
    table = jnp.where(piece == 0, high, jnp.where(piece == 1, middle, jnp.where(piece == 2, low, 0.0)))
    out_ref[:, width:] = table.T.astype(BF16)
    moves[2].wait()


def pack(tokens, routes, gates, experts):
    rows, width = tokens.shape
    extra = pl.cdiv(3 * experts, 128) * 128
    there = pl.BlockSpec(memory_space=pltpu.HBM)
    return pl.pallas_call(
        functools.partial(pack_kernel, experts),
        out_shape=pltpu.VMEM((rows, width + extra), BF16),
        in_specs=[there] * 3,
        out_specs=pl.BlockSpec(memory_space=pltpu.VMEM),
        scratch_shapes=[
            pltpu.VMEM(routes.shape[::-1], routes.dtype),
            pltpu.VMEM(gates.shape[::-1], gates.dtype),
            pltpu.SemaphoreType.DMA((3,)),
        ],
        compiler_params=pltpu.CompilerParams(vmem_limit_bytes=SCRATCH),
        cost_estimate=pl.CostEstimate(flops=10 * 2**30, bytes_accessed=0, transcendentals=0),
    )(hbm(tokens), hbm(routes.T), hbm(gates.T))


def hbm(a):
    return pltpu.with_memory_space_constraint(a, pltpu.HBM)


def gather_rows(blocks, x_ref):
    rows, width = blocks[0].shape[0], x_ref.shape[1]
    for at, ref in enumerate(blocks):
        x_ref[at * rows : (at + 1) * rows, :] = ref[:, :width]


def gather_weights(experts, blocks, width, w_ref):
    me = lax.axis_index("node")
    rows = blocks[0].shape[0]
    for at, ref in enumerate(blocks):
        table = ref[:, width:].astype(F32)
        lane = lax.broadcasted_iota(jnp.int32, table.shape, 1)
        own = lax.rem(lane, experts) == me
        w_ref[at * rows : (at + 1) * rows, :] = jnp.sum(jnp.where(own, table, 0.0), axis=1, keepdims=True)


def first_half(x_ref, gate_ref, up_ref, h_ref, tile, begin, end):
    for j in range(begin // tile, end // tile):
        at = slice(j * tile, (j + 1) * tile)
        gate = jnp.dot(x_ref[...], gate_ref[0, :, at], preferred_element_type=F32)
        upper = jnp.dot(x_ref[...], up_ref[0, :, at], preferred_element_type=F32)
        h_ref[:, at] = (gate / (1.0 + jnp.exp(-gate)) * upper).astype(BF16)


def second_half(h_ref, down_ref, w_ref, out_refs, tile, begin, end):
    for j in range(begin // tile, end // tile):
        at = slice(j * tile, (j + 1) * tile)
        out = jnp.dot(h_ref[...], down_ref[0, :, at], preferred_element_type=F32) * w_ref[...]
        row = 0
        for ref in out_refs:
            ref[:, at] = out[row : row + ref.shape[0]].astype(ref.dtype)
            row += ref.shape[0]


def tiles(width, ff):
    return (256 if ff % 256 == 0 else ff), next(t for t in (512, 256, 128, width) if width % t == 0)


def hidden_kernel(count, tile, *refs):
    blocks, (gate_ref, up_ref, h_ref, x_ref) = refs[:count], refs[count:]
    gather_rows(blocks, x_ref)
    first_half(x_ref, gate_ref, up_ref, h_ref, tile, 0, h_ref.shape[1])


def hidden(blocks, w_gate, w_up):
    count, rows = len(blocks), blocks[0].shape[0]
    _, width, ff = w_gate.shape
    here = pl.BlockSpec(memory_space=pltpu.VMEM)
    return pl.pallas_call(
        functools.partial(hidden_kernel, count, tiles(width, ff)[0]),
        out_shape=pltpu.VMEM((count * rows, ff), BF16),
        in_specs=[here] * (count + 2),
        out_specs=here,
        scratch_shapes=[pltpu.VMEM((count * rows, width), BF16)],
        compiler_params=pltpu.CompilerParams(vmem_limit_bytes=SCRATCH),
        cost_estimate=pl.CostEstimate(
            flops=4 * max(count * rows, 256) * width * ff, bytes_accessed=0, transcendentals=count * rows * ff
        ),
    )(*blocks, w_gate, w_up)


def output_kernel(count, experts, tile, begin, *refs):
    blocks, (h_ref, down_ref, *out_refs), w_ref = refs[:count], refs[count:-1], refs[-1]
    width = out_refs[0].shape[1]
    gather_weights(experts, blocks, width, w_ref)
    second_half(h_ref.at[begin : begin + w_ref.shape[0]], down_ref, w_ref, out_refs, tile, 0, width)


def output(blocks, h, first, pieces, experts, w_down):
    count, rows = len(blocks), blocks[0].shape[0]
    _, ff, width = w_down.shape
    here = pl.BlockSpec(memory_space=pltpu.VMEM)
    return pl.pallas_call(
        functools.partial(output_kernel, count, experts, tiles(width, ff)[1], first * rows),
        out_shape=[pltpu.VMEM((n * rows, width), kind) for n, kind in pieces],
        in_specs=[here] * (count + 2),
        out_specs=[here] * len(pieces),
        scratch_shapes=[pltpu.VMEM((count * rows, 1), F32)],
        compiler_params=pltpu.CompilerParams(vmem_limit_bytes=SCRATCH),
        cost_estimate=pl.CostEstimate(
            flops=2 * max(count * rows, 256) * width * ff, bytes_accessed=0, transcendentals=0
        ),
    )(*blocks, h, w_down)


def local(order, tokens, routes, gates, w_gate, w_up, w_down):
    chips = len(order)
    experts = 2 * chips
    rows, width = tokens.shape
    forth = [(2 * order[i], 2 * order[(i + 1) % chips]) for i in range(chips)]
    spin = forth + [(b + 1, a + 1) for a, b in forth]
    swap = [(i, i ^ 1) for i in range(experts)]
    turn = dict(spin)
    send = lambda a: lax.ppermute(a, "node", spin)
    send_two = lambda a: lax.ppermute(a, "node", [(a, turn[b]) for a, b in spin])
    sibling = lambda a: lax.ppermute(a, "node", swap)
    together = lax.optimization_barrier
    block = lambda a, j: a[j * rows : (j + 1) * rows]

    far = chips // 2
    own = pack(tokens, routes, gates, experts)
    up, up_twin, down, down_twin = {0: own}, {0: sibling(own)}, {}, {}
    for k in range(1, far):
        up[k] = send(up[k - 1])
        up_twin[k] = send(up_twin[k - 1])
        down_twin[k], down[k] = sibling(up[k]), sibling(up_twin[k])
    up[far] = send(up[far - 1])
    far_twin = sibling(up[far])

    kept, given = [up[far]], [far_twin]
    for k in range(far - 1, 0, -1):
        kept += [down_twin[k], down[k]]
        given += [up[k], up_twin[k]]
    kept, given = kept + [own], given + [up_twin[0]]
    end = len(kept) - 1
    mine, theirs = {}, {}

    def note(keep, out, give, pieces):
        mine.update({j: (out, at) for at, j in enumerate(keep)})
        theirs.update(zip(give, [(piece, at) for piece in pieces for at in range(piece.shape[0] // rows)]))

    keep, give = [end - 2, end - 1, end], list(range(end - 4, end + 1))
    blocks = [kept[j] for j in keep] + [given[j] for j in give]
    h = hidden(blocks, w_gate, w_up)
    others = kept[1:2] + kept[3 : end - 2]
    h, kept[0], given[2], others = together((h, kept[0], given[2], others))
    kept[1], kept[3 : end - 2] = others[0], others[1:]
    given[0], kept[2] = sibling(kept[0]), sibling(given[2])
    near, near_given = output(blocks, h, 0, [(3, F32), (5, BF16)], experts, w_down)
    given[0], kept[2], near_given = together((given[0], kept[2], near_given))
    near_sent = sibling(near_given)

    keep_last, give_last = list(range(end - 2)), list(range(end - 4))
    kept_blocks, given_blocks = [kept[j] for j in keep_last], [given[j] for j in give_last]
    h = hidden(given_blocks + kept_blocks, w_gate, w_up)
    pieces = output(given_blocks, h, 0, [(2, BF16), (len(give_last) - 2, BF16)], experts, w_down)
    h, pieces = together((h, pieces))
    sent = [sibling(p) for p in pieces]
    (out,) = output(kept_blocks, h, len(give_last), [(len(keep_last), F32)], experts, w_down)
    out, near_sent = together((out, near_sent))
    note(keep, near, give, [near_sent])
    note(keep_last, out, give_last, sent)

    def add(j, *arrived):
        nonlocal last
        piece, at = theirs[j]
        (piece, *arrived), _ = together(((piece, *arrived), last))
        total = block(*mine[j]) + block(piece, at).astype(F32)
        for a in arrived:
            total = total + a.astype(F32)
        last = total.astype(BF16)
        return last

    last = mine[0][0]
    sums, sums_twin = [send_two(add(0))], []
    for j in range(1, end, 2):
        sums_twin = [send(add(j, *sums_twin))]
        if j == 1:
            sums.append(send(add(2)))
        else:
            sums = [send(add(j + 1, *sums))]
    (sums,) = sums
    piece, sums = together((theirs[end][0], sums))
    total = block(*mine[end]) + block(piece, theirs[end][1]).astype(F32) + sums.astype(F32)
    for a in sums_twin:
        a, _ = together((a, last))
        a, total = together((sibling(a), total))
        total = total + a.astype(F32)
    return total.astype(BF16)


def solution(mesh):
    order = chip_order(mesh)
    in_specs = (
        P(("groups", "node"), None),
        P(("groups", "node"), None),
        P(("groups", "node"), None),
        P("node", None, None),
        P("node", None, None),
        P("node", None, None),
    )
    out_specs = P(("groups", "node"), None)
    body = functools.partial(local, order)
    return jax.shard_map(body, mesh=mesh, in_specs=in_specs, out_specs=out_specs, check_vma=False)
```

```python
import functools

import jax
import jax.numpy as jnp
from jax import lax
from jax.experimental import pallas as pl
from jax.experimental.pallas import tpu as pltpu
from jax.sharding import PartitionSpec as P

F32, BF16 = jnp.float32, jnp.bfloat16
SCRATCH = 20 * 2**20


def chip_order(mesh):
    names = list(mesh.axis_names)
    count = mesh.shape["node"]
    row = mesh.devices.transpose([names.index(n) for n in names if n != "node"] + [names.index("node")])
    row = list(row.reshape(-1, count)[0])
    chips = [tuple(getattr(d, "coords", None) or (i // 2,)) for i, d in enumerate(row)][::2]
    order = list(range(len(chips)))
    axes = [a for a in range(len(chips[0])) if len({c[a] for c in chips}) > 1]
    if len(axes) == 2:
        short, long = sorted(axes, key=lambda a: len({c[a] for c in chips}))
        low = min(c[short] for c in chips)
        if len({c[short] for c in chips}) == 2:
            order.sort(key=lambda i: (chips[i][short], chips[i][long] if chips[i][short] == low else -chips[i][long]))
    return order


def pack_kernel(experts, tok_hbm, routes_hbm, gates_hbm, out_ref, routes_ref, gates_ref, sems):
    rows, width = tok_hbm.shape
    extra = out_ref.shape[1] - width
    moves = [
        pltpu.make_async_copy(routes_hbm, routes_ref, sems.at[0]),
        pltpu.make_async_copy(gates_hbm, gates_ref, sems.at[1]),
        pltpu.make_async_copy(tok_hbm, out_ref.at[:, :width], sems.at[2]),
    ]
    for move in moves:
        move.start()
    for move in moves[:2]:
        move.wait()
    lane = lax.broadcasted_iota(jnp.int32, (extra, rows), 0)
    expert, piece = lax.rem(lane, experts), lax.div(lane, experts)
    weight = jnp.zeros((extra, rows), F32)
    for k in range(routes_ref.shape[0]):
        weight += jnp.where(routes_ref[k : k + 1] == expert, gates_ref[k : k + 1], 0.0)
    high = weight.astype(BF16).astype(F32)
    middle = (weight - high).astype(BF16).astype(F32)
    low = weight - high - middle
    table = jnp.where(piece == 0, high, jnp.where(piece == 1, middle, jnp.where(piece == 2, low, 0.0)))
    out_ref[:, width:] = table.T.astype(BF16)
    moves[2].wait()


def pack(tokens, routes, gates, experts):
    rows, width = tokens.shape
    extra = pl.cdiv(3 * experts, 128) * 128
    there = pl.BlockSpec(memory_space=pltpu.HBM)
    return pl.pallas_call(
        functools.partial(pack_kernel, experts),
        out_shape=pltpu.VMEM((rows, width + extra), BF16),
        in_specs=[there] * 3,
        out_specs=pl.BlockSpec(memory_space=pltpu.VMEM),
        scratch_shapes=[
            pltpu.VMEM(routes.shape[::-1], routes.dtype),
            pltpu.VMEM(gates.shape[::-1], gates.dtype),
            pltpu.SemaphoreType.DMA((3,)),
        ],
        compiler_params=pltpu.CompilerParams(vmem_limit_bytes=SCRATCH),
        cost_estimate=pl.CostEstimate(flops=10 * 2**30, bytes_accessed=0, transcendentals=0),
    )(hbm(tokens), hbm(routes.T), hbm(gates.T))


def hbm(a):
    return pltpu.with_memory_space_constraint(a, pltpu.HBM)


def gather_rows(blocks, x_ref):
    rows, width = blocks[0].shape[0], x_ref.shape[1]
    for at, ref in enumerate(blocks):
        x_ref[at * rows : (at + 1) * rows, :] = ref[:, :width]


def gather_weights(experts, blocks, width, w_ref):
    me = lax.axis_index("node")
    rows = blocks[0].shape[0]
    for at, ref in enumerate(blocks):
        table = ref[:, width:].astype(F32)
        lane = lax.broadcasted_iota(jnp.int32, table.shape, 1)
        own = lax.rem(lane, experts) == me
        w_ref[at * rows : (at + 1) * rows, :] = jnp.sum(jnp.where(own, table, 0.0), axis=1, keepdims=True)


def first_half(x_ref, gate_ref, up_ref, h_ref, tile, begin, end):
    for j in range(begin // tile, end // tile):
        at = slice(j * tile, (j + 1) * tile)
        gate = jnp.dot(x_ref[...], gate_ref[0, :, at], preferred_element_type=F32)
        upper = jnp.dot(x_ref[...], up_ref[0, :, at], preferred_element_type=F32)
        h_ref[:, at] = (gate / (1.0 + jnp.exp(-gate)) * upper).astype(BF16)


def second_half(h_ref, down_ref, w_ref, out_refs, tile, begin, end):
    for j in range(begin // tile, end // tile):
        at = slice(j * tile, (j + 1) * tile)
        out = jnp.dot(h_ref[...], down_ref[0, :, at], preferred_element_type=F32) * w_ref[...]
        row = 0
        for ref in out_refs:
            ref[:, at] = out[row : row + ref.shape[0]].astype(ref.dtype)
            row += ref.shape[0]


def tiles(width, ff):
    return (256 if ff % 256 == 0 else ff), next(t for t in (512, 256, 128, width) if width % t == 0)


def hidden_kernel(count, tile, *refs):
    blocks, (gate_ref, up_ref, h_ref, x_ref) = refs[:count], refs[count:]
    gather_rows(blocks, x_ref)
    first_half(x_ref, gate_ref, up_ref, h_ref, tile, 0, h_ref.shape[1])


def hidden(blocks, w_gate, w_up):
    count, rows = len(blocks), blocks[0].shape[0]
    _, width, ff = w_gate.shape
    here = pl.BlockSpec(memory_space=pltpu.VMEM)
    return pl.pallas_call(
        functools.partial(hidden_kernel, count, tiles(width, ff)[0]),
        out_shape=pltpu.VMEM((count * rows, ff), BF16),
        in_specs=[here] * (count + 2),
        out_specs=here,
        scratch_shapes=[pltpu.VMEM((count * rows, width), BF16)],
        compiler_params=pltpu.CompilerParams(vmem_limit_bytes=SCRATCH),
        cost_estimate=pl.CostEstimate(
            flops=4 * max(count * rows, 256) * width * ff, bytes_accessed=0, transcendentals=count * rows * ff
        ),
    )(*blocks, w_gate, w_up)


def output_kernel(count, experts, tile, begin, *refs):
    blocks, (h_ref, down_ref, *out_refs), w_ref = refs[:count], refs[count:-1], refs[-1]
    width = out_refs[0].shape[1]
    gather_weights(experts, blocks, width, w_ref)
    second_half(h_ref.at[begin : begin + w_ref.shape[0]], down_ref, w_ref, out_refs, tile, 0, width)


def output(blocks, h, first, pieces, experts, w_down):
    count, rows = len(blocks), blocks[0].shape[0]
    _, ff, width = w_down.shape
    here = pl.BlockSpec(memory_space=pltpu.VMEM)
    return pl.pallas_call(
        functools.partial(output_kernel, count, experts, tiles(width, ff)[1], first * rows),
        out_shape=[pltpu.VMEM((n * rows, width), kind) for n, kind in pieces],
        in_specs=[here] * (count + 2),
        out_specs=[here] * len(pieces),
        scratch_shapes=[pltpu.VMEM((count * rows, 1), F32)],
        compiler_params=pltpu.CompilerParams(vmem_limit_bytes=SCRATCH),
        cost_estimate=pl.CostEstimate(
            flops=2 * max(count * rows, 256) * width * ff, bytes_accessed=0, transcendentals=0
        ),
    )(*blocks, h, w_down)


def local(order, tokens, routes, gates, w_gate, w_up, w_down):
    chips = len(order)
    experts = 2 * chips
    rows, width = tokens.shape
    forth = [(2 * order[i], 2 * order[(i + 1) % chips]) for i in range(chips)]
    spin = forth + [(b + 1, a + 1) for a, b in forth]
    swap = [(i, i ^ 1) for i in range(experts)]
    send = lambda a: lax.ppermute(a, "node", spin)
    sibling = lambda a: lax.ppermute(a, "node", swap)
    together = lax.optimization_barrier
    block = lambda a, j: a[j * rows : (j + 1) * rows]

    far = chips // 2
    own = pack(tokens, routes, gates, experts)
    up, up_twin, down, down_twin = {0: own}, {0: sibling(own)}, {}, {}
    for k in range(1, far):
        up[k] = send(up[k - 1])
        up_twin[k] = send(up_twin[k - 1])
        down_twin[k], down[k] = sibling(up[k]), sibling(up_twin[k])
    up[far] = send(up[far - 1])
    far_twin = sibling(up[far])

    kept, given = [up[far]], [far_twin]
    for k in range(far - 1, 0, -1):
        kept += [down_twin[k], down[k]]
        given += [up[k], up_twin[k]]
    kept, given = kept + [own], given + [up_twin[0]]
    end = len(kept) - 1
    mine, theirs = {}, {}

    def note(keep, out, give, pieces):
        mine.update({j: (out, at) for at, j in enumerate(keep)})
        theirs.update(zip(give, [(piece, at) for piece in pieces for at in range(piece.shape[0] // rows)]))

    keep, give = [end - 2, end - 1, end], list(range(end - 4, end + 1))
    blocks = [kept[j] for j in keep] + [given[j] for j in give]
    h = hidden(blocks, w_gate, w_up)
    others = kept[1:2] + kept[3 : end - 2]
    h, kept[0], given[2], others = together((h, kept[0], given[2], others))
    kept[1], kept[3 : end - 2] = others[0], others[1:]
    given[0], kept[2] = sibling(kept[0]), sibling(given[2])
    (near_given,) = output(blocks[3:], h, 3, [(5, BF16)], experts, w_down)
    h_near, near_blocks = h, blocks[:3]
    given[0], kept[2], near_given = together((given[0], kept[2], near_given))
    near_sent = sibling(near_given)

    keep_last, give_last = list(range(end - 2)), list(range(end - 4))
    kept_blocks, given_blocks = [kept[j] for j in keep_last], [given[j] for j in give_last]
    h = hidden(given_blocks + kept_blocks, w_gate, w_up)
    pieces = output(given_blocks, h, 0, [(2, BF16), (len(give_last) - 2, BF16)], experts, w_down)
    h, pieces = together((h, pieces))
    sent = [sibling(p) for p in pieces]
    (out,) = output(kept_blocks, h, len(give_last), [(len(keep_last), F32)], experts, w_down)
    out, near_sent = together((out, near_sent))
    theirs.update({j: (near_sent, at) for at, j in enumerate(give)})
    note(keep_last, out, give_last, sent)

    def add(j, *arrived):
        nonlocal last
        piece, at = theirs[j]
        (piece, *arrived), _ = together(((piece, *arrived), last))
        total = block(*mine[j]) + block(piece, at).astype(F32)
        for a in arrived:
            total = total + a.astype(F32)
        last = total.astype(BF16)
        return last

    last = mine[0][0]
    sums = send(add(0))
    sums_twin = []
    for j in range(1, end, 2):
        sums_twin = [send(add(j, *sums_twin))]
        if j == 1:
            h_near, _ = together((h_near, last))
            (near,) = output(near_blocks, h_near, 0, [(3, F32)], experts, w_down)
            near, sums = together((near, sums))
            mine.update({k: (near, at) for at, k in enumerate(keep)})
        sums = send(add(j + 1, sums))
    piece, sums = together((theirs[end][0], sums))
    total = block(*mine[end]) + block(piece, theirs[end][1]).astype(F32) + sums.astype(F32)
    for a in sums_twin:
        a, total = together((sibling(a), total))
        total = total + a.astype(F32)
    return total.astype(BF16)


def solution(mesh):
    order = chip_order(mesh)
    in_specs = (
        P(("groups", "node"), None),
        P(("groups", "node"), None),
        P(("groups", "node"), None),
        P("node", None, None),
        P("node", None, None),
        P("node", None, None),
    )
    out_specs = P(("groups", "node"), None)
    body = functools.partial(local, order)
    return jax.shard_map(body, mesh=mesh, in_specs=in_specs, out_specs=out_specs, check_vma=False)
```
